32 devices in a mesh: group: 2 (over x), row: 16 (over z, y, core).
Axes of the slice: x: 2, y: 2, z: 4, core: 2. Of those that a mesh axis runs over, the one named last changes fastest.
Arguments:
- first_frame: bfloat16 [128, 128, 256], P(('group', 'row')), parts along dimension 0, may hold values from -6 to 6
- second_frame: bfloat16 [128, 128, 256], P(('group', 'row')), parts along dimension 0, may hold values from -6 to 6
- context: bfloat16 [128, 128, 128], P(('group', 'row')), parts along dimension 0, may hold values from -6 to 6
- hidden_init: bfloat16 [128, 128, 128], P(('group', 'row')), parts along dimension 0, may hold values from -1 to 1
- flow_rows: int32 [2, 128, 128], P(None, ('group', 'row')), parts along dimension 1, may hold values from -8 to 8
- flow_cols: int32 [2, 128, 128], P(None, ('group', 'row')), parts along dimension 1, may hold values from -12 to 12
- block_ids: int32 [2, 32, 4], P(None, ('group', 'row')), parts along dimension 1, may hold values from 0 to 15, as said below
- block_counts: int32 [2, 32], P(None, ('group', 'row')), parts along dimension 1, may hold values from 1 to 4
- w_corr: bfloat16 [81, 256], replicated, may hold values from -0.625 to 0.625
- w_corr2: bfloat16 [2304, 192], replicated, may hold values from -0.125 to 0.125
- w_flow1: bfloat16 [98, 128], replicated, may hold values from -0.625 to 0.625
- w_flow2: bfloat16 [1152, 64], replicated, may hold values from -0.1875 to 0.1875
- w_motion: bfloat16 [2304, 126], replicated, may hold values from -0.125 to 0.125
- w_gates: bfloat16 [1920, 256], replicated, may hold values from -0.125 to 0.125
- w_cand: bfloat16 [1920, 128], replicated, may hold values from -0.125 to 0.125
- w_head1: bfloat16 [1152, 256], replicated, may hold values from -0.1875 to 0.1875
- w_head2: bfloat16 [2304, 2], replicated, may hold values from -0.125 to 0.125
Outputs:
- hidden_out: bfloat16 [128, 128, 128], P(('group', 'row')), parts along dimension 0
- flow_deltas: float32 [2, 2, 128, 128], P(None, None, ('group', 'row')), parts along dimension 2
The draws below stay inside these ranges and needn't reach their ends.
There are 2 independent parts, one for each index of `group`. The reference program is written for one: setup_inputs(seed, part) draws one part's arguments, and reference() takes and returns one part's arrays. A program takes and returns all parts, laid end to end along the dimension named above; an argument that names none is the same for every part. Nothing has to cross between parts.
Inputs may be any that keep to these rules, and one draw needn't show every extreme that they name: `block_ids`: for each iteration and tile, 4 ids of second-frame blocks, each within 3 blocks of the tile's own. The first block_counts entries form the tile's search window: consecutive blocks, cut at the frame's ends, that include the tile's own block; the later entries are not part of it.
All inputs are finite; a program needn't handle non-finite values.
Results may differ from the reference program's by a relative error of at most 0.006.
Values may be sent and summed in bfloat16 or wider, within the bound.
No kernel may reach another device: no remote copies, remote signals or barrier semaphores. Data moves between devices by JAX's collectives and lax.ppermute only.
A program may use at most 64 MiB of HBM per device.

```python
import math
import jax
import jax.numpy as jnp
from jax import lax

C = 256
HID = 128
CORR1 = 256
CORR2 = 192
FLO1 = 128
FLO2 = 64
HEAD = 256
RAD = 4
R_DEV = 4
W = 128
ITERS = 2
REACH = 3
K_MAX = 4
FX_MAX = 12
N_TILES = 16
H = 64
NB = 7
TAPS = 81
FY_MAX = 8
MOT = 126


def window_lists(key):
    subkeys = jax.random.split(jax.random.fold_in(key, 11), 6)
    tile_index = jnp.arange(N_TILES, dtype=jnp.int32)[None, :]
    counts = jax.random.randint(subkeys[0], (ITERS, N_TILES), 1, K_MAX + 1)
    forced = jax.random.randint(subkeys[1], (ITERS, 1), 0, N_TILES)
    single = (forced + 1 + jax.random.randint(subkeys[2], (ITERS, 1), 0, N_TILES - 1)) % N_TILES
    counts = jnp.where(tile_index == forced, K_MAX, counts)
    counts = jnp.where(tile_index == single, 1, counts)
    window_start = jnp.maximum(-jax.random.randint(subkeys[3], (ITERS, N_TILES), 0, K_MAX), -(counts - 1))
    rotation = jax.random.randint(subkeys[4], (ITERS, N_TILES), 0, K_MAX)
    slot_index = jnp.arange(K_MAX, dtype=jnp.int32)[None, None, :]
    inside = window_start[..., None] + (slot_index + rotation[..., None]) % counts[..., None]
    filler = jax.random.randint(subkeys[5], (ITERS, N_TILES, K_MAX), -REACH, REACH + 1)
    offset = jnp.where(slot_index < counts[..., None], inside, filler)
    block_list = jnp.clip(tile_index[..., None] + offset, 0, N_TILES - 1)
    return (block_list.astype(jnp.int32), counts.astype(jnp.int32))


def draw_block_ids(key, part):
    block_list, counts = window_lists(key)
    return block_list


def draw_block_counts(key, part):
    block_list, counts = window_lists(key)
    return counts


def touch_ends(values, key, smallest, top_value):
    longest = values.shape.index(max(values.shape))
    spots = []
    for shift in (0, 1):
        where = [jax.random.randint(jax.random.fold_in(key, axis), (), 0, length) for axis, length in enumerate(values.shape)]
        where[longest] = (where[longest] + shift) % values.shape[longest]
        spots.append(tuple(where))
    return values.at[spots[0]].set(smallest).at[spots[1]].set(top_value)


def block_scale(rng, extent, cuts, least, largest):
    factor_of, own = 1.0, jax.random.fold_in(rng, 6)
    for dim, shards_of in cuts:
        heights = jnp.exp(jax.random.uniform(jax.random.fold_in(own, dim), (shards_of,), jnp.float32, least / len(cuts), largest / len(cuts)))
        factor_of = factor_of * jnp.repeat(heights, extent[dim] // shards_of).reshape([-1 if axis == dim else 1 for axis in range(len(extent))])
    return factor_of


def gaussian(rng, extent, scale, bound, cuts=(), kind=jnp.bfloat16):
    values = jax.random.normal(rng, extent, jnp.float32) * scale
    if len(cuts) > 0:
        values = block_scale(rng, extent, cuts, -0.22, 0.18) * values
    return jnp.clip(values, min=-bound, max=bound).astype(kind)


def setup_inputs(seed: int = 0, part: int = 0) -> dict:
    arg_keys = jax.random.split(jax.random.key(seed), 18)
    own_keys = jax.random.split(jax.random.fold_in(arg_keys[17], part), 18)
    first_frame = gaussian(own_keys[0], (H, W, C), 1.0, 6.0, ((0, 16),))
    second_frame = gaussian(own_keys[1], (H, W, C), 1.0, 6.0, ((0, 16),))
    context = gaussian(own_keys[2], (H, W, HID), 1.0, 6.0, ((0, 16),))
    hidden_init = jnp.clip(jax.random.uniform(own_keys[3], (H, W, HID), jnp.float32, -1.0, 1.0) * block_scale(own_keys[3], (H, W, HID), ((0, 16),), -0.4, 0.0), -1.0, 1.0).astype(jnp.bfloat16)
    flow_rows = touch_ends(jax.random.randint(own_keys[4], (ITERS, H, W), 0 - FY_MAX, FY_MAX + 1), jax.random.fold_in(own_keys[4], 1), 0 - FY_MAX, FY_MAX).astype(jnp.int32)
    flow_cols = touch_ends(jax.random.randint(own_keys[5], (ITERS, H, W), 0 - FX_MAX, FX_MAX + 1), jax.random.fold_in(own_keys[5], 1), 0 - FX_MAX, FX_MAX).astype(jnp.int32)
    block_ids = draw_block_ids(jax.random.fold_in(jax.random.fold_in(arg_keys[17], part), 71), part)
    block_counts = draw_block_counts(jax.random.fold_in(jax.random.fold_in(arg_keys[17], part), 71), part)
    w_corr = gaussian(arg_keys[8], (TAPS, CORR1), TAPS ** -0.5, 0.625)
    w_corr2 = gaussian(arg_keys[9], (9 * CORR1, CORR2), (9 * CORR1) ** -0.5, 0.125)
    w_flow1 = gaussian(arg_keys[10], (98, FLO1), 98 ** -0.5, 0.625)
    w_flow2 = gaussian(arg_keys[11], (9 * FLO1, FLO2), (9 * FLO1) ** -0.5, 0.1875)
    w_motion = gaussian(arg_keys[12], (9 * (CORR2 + FLO2), MOT), (9 * (CORR2 + FLO2)) ** -0.5, 0.125)
    w_gates = gaussian(arg_keys[13], (15 * HID, 2 * HID), (15 * HID) ** -0.5, 0.125)
    w_cand = gaussian(arg_keys[14], (15 * HID, HID), (15 * HID) ** -0.5, 0.125)
    w_head1 = gaussian(arg_keys[15], (9 * HID, HEAD), (9 * HID) ** -0.5, 0.1875)
    w_head2 = gaussian(arg_keys[16], (9 * HEAD, 2), (9 * HEAD) ** -0.5, 0.125)
    return {"first_frame": first_frame, "second_frame": second_frame, "context": context, "hidden_init": hidden_init, "flow_rows": flow_rows, "flow_cols": flow_cols, "block_ids": block_ids, "block_counts": block_counts, "w_corr": w_corr, "w_corr2": w_corr2, "w_flow1": w_flow1, "w_flow2": w_flow2, "w_motion": w_motion, "w_gates": w_gates, "w_cand": w_cand, "w_head1": w_head1, "w_head2": w_head2}


flow_scale = 0.125

def convolve(extended, weight, kernel_rows, kernel_cols):
    out_rows = extended.shape[0] - kernel_rows + 1
    frame_width = extended.shape[1]
    in_chans = extended.shape[2]
    margin = kernel_cols // 2
    padded = jnp.pad(extended, ((0, 0), (margin, margin), (0, 0)))
    if in_chans * kernel_rows * kernel_cols <= 256:
        windows = [padded[tap_row:tap_row + out_rows, tap_col:tap_col + frame_width] for tap_row in range(kernel_rows) for tap_col in range(kernel_cols)]
        patches = jnp.concatenate(windows, axis=-1).reshape(out_rows * frame_width, -1)
        summed = jnp.dot(patches, weight, preferred_element_type=jnp.float32)
    else:
        summed = jnp.zeros((out_rows * frame_width, weight.shape[1]), jnp.float32)
        for tap_row in range(kernel_rows):
            for tap_col in range(kernel_cols):
                tap_index = tap_row * kernel_cols + tap_col
                window_piece = padded[tap_row:tap_row + out_rows, tap_col:tap_col + frame_width].reshape(-1, in_chans)
                summed = summed + jnp.dot(window_piece, weight[tap_index * in_chans:(tap_index + 1) * in_chans], preferred_element_type=jnp.float32)
    return summed.reshape(out_rows, frame_width, weight.shape[1])

def conv_same(field, weight, kernel_rows, kernel_cols):
    reach_rows = kernel_rows // 2
    extended = jnp.pad(field, ((reach_rows, reach_rows), (0, 0), (0, 0)))
    return convolve(extended, weight, kernel_rows, kernel_cols)

def window_mask(tile_index, block_list, block_count, tile_count):
    global_block = tile_index - REACH + jnp.arange(NB, dtype=jnp.int32)
    listed = jnp.arange(block_list.shape[0], dtype=jnp.int32) < block_count
    matched = jnp.any((global_block[:, None] == block_list[None, :]) & listed[None, :], axis=1)
    inside = (global_block >= 0) & (global_block < tile_count)
    return (matched & inside).astype(jnp.float32)

def correlate(first_tile, band_flat, flow_down, flow_across, allowed):
    rows_dev, frame_width, channels = first_tile.shape
    band_rows = band_flat.shape[0] // frame_width
    row_pos = jnp.arange(rows_dev, dtype=jnp.int32)[:, None]
    col_pos = jnp.arange(frame_width, dtype=jnp.int32)[None, :]
    shifts = jnp.arange(-RAD, RAD + 1, dtype=jnp.int32)[:, None, None]
    target_cols = col_pos[None] + flow_across[None] + shifts
    inside = ((target_cols >= 0) & (target_cols < frame_width)).astype(jnp.float32)
    safe_cols = jnp.clip(target_cols, 0, frame_width - 1)
    corr_scale = 1.0 / math.sqrt(channels)
    blocks = []
    for row_shift in range(-RAD, RAD + 1):
        target_rows = jnp.clip(row_pos + REACH * rows_dev + flow_down + row_shift, 0, band_rows - 1)
        owner_block = target_rows // rows_dev
        listed_weight = lax.optimization_barrier(jnp.sum((owner_block[..., None] == jnp.arange(NB, dtype=jnp.int32)).astype(jnp.float32) * allowed, axis=-1))
        picked = jnp.take(band_flat, target_rows[None] * frame_width + safe_cols, axis=0)
        products = jnp.einsum('dijc,ijc->dij', picked.astype(jnp.float32), first_tile.astype(jnp.float32))
        blocks.append(products * corr_scale * inside * listed_weight[None])
    return jnp.stack(blocks).reshape(TAPS, rows_dev, frame_width).astype(jnp.bfloat16)

def reference(first_frame, second_frame, context, hidden_init, flow_rows, flow_cols, block_ids, block_counts, w_corr, w_corr2, w_flow1, w_flow2, w_motion, w_gates, w_cand, w_head1, w_head2):
    margin = REACH * R_DEV
    padded = jnp.pad(second_frame, ((margin, margin), (0, 0), (0, 0)))
    band_rows = NB * R_DEV
    hidden = hidden_init
    hidden_units = hidden_init.shape[2]
    deltas = []
    for iteration in range(ITERS):

        def one_tile(tile_index):
            start_row = tile_index * R_DEV
            first_tile = lax.dynamic_slice_in_dim(first_frame, start_row, R_DEV, 0)
            second_band = lax.dynamic_slice_in_dim(padded, start_row, band_rows, 0)
            flow_down = lax.dynamic_slice_in_dim(flow_rows[iteration], start_row, R_DEV, 0)
            flow_across = lax.dynamic_slice_in_dim(flow_cols[iteration], start_row, R_DEV, 0)
            allowed = window_mask(tile_index, block_ids[iteration, tile_index], block_counts[iteration, tile_index], N_TILES)
            return correlate(first_tile, second_band.reshape(band_rows * W, C), flow_down, flow_across, allowed)
        correlation = lax.map(one_tile, jnp.arange(N_TILES, dtype=jnp.int32))
        correlation = correlation.transpose(1, 0, 2, 3).reshape(TAPS, H * W)
        corr_first = jax.nn.relu(jnp.dot(correlation.T, w_corr, preferred_element_type=jnp.float32)).astype(jnp.bfloat16).reshape(H, W, -1)
        flow_in = (jnp.stack([flow_rows[iteration], flow_cols[iteration]], axis=-1).astype(jnp.float32) * flow_scale).astype(jnp.bfloat16)
        flow_first = jax.nn.relu(conv_same(flow_in, w_flow1, 7, 7)).astype(jnp.bfloat16)
        corr_second = jax.nn.relu(conv_same(corr_first, w_corr2, 3, 3)).astype(jnp.bfloat16)
        flow_second = jax.nn.relu(conv_same(flow_first, w_flow2, 3, 3)).astype(jnp.bfloat16)
        motion = jax.nn.relu(conv_same(jnp.concatenate([corr_second, flow_second], axis=-1), w_motion, 3, 3)).astype(jnp.bfloat16)
        inputs = jnp.concatenate([context, motion, flow_in], axis=-1)
        gate_values = jax.nn.sigmoid(conv_same(jnp.concatenate([hidden, inputs], axis=-1), w_gates, 5, 1))
        update = gate_values[..., :hidden_units]
        reset_state = (gate_values[..., hidden_units:] * hidden).astype(jnp.bfloat16)
        candidate = jnp.tanh(conv_same(jnp.concatenate([reset_state, inputs], axis=-1), w_cand, 5, 1))
        hidden = ((1.0 - update) * hidden + update * candidate).astype(jnp.bfloat16)
        head_out = jax.nn.relu(conv_same(hidden, w_head1, 3, 3)).astype(jnp.bfloat16)
        flow_delta = conv_same(head_out, w_head2, 3, 3)
        deltas.append(flow_delta.transpose(2, 0, 1))
    return (hidden, jnp.stack(deltas))
```

```python
import functools
import math

import jax
import jax.numpy as jnp
from jax import lax
from jax.experimental import pallas as pl
from jax.experimental.pallas import tpu as pltpu
from jax.sharding import PartitionSpec as P

RAD = 4
ITERS = 2
REACH = 3
NB = 7
SIDE = 9
TAPS = 81
LANES = 128
FY_MAX = 8
FLOW_SCALE = 0.125
F32 = jnp.float32
BF16 = jnp.bfloat16
VMEM_BYTES = 56 * 1024 * 1024

ROWS = 4
MOTION_REACH = 4
SECOND_REACH = MOTION_REACH + 1
FIRST_REACH = MOTION_REACH + 2
GATE_REACH = 2


def swap(block, partner):
    devices = lax.axis_size("row")
    route = []
    for i in range(devices):
        j = partner(i)
        route.append((i, j if 0 <= j < devices else i))
    return lax.ppermute(block, "row", route)


def in_chip(i):
    return i ^ 1


def next_row(i):
    return ((i + 1) ^ 1) - 1


def chip_even(i):
    return i ^ 2


def chip_odd(i):
    return ((i + 2) ^ 2) - 2


def three_away(i):
    return i - 3 if i % 2 == 0 else i + 3


def near_tiles(block):
    even, odd = swap(block, chip_even), swap(block, chip_odd)
    return even, odd, swap(block, in_chip), swap(even, in_chip), swap(odd, in_chip)


def side_tiles(block):
    return swap(block, next_row), swap(block, in_chip)


def pick(flag, yes, no):
    return jnp.where(flag, yes, no)


def shift_cols(values, shift):
    size = values.shape[0]
    column = lax.broadcasted_iota(jnp.int32, values.shape, 0) & (LANES - 1)
    edge = 0 if shift == 1 else LANES - 1
    return jnp.where(column == edge, 0.0, pltpu.roll(values, shift % size, 0))


def tap_rows(ref, row, rows, taps, lanes=None):
    parts = []
    for u in range(taps):
        piece = ref[pl.ds(row + u, rows)] if lanes is None else ref[pl.ds(row + u, rows), :, lanes]
        parts.append(piece.reshape(rows * LANES, piece.shape[-1]))
    return jnp.concatenate(parts, axis=-1)


def by_row(values, start, meta, apply):
    first = meta[0] * ROWS + start
    height = meta[3] * ROWS
    done = []
    for r in range(values.shape[0] // LANES):
        inside = (first + r >= 0) & (first + r < height)
        done.append(jnp.where(inside, apply(values[r * LANES : (r + 1) * LANES]), 0.0))
    return jnp.concatenate(done, axis=0)


def relu(x):
    return jnp.maximum(x, 0.0)


def corr_kernel(meta, ids, counts, code, first, own, even, odd, far, pair, pair_even, pair_odd, out, volume):
    tile, core, even_chip = meta[0], meta[1], meta[2]
    frame = first[...].reshape(ROWS * LANES, first.shape[-1])
    plus = pick(core == 0, 1, -1)
    two = pick(even_chip == 1, 2, -2)
    spots = (
        (own, REACH),
        (pair, REACH + plus),
        (even, REACH + two),
        (odd, REACH - two),
        (pair_even, REACH + plus + two),
        (pair_odd, REACH + plus - two),
        (far, REACH - 3 * plus),
    )
    for block, spot in spots:
        for half in range(2):
            rows = block[half * 2 * LANES : (half + 1) * 2 * LANES, :]
            product = lax.dot_general(
                frame, rows, (((1,), (1,)), ((), ())), preferred_element_type=F32
            )
            volume[spot * ROWS + 2 * half] = product[:, :LANES]
            volume[spot * ROWS + 2 * half + 1] = product[:, LANES:]
    scale = 1.0 / math.sqrt(first.shape[-1])
    chunk = 16
    lane = lax.broadcasted_iota(jnp.int32, (chunk, LANES), 1)
    sub = lax.broadcasted_iota(jnp.int32, (chunk, LANES), 0)
    lane_dy = (lane * 57) >> 9
    lane_dx = lane - lane_dy * SIDE
    for n in range(ITERS):
        bits = jnp.int32(0)
        for k in range(ids.shape[2]):
            spot = ids[n, 0, k] - tile + REACH
            listed = (k < counts[n, 0]) & (spot >= 0) & (spot < NB)
            bits = bits | jnp.where(listed, 1 << jnp.clip(spot, 0, NB - 1), 0)

        def step(index, carry, n=n, bits=bits):
            i = index // (LANES // chunk)
            j0 = pl.multiple_of((index % (LANES // chunk)) * chunk, chunk)
            packed = code[n, i, pl.ds(j0, chunk), :]
            packed = jnp.broadcast_to(packed, (chunk, LANES))
            lift = packed >> 6
            across = (packed & 63) - 32
            at = pl.ds(pl.multiple_of(i * LANES + j0, chunk), chunk)
            level = [volume[i + k, at, :] for k in range(2 * FY_MAX + SIDE)]
            for bit in (16, 8, 4, 2, 1):
                on = (lift & bit) != 0
                keep = SIDE + bit - 1 if bit < 16 else 24
                level = [
                    jnp.where(on, level[k + bit], level[k]) if k + bit < len(level) else level[k]
                    for k in range(keep)
                ]
            column = sub + j0 + across + lane_dx - RAD
            wrapped = column & (LANES - 1)
            value = jnp.zeros((chunk, LANES), F32)
            for dy in range(SIDE):
                moved = jnp.take_along_axis(level[dy], wrapped, axis=1, mode="promise_in_bounds")
                value = jnp.where(lane_dy == dy, moved, value)
            block = (lift + i + lane_dy) >> 2
            seen = ((jnp.broadcast_to(bits, (chunk, LANES)) >> block) & 1) == 1
            seen = seen & (column >= 0) & (column < LANES) & (lane < TAPS)
            value = jnp.where(seen, value * scale, 0.0).astype(BF16)
            out[i, pl.ds(j0, chunk), n * LANES : (n + 1) * LANES] = value
            return carry

        lax.fori_loop(0, ROWS * (LANES // chunk), step, 0)


def flow_kernel(meta, patches, w_one, w_two, second, given, first):
    top = 3 * ROWS - FIRST_REACH - 3
    first_rows = ROWS + 2 * FIRST_REACH
    second_rows = ROWS + 2 * SECOND_REACH
    offset = FIRST_REACH - MOTION_REACH

    def one(n, carry):
        for r in range(first_rows):
            window = patches[n, top + r : top + r + 7].reshape(7 * 16, LANES)
            made = lax.dot_general(
                window, w_one[...], (((0,), (0,)), ((), ())), preferred_element_type=F32
            )
            value = by_row(made[:, :LANES], r - FIRST_REACH, meta, relu)
            first[r] = value.astype(BF16)
            if offset <= r < first_rows - offset:
                given[n, r - offset] = made[:, LANES:].astype(BF16)
        step = 2
        for r in range(0, second_rows, step):
            made = jnp.dot(tap_rows(first, r, step, 3), w_two[...], preferred_element_type=F32)
            total = (
                made[:, LANES : 2 * LANES]
                + shift_cols(made[:, :LANES], 1)
                + shift_cols(made[:, 2 * LANES :], -1)
            )
            total = by_row(total, r - SECOND_REACH, meta, relu).astype(BF16)
            second[n, r : r + step] = total.reshape(step, LANES, LANES)
        return carry

    lax.fori_loop(0, ITERS, one, 0)


def motion_kernel(
    meta, own, even, odd, pair, pair_even, pair_odd, second, given, w_corr, w_two, w_three, out, one, two
):
    core, even_chip = meta[0 + 1], meta[2]
    is_even, is_zero = even_chip == 1, core == 0

    def corr_row(row):
        tile, r = (row + 2 * ROWS) // ROWS - 2, row % ROWS
        if tile == 0:
            return own[r]
        if tile == -2:
            return pick(is_even, odd[r], even[r])
        if tile == 2:
            return pick(is_even, even[r], odd[r])
        if tile == -1:
            return pick(is_zero, pick(is_even, pair_odd[r], pair_even[r]), pair[r])
        return pick(is_zero, pair[r], pick(is_even, pair_even[r], pair_odd[r]))

    for r in range(ROWS + 2 * FIRST_REACH):
        made = jnp.dot(corr_row(r - FIRST_REACH), w_corr[...], preferred_element_type=F32)
        one[r] = by_row(made, r - FIRST_REACH, meta, relu).astype(BF16)

    step = 2
    zeros = jnp.zeros((step * LANES, LANES), BF16)

    def second_step(index, carry):
        r = index * step
        left = tap_rows(one, r, step, 3)
        made = [jnp.dot(left, w_two[s], preferred_element_type=F32) for s in range(3)]
        total = made[1] + shift_cols(made[0], 1) + shift_cols(made[2], -1)
        total = by_row(total, r - SECOND_REACH, meta, relu).astype(BF16)
        flow = second[pl.ds(r, step)].reshape(step * LANES, LANES)
        total = total + jnp.concatenate([zeros, flow], axis=-1)
        two[pl.ds(r, step)] = total.reshape(step, LANES, 2 * LANES)
        return carry

    lax.fori_loop(0, (ROWS + 2 * SECOND_REACH) // step, second_step, 0)

    def third_step(index, carry):
        r = index * step
        made = jnp.dot(tap_rows(two, r, step, 3), w_three[...], preferred_element_type=F32)
        total = (
            made[:, LANES : 2 * LANES]
            + shift_cols(made[:, :LANES], 1)
            + shift_cols(made[:, 2 * LANES :], -1)
        )
        total = by_row(total, r - MOTION_REACH, meta, relu).astype(BF16)
        total = total + given[pl.ds(r, step)].reshape(step * LANES, LANES)
        out[pl.ds(r, step)] = total.reshape(step, LANES, LANES)
        return carry

    lax.fori_loop(0, (ROWS + 2 * MOTION_REACH) // step, third_step, 0)


def spread(scratch, lanes, meta, own, across, pair):
    tile, core, tiles = meta[0], meta[1], meta[3]
    is_zero = core == 0
    nothing = jnp.zeros((), BF16)
    for r in range(ROWS):
        above = pick(is_zero, across[r], pair[r])
        below = pick(is_zero, pair[r], across[r])
        scratch[r, :, lanes] = jnp.where(tile > 0, above, nothing)
        scratch[ROWS + r, :, lanes] = own[r]
        scratch[2 * ROWS + r, :, lanes] = jnp.where(tile < tiles - 1, below, nothing)


def gate_kernel(
    meta, h_own, h_across, h_pair, c_own, c_across, c_pair, motion, w_gates, w_cand, out, joined, state, keep
):
    spread(joined, slice(0, LANES), meta, h_own, h_across, h_pair)
    spread(joined, slice(LANES, 2 * LANES), meta, c_own, c_across, c_pair)
    joined[:, :, 2 * LANES :] = motion[...]
    gate_rows = ROWS + 2 * GATE_REACH
    step = 4
    for r in range(0, gate_rows, step):
        left = tap_rows(joined, r, step, 5)
        gates = jnp.dot(left, w_gates[...], preferred_element_type=F32)
        reset = 0.5 * jnp.tanh(0.5 * gates[:, LANES:]) + 0.5
        hidden = joined[r + 2 : r + 2 + step, :, :LANES].reshape(step * LANES, LANES).astype(F32)
        state[r : r + step] = (reset * hidden).astype(BF16).reshape(step, LANES, LANES)
        keep[r : r + step] = gates[:, :LANES].reshape(step, LANES, LANES)
    parts = []
    for u in range(5):
        parts.append(state[u : u + ROWS].reshape(ROWS * LANES, LANES))
        parts.append(joined[u + 2 : u + 2 + ROWS, :, LANES:].reshape(ROWS * LANES, 2 * LANES))
    left = jnp.concatenate(parts, axis=-1)
    candidate = jnp.tanh(jnp.dot(left, w_cand[...], preferred_element_type=F32))
    update = keep[2 : 2 + ROWS].reshape(ROWS * LANES, LANES)
    update = 0.5 * jnp.tanh(0.5 * update) + 0.5
    hidden = h_own[...].reshape(ROWS * LANES, LANES).astype(F32)
    new = (1.0 - update) * hidden + update * candidate
    out[...] = new.astype(BF16).reshape(ROWS, LANES, LANES)


def head_kernel(meta, h_own, h_across, h_pair, w_one, w_two, out, joined, hidden):
    spread(joined, slice(0, LANES), meta, h_own, h_across, h_pair)
    step = 2
    for r in range(0, ROWS + 2, step):
        left = tap_rows(joined, r + 2, step, 3)
        made = [jnp.dot(left, w_one[s], preferred_element_type=F32) for s in range(3)]
        total = made[1] + shift_cols(made[0], 1) + shift_cols(made[2], -1)
        total = by_row(total, r - 1, meta, relu).astype(BF16)
        hidden[r : r + step] = total.reshape(step, LANES, 2 * LANES)
    lane = lax.broadcasted_iota(jnp.int32, (2, LANES), 1)
    for r in range(ROWS):
        made = lax.dot_general(
            w_two[...], tap_rows(hidden, r, 1, 3), (((1,), (1,)), ((), ())), preferred_element_type=F32
        )
        left = jnp.where(lane == 0, 0.0, pltpu.roll(made[0:2], 1, 1))
        right = jnp.where(lane == LANES - 1, 0.0, pltpu.roll(made[4:6], LANES - 1, 1))
        total = left + made[2:4] + right
        out[0, r : r + 1, :] = total[0:1]
        out[1, r : r + 1, :] = total[1:2]


SMEM = pltpu.SMEM
PARAMS = pltpu.CompilerParams(vmem_limit_bytes=VMEM_BYTES)


def call(kernel, args, out_shape, scratch, flops, smem=1, blocks=None):
    specs = []
    for k, arg in enumerate(args):
        if k < smem:
            specs.append(pl.BlockSpec(memory_space=SMEM))
        elif blocks and k in blocks:
            specs.append(blocks[k])
        else:
            specs.append(pl.BlockSpec(memory_space=pltpu.VMEM))
    outs = out_shape if isinstance(out_shape, (list, tuple)) else [out_shape]
    moved = sum(a.size * a.dtype.itemsize for a in args) + sum(
        math.prod(o.shape) * o.dtype.itemsize for o in outs
    )
    return pl.pallas_call(
        kernel,
        out_shape=out_shape,
        grid=(1,) if blocks else (),
        in_specs=specs,
        out_specs=jax.tree.map(lambda o: pl.BlockSpec(memory_space=pltpu.VMEM), out_shape),
        scratch_shapes=scratch,
        compiler_params=PARAMS,
        cost_estimate=pl.CostEstimate(flops=flops, bytes_accessed=moved, transcendentals=0),
    )(*args)


def shards(
    first_frame,
    second_frame,
    context,
    hidden_init,
    flow_rows,
    flow_cols,
    block_ids,
    block_counts,
    w_corr,
    w_corr2,
    w_flow1,
    w_flow2,
    w_motion,
    w_gates,
    w_cand,
    w_head1,
    w_head2,
):
    rows_dev, width, channels = first_frame.shape
    tile_count = lax.axis_size("row")
    tile = lax.axis_index("row")
    core = tile & 1
    even_chip = ((tile >> 1) & 1) ^ 1
    meta = jnp.stack([tile, core, even_chip, jnp.int32(tile_count)]).astype(jnp.int32)
    SDS = jax.ShapeDtypeStruct

    flows = jnp.stack([flow_rows, flow_cols], axis=1).astype(BF16)
    flow_lines = flows.reshape(ITERS * 2 * rows_dev * width // channels, channels)
    pixels = rows_dev * width
    payload = jnp.concatenate(
        [
            second_frame.reshape(pixels, channels),
            jnp.pad(flow_lines, ((0, 16 - flow_lines.shape[0]), (0, 0))),
        ]
    )
    even, odd, far = swap(payload, chip_even), swap(payload, chip_odd), swap(payload, three_away)
    pair = swap(payload, in_chip)
    pair_even, pair_odd = swap(even, in_chip), swap(odd, in_chip)

    corr_w = jnp.pad(w_corr, ((0, LANES - TAPS), (0, 0)))
    second_out = w_corr2.shape[1]
    corr2_w = w_corr2.reshape(3, 3, -1, second_out).transpose(1, 0, 2, 3)
    corr2_w = jnp.pad(corr2_w.reshape(3, -1, second_out), ((0, 0), (0, 0), (0, 256 - second_out)))
    mot = w_motion.shape[1]
    motion_w = w_motion.reshape(3, 3, -1, mot).transpose(0, 2, 1, 3)
    motion_w = jnp.pad(motion_w, ((0, 0), (0, 0), (0, 0), (0, LANES - mot))).reshape(-1, 3 * LANES)
    flow1_w = jnp.pad(w_flow1.reshape(7, 14, -1), ((0, 0), (0, 2), (0, 0))).reshape(7 * 16, -1)
    place = jnp.zeros((7 * 16, LANES), BF16)
    place = place.at[3 * 16 + 6, mot].set(1.0).at[3 * 16 + 7, mot + 1].set(1.0)
    flow1_w = jnp.concatenate([flow1_w, place], axis=1)
    flo2 = w_flow2.shape[1]
    flow2_w = w_flow2.reshape(3, 3, -1, flo2).transpose(0, 2, 1, 3)
    flow2_w = jnp.pad(flow2_w, ((0, 0), (0, 0), (0, 0), (LANES - flo2, 0))).reshape(-1, 3 * LANES)
    head1_w = w_head1.reshape(3, 3, -1, w_head1.shape[1]).transpose(1, 0, 2, 3)
    head1_w = head1_w.reshape(3, -1, w_head1.shape[1])
    head2_w = w_head2.reshape(3, 3, -1, 2).transpose(1, 3, 0, 2).reshape(6, -1)
    head2_w = jnp.pad(head2_w, ((0, 10), (0, 0)))

    code = ((flow_rows + FY_MAX) * 64 + flow_cols + 32)[..., None]
    corr = call(
        corr_kernel,
        [meta, block_ids, block_counts, code, first_frame]
        + [payload, even, odd, far, pair, pair_even, pair_odd],
        SDS((rows_dev, width, 2 * LANES), BF16),
        [pltpu.VMEM((NB * rows_dev, pixels, LANES), F32)],
        2 * pixels * NB * pixels * channels,
        smem=3,
    )
    near = (corr,) + near_tiles(corr)

    lines = flow_lines.shape[0]
    lower = core == 0

    def order(a, b, c, d):
        return jnp.where(lower, jnp.where(even_chip == 1, a, b), jnp.where(even_chip == 1, c, d))

    tails = [x[pixels : pixels + lines] for x in (even, odd, far, pair, pair_even, pair_odd)]
    te, to, tf, tp, tpe, tpo = tails
    band = [
        order(tf, tf, tpo, tpe),
        order(to, te, to, te),
        order(tpo, tpe, tp, tp),
        flow_lines,
        order(tp, tp, tpe, tpo),
        order(te, to, te, to),
        order(tpe, tpo, tf, tf),
    ]
    band = jnp.stack(band).reshape(NB, ITERS, 2, rows_dev, width)
    spots = tile + jnp.arange(-REACH, REACH + 1, dtype=jnp.int32)
    inside = (spots >= 0) & (spots < tile_count)
    band = jnp.where(inside[:, None, None, None, None], band.astype(F32) * FLOW_SCALE, 0.0)
    band = band.astype(BF16).transpose(1, 0, 3, 2, 4).reshape(ITERS, NB * rows_dev, 2, width)
    padded = jnp.pad(band, ((0, 0), (0, 0), (0, 0), (3, 3)))
    patches = jnp.concatenate([padded[..., s : s + width] for s in range(7)], axis=2)
    patches = jnp.pad(patches, ((0, 0), (0, 0), (0, 2), (0, 0)))
    second_rows = rows_dev + 2 * SECOND_REACH
    first_rows = rows_dev + 2 * FIRST_REACH
    motion_rows = rows_dev + 2 * MOTION_REACH
    flow_second, flow_given = call(
        flow_kernel,
        [meta, patches, flow1_w, flow2_w],
        (
            SDS((ITERS, second_rows, width, LANES), BF16),
            SDS((ITERS, motion_rows, width, LANES), BF16),
        ),
        [pltpu.VMEM((first_rows, width, LANES), BF16)],
        2 * ITERS * width * second_rows * 1152 * LANES,
    )

    def motion_of(n):
        def lane_block(shape):
            return pl.BlockSpec(shape[:2] + (LANES,), lambda i: (0, 0, n))

        def whole(shape):
            return pl.BlockSpec((None,) + shape[1:], lambda i: (n, 0, 0, 0))

        blocks = {1 + k: lane_block(x.shape) for k, x in enumerate(near)}
        blocks[7] = whole(flow_second.shape)
        blocks[8] = whole(flow_given.shape)
        return call(
            motion_kernel,
            [meta, *near, flow_second, flow_given, corr_w, corr2_w, motion_w],
            SDS((motion_rows, width, LANES), BF16),
            [
                pltpu.VMEM((first_rows, width, 2 * LANES), BF16),
                pltpu.VMEM((second_rows, width, 2 * LANES), BF16),
            ],
            2 * width * second_rows * 2304 * 256 * 2,
            blocks=blocks,
        )

    def hidden_of(h, h_sides, c, c_sides, motion):
        return call(
            gate_kernel,
            [meta, h, *h_sides, c, *c_sides, motion, w_gates, w_cand],
            SDS((rows_dev, width, LANES), BF16),
            [
                pltpu.VMEM((motion_rows, width, 3 * LANES), BF16),
                pltpu.VMEM((rows_dev + 2 * GATE_REACH, width, LANES), BF16),
                pltpu.VMEM((rows_dev + 2 * GATE_REACH, width, LANES), F32),
            ],
            2 * width * 12 * 1920 * 256,
        )

    def head_of(h, h_sides):
        return call(
            head_kernel,
            [meta, h, *h_sides, head1_w, head2_w],
            SDS((2, rows_dev, width), F32),
            [
                pltpu.VMEM((3 * rows_dev, width, LANES), BF16),
                pltpu.VMEM((rows_dev + 2, width, 2 * LANES), BF16),
            ],
            2 * width * 6 * 1152 * 256,
        )

    h_sides, c_sides = side_tiles(hidden_init), side_tiles(context)
    h_one = hidden_of(hidden_init, h_sides, context, c_sides, motion_of(0))
    one_sides = side_tiles(h_one)
    h_two = hidden_of(h_one, one_sides, context, c_sides, motion_of(1))
    delta_one = head_of(h_one, one_sides)
    delta_two = head_of(h_two, side_tiles(h_two))
    return (h_two, jnp.stack([delta_one, delta_two]))


def solution(mesh):
    tiled = P(("group", "row"), None, None)
    listed = P(None, ("group", "row"), None)
    placed = (tiled,) * 4 + (listed,) * 3 + (P(None, ("group", "row")),) + (P(),) * 9
    return jax.shard_map(
        shards,
        mesh=mesh,
        in_specs=placed,
        out_specs=(tiled, P(None, None, ("group", "row"), None)),
        check_vma=False,
    )
```

```python
import math

import jax
import jax.numpy as jnp
import numpy as np
from jax import lax
from jax.experimental import pallas as pl
from jax.experimental.pallas import tpu as pltpu
from jax.sharding import PartitionSpec as P

RAD = 4
ITERS = 2
REACH = 3
NB = 7
SIDE = 9
TAPS = 81
LANES = 128
FY_MAX = 8
FLOW_SCALE = 0.125
F32 = jnp.float32
BF16 = jnp.bfloat16

ROWS = 4
MOTION_REACH = 4
SECOND_REACH = MOTION_REACH + 1
FIRST_REACH = MOTION_REACH + 2
GATE_REACH = 2


def swap(block, partner):
    devices = lax.axis_size("row")
    route = []
    for i in range(devices):
        j = partner(i)
        route.append((i, j if 0 <= j < devices else i))
    return lax.ppermute(block, "row", route)


def in_chip(i):
    return i ^ 1


def next_row(i):
    return ((i + 1) ^ 1) - 1


def chip_even(i):
    return i ^ 2


def chip_odd(i):
    return ((i + 2) ^ 2) - 2


def three_away(i):
    return i - 3 if i % 2 == 0 else i + 3


def near_tiles(block):
    even, odd = swap(block, chip_even), swap(block, chip_odd)
    return even, odd, swap(block, in_chip), swap(even, in_chip), swap(odd, in_chip)


def side_tiles(block):
    return swap(block, next_row), swap(block, in_chip)


def pick(flag, yes, no):
    return jnp.where(flag, yes, no)


def shift_cols(values, shift):
    size = values.shape[0]
    column = lax.broadcasted_iota(jnp.int32, values.shape, 0) & (LANES - 1)
    edge = 0 if shift == 1 else LANES - 1
    return jnp.where(column == edge, 0.0, pltpu.roll(values, shift % size, 0))


def tap_rows(ref, row, rows, taps, lanes=None):
    parts = []
    for u in range(taps):
        piece = ref[pl.ds(row + u, rows)] if lanes is None else ref[pl.ds(row + u, rows), :, lanes]
        parts.append(piece.reshape(rows * LANES, piece.shape[-1]))
    return jnp.concatenate(parts, axis=-1)


def by_row(values, start, meta, apply):
    first = meta[0] * ROWS + start
    height = meta[3] * ROWS
    done = []
    for r in range(values.shape[0] // LANES):
        inside = (first + r >= 0) & (first + r < height)
        done.append(jnp.where(inside, apply(values[r * LANES : (r + 1) * LANES]), 0.0))
    return jnp.concatenate(done, axis=0)


def turned_dot(left, right):
    return lax.dot_general(left, right, (((1,), (1,)), ((), ())), preferred_element_type=F32)


def relu(x):
    return jnp.maximum(x, 0.0)


def choose(planes, index):
    bit = 1
    while len(planes) > 1:
        on = (index & bit) != 0
        pairs = [
            jnp.where(on, planes[k + 1], planes[k]) if k + 1 < len(planes) else planes[k]
            for k in range(0, len(planes), 2)
        ]
        planes, bit = pairs, 2 * bit
    return planes[0]


def corr_kernel(meta, ids, counts, rows, cols, first, own, even, odd, far, pair, pair_even, pair_odd, out, volume, turned):
    tile, core, even_chip = meta[0], meta[1], meta[2]
    frame = first[...].reshape(ROWS * LANES, first.shape[-1])
    plus = pick(core == 0, 1, -1)
    two = pick(even_chip == 1, 2, -2)
    spots = (
        (own, REACH),
        (pair, REACH + plus),
        (even, REACH + two),
        (odd, REACH - two),
        (pair_even, REACH + plus + two),
        (pair_odd, REACH + plus - two),
        (far, REACH - 3 * plus),
    )
    part = LANES // 8
    for block, spot in spots:
        for half in range(2):
            pieces = []
            for r in (2 * half, 2 * half + 1):
                for m in range(8):
                    source = (m - r - 4 * spot) & 7
                    pieces.append(block[r, pl.ds(pl.multiple_of(source * part, part), part), :])
            product = lax.dot_general(
                frame, jnp.concatenate(pieces, axis=0), (((1,), (1,)), ((), ())), preferred_element_type=F32
            )
            volume[spot * ROWS + 2 * half] = product[:, :LANES]
            volume[spot * ROWS + 2 * half + 1] = product[:, LANES:]
    for n in range(ITERS):
        for i in range(ROWS):
            packed = (rows[n, i : i + 1, :] + FY_MAX) * 64 + cols[n, i : i + 1, :] + 32
            turned[n, i] = jnp.broadcast_to(packed, (LANES, LANES)).T
    scale = 1.0 / math.sqrt(first.shape[-1])
    chunk = 16
    lane = lax.broadcasted_iota(jnp.int32, (chunk, LANES), 1)
    sub = lax.broadcasted_iota(jnp.int32, (chunk, LANES), 0)
    lane_dy = (lane * 57) >> 9
    lane_dx = lane - lane_dy * SIDE - RAD
    for n in range(ITERS):
        bits = jnp.int32(0)
        for k in range(ids.shape[2]):
            spot = ids[n, 0, k] - tile + REACH
            listed = (k < counts[n, 0]) & (spot >= 0) & (spot < NB)
            bits = bits | jnp.where(listed, 1 << jnp.clip(spot, 0, NB - 1), 0)
        for i in range(ROWS):

            def step(index, carry, n=n, bits=bits, i=i):
                j0 = pl.multiple_of(index * chunk, chunk)
                packed = turned[n, i, pl.ds(j0, chunk), :]
                lift = packed >> 6
                start = sub + (j0 - 32) + (packed & 63)
                at = pl.ds(pl.multiple_of(i * LANES + j0, chunk), chunk)
                planes = [volume[i + k, at, :] for k in range(2 * FY_MAX + SIDE)]
                group = ((lane - start + RAD) & (LANES - 1)) >> 4
                most = choose(planes[:24], lift + ((group - lift - i) & 7))
                last = choose(planes[8:], lift)
                column = start + lane_dx
                row = lift + i + lane_dy
                wrapped = (column + (row & 7) * part) & (LANES - 1)
                value = jnp.where(
                    lane_dy == 8,
                    jnp.take_along_axis(last, wrapped, axis=1, mode="promise_in_bounds"),
                    jnp.take_along_axis(most, wrapped, axis=1, mode="promise_in_bounds"),
                )
                seen = ((bits >> (row >> 2)) & 1) == 1
                seen = seen & (column >= 0) & (column < LANES) & (lane < TAPS)
                value = jnp.where(seen, value * scale, 0.0).astype(BF16)
                out[n, i, pl.ds(j0, chunk), :] = value
                return carry

            lax.fori_loop(0, LANES // chunk, step, 0, unroll=8)


def flow_kernel(meta, patches, w_one, w_flow2, second, given, first, w_two):
    w_two[...] = jnp.zeros(w_two.shape, BF16)
    made, wide = w_flow2.shape[0], first.shape[2]
    for u in range(3):
        for s in range(3):
            low = (s + 1) * LANES - made
            tap = slice((u * 3 + s) * wide, (u * 3 + s + 1) * wide)
            w_two[low : low + made, u * wide : (u + 1) * wide] = w_flow2[:, tap]
    top = 3 * ROWS - FIRST_REACH - 3
    first_rows = ROWS + 2 * FIRST_REACH
    second_rows = ROWS + 2 * SECOND_REACH
    offset = FIRST_REACH - MOTION_REACH

    def one(n, carry):
        for r in range(first_rows):
            window = patches[n, top + r : top + r + 7].reshape(7 * 16, LANES)
            made = lax.dot_general(
                window, w_one[...], (((0,), (0,)), ((), ())), preferred_element_type=F32
            )
            value = by_row(made[:, :LANES], r - FIRST_REACH, meta, relu)
            first[r] = value.astype(BF16)
            if offset <= r < first_rows - offset:
                given[n, r - offset] = made[:, LANES:].astype(BF16)
        step = 2
        for r in range(0, second_rows, step):
            made = turned_dot(tap_rows(first, r, step, 3), w_two[...])
            total = (
                made[:, LANES : 2 * LANES]
                + shift_cols(made[:, :LANES], 1)
                + shift_cols(made[:, 2 * LANES :], -1)
            )
            total = by_row(total, r - SECOND_REACH, meta, relu).astype(BF16)
            second[n, r : r + step] = total.reshape(step, LANES, LANES)
        return carry

    lax.fori_loop(0, ITERS, one, 0)


def motion_kernel(
    meta, own, even, odd, pair, pair_even, pair_odd, second, given, w_corr, w_corr2, w_motion, out, one, two, w_one, w_two, w_three
):
    core, even_chip = meta[1], meta[2]
    is_even, is_zero = even_chip == 1, core == 0

    w_one[...] = jnp.zeros(w_one.shape, BF16)
    w_one[: w_corr.shape[0], :] = w_corr[...]
    w_three[...] = jnp.zeros(w_three.shape, BF16)
    wide, made_two, made_three = w_one.shape[1], w_corr2.shape[0], w_motion.shape[1]
    w_two[:, made_two:, :] = jnp.zeros((3, w_two.shape[1] - made_two, w_two.shape[2]), BF16)
    for u in range(3):
        for s in range(3):
            tap = slice((u * 3 + s) * wide, (u * 3 + s + 1) * wide)
            w_two[s, :made_two, u * wide : (u + 1) * wide] = w_corr2[:, tap]
            w_three[u * wide : (u + 1) * wide, s * LANES : s * LANES + made_three] = w_motion[tap, :]

    def corr_row(row):
        tile, r = (row + 2 * ROWS) // ROWS - 2, row % ROWS
        if tile == 0:
            return own[r]
        if tile == -2:
            return pick(is_even, odd[r], even[r])
        if tile == 2:
            return pick(is_even, even[r], odd[r])
        if tile == -1:
            return pick(is_zero, pick(is_even, pair_odd[r], pair_even[r]), pair[r])
        return pick(is_zero, pair[r], pick(is_even, pair_even[r], pair_odd[r]))

    for r in range(ROWS + 2 * FIRST_REACH):
        made = jnp.dot(corr_row(r - FIRST_REACH), w_one[...], preferred_element_type=F32)
        one[r] = by_row(made, r - FIRST_REACH, meta, relu).astype(BF16)

    step = 2
    zeros = jnp.zeros((step * LANES, LANES), BF16)

    def second_step(index, carry):
        r = index * step
        left = tap_rows(one, r, step, 3)
        made = [turned_dot(left, w_two[s]) for s in range(3)]
        total = made[1] + shift_cols(made[0], 1) + shift_cols(made[2], -1)
        total = by_row(total, r - SECOND_REACH, meta, relu).astype(BF16)
        flow = second[pl.ds(r, step)].reshape(step * LANES, LANES)
        total = total + jnp.concatenate([zeros, flow], axis=-1)
        two[pl.ds(r, step)] = total.reshape(step, LANES, 2 * LANES)
        return carry

    lax.fori_loop(0, (ROWS + 2 * SECOND_REACH) // step, second_step, 0, unroll=7)

    step3 = 2

    def third_step(index, carry):
        r = index * step3
        made = jnp.dot(tap_rows(two, r, step3, 3), w_three[...], preferred_element_type=F32)
        total = (
            made[:, LANES : 2 * LANES]
            + shift_cols(made[:, :LANES], 1)
            + shift_cols(made[:, 2 * LANES :], -1)
        )
        total = by_row(total, r - MOTION_REACH, meta, relu).astype(BF16)
        total = total + given[pl.ds(r, step3)].reshape(step3 * LANES, LANES)
        out[pl.ds(r, step3)] = total.reshape(step3, LANES, LANES)
        return carry

    lax.fori_loop(0, (ROWS + 2 * MOTION_REACH) // step3, third_step, 0, unroll=6)


def spread(scratch, lanes, meta, own, across, pair):
    tile, core, tiles = meta[0], meta[1], meta[3]
    is_zero = core == 0
    nothing = jnp.zeros((), BF16)
    for r in range(ROWS):
        above = pick(is_zero, across[r], pair[r])
        below = pick(is_zero, pair[r], across[r])
        scratch[r, :, lanes] = jnp.where(tile > 0, above, nothing)
        scratch[ROWS + r, :, lanes] = own[r]
        scratch[2 * ROWS + r, :, lanes] = jnp.where(tile < tiles - 1, below, nothing)


def gate_kernel(
    meta, h_own, h_across, h_pair, c_own, c_across, c_pair, motion, w_gates, w_cand, out, joined, state, keep
):
    spread(joined, slice(0, LANES), meta, h_own, h_across, h_pair)
    spread(joined, slice(LANES, 2 * LANES), meta, c_own, c_across, c_pair)
    joined[:, :, 2 * LANES :] = motion[...]
    gate_rows = ROWS + 2 * GATE_REACH
    step = 4
    for r in range(0, gate_rows, step):
        left = tap_rows(joined, r, step, 5)
        gates = jnp.dot(left, w_gates[...], preferred_element_type=F32)
        reset = 0.5 * jnp.tanh(0.5 * gates[:, LANES:]) + 0.5
        hidden = joined[r + 2 : r + 2 + step, :, :LANES].reshape(step * LANES, LANES).astype(F32)
        state[r : r + step] = (reset * hidden).astype(BF16).reshape(step, LANES, LANES)
        keep[r : r + step] = gates[:, :LANES].reshape(step, LANES, LANES)
    parts = []
    for u in range(5):
        parts.append(state[u : u + ROWS].reshape(ROWS * LANES, LANES))
        parts.append(joined[u + 2 : u + 2 + ROWS, :, LANES:].reshape(ROWS * LANES, 2 * LANES))
    left = jnp.concatenate(parts, axis=-1)
    candidate = jnp.tanh(jnp.dot(left, w_cand[...], preferred_element_type=F32))
    update = keep[2 : 2 + ROWS].reshape(ROWS * LANES, LANES)
    update = 0.5 * jnp.tanh(0.5 * update) + 0.5
    hidden = h_own[...].reshape(ROWS * LANES, LANES).astype(F32)
    new = (1.0 - update) * hidden + update * candidate
    out[...] = new.astype(BF16).reshape(ROWS, LANES, LANES)


def head_kernel(meta, h_own, h_across, h_pair, w_head1, w_head2, *rest):
    before, out, joined, hidden, w_two = rest if len(rest) == 5 else (None,) + rest
    spread(joined, slice(0, LANES), meta, h_own, h_across, h_pair)
    deep, wide = h_own.shape[2], w_head1.shape[1]
    w_two[...] = jnp.zeros(w_two.shape, F32)
    for s in range(3):
        for u in range(3):
            k = u * 3 + s
            w_two[2 * s : 2 * s + 2, u * wide : (u + 1) * wide] = w_head2[:, k * wide : (k + 1) * wide].astype(F32)
    step = 2
    for r in range(0, ROWS + 2, step):
        left = tap_rows(joined, r + 2, step, 3)
        made = []
        for s in range(3):
            taps = [w_head1[(u * 3 + s) * deep : (u * 3 + s + 1) * deep, :] for u in range(3)]
            made.append(jnp.dot(left, jnp.concatenate(taps, axis=0), preferred_element_type=F32))
        total = made[1] + shift_cols(made[0], 1) + shift_cols(made[2], -1)
        total = by_row(total, r - 1, meta, relu).astype(BF16)
        hidden[r : r + step] = total.reshape(step, LANES, 2 * LANES)
    lane = lax.broadcasted_iota(jnp.int32, (2, LANES), 1)
    target = out
    if before is not None:
        out[0] = before[...]
        target = out.at[1]
    made_all = turned_dot(w_two[...].astype(BF16), tap_rows(hidden, 0, ROWS, 3))
    for r in range(ROWS):
        made = made_all[:, r * LANES : (r + 1) * LANES]
        left = jnp.where(lane == 0, 0.0, pltpu.roll(made[0:2], 1, 1))
        right = jnp.where(lane == LANES - 1, 0.0, pltpu.roll(made[4:6], LANES - 1, 1))
        total = left + made[2:4] + right
        target[0, r : r + 1, :] = total[0:1]
        target[1, r : r + 1, :] = total[1:2]


SMEM = pltpu.SMEM
MIB = 1024 * 1024


def call(kernel, args, out_shape, scratch, flops, smem=1, blocks=None, vmem=20):
    specs = []
    for k, arg in enumerate(args):
        if k < smem:
            specs.append(pl.BlockSpec(memory_space=SMEM))
        elif blocks and k in blocks:
            specs.append(blocks[k])
        else:
            specs.append(pl.BlockSpec(memory_space=pltpu.VMEM))
    outs = out_shape if isinstance(out_shape, (list, tuple)) else [out_shape]
    moved = sum(a.size * a.dtype.itemsize for a in args) + sum(
        math.prod(o.shape) * o.dtype.itemsize for o in outs
    )
    return pl.pallas_call(
        kernel,
        out_shape=out_shape,
        grid=(1,) if blocks else (),
        in_specs=specs,
        out_specs=jax.tree.map(lambda o: pl.BlockSpec(memory_space=pltpu.VMEM), out_shape),
        scratch_shapes=scratch,
        compiler_params=pltpu.CompilerParams(vmem_limit_bytes=vmem * MIB),
        cost_estimate=pl.CostEstimate(flops=flops, bytes_accessed=moved, transcendentals=0),
    )(*args)


def shards(
    first_frame,
    second_frame,
    context,
    hidden_init,
    flow_rows,
    flow_cols,
    block_ids,
    block_counts,
    w_corr,
    w_corr2,
    w_flow1,
    w_flow2,
    w_motion,
    w_gates,
    w_cand,
    w_head1,
    w_head2,
):
    rows_dev, width, channels = first_frame.shape
    tile_count = lax.axis_size("row")
    tile = lax.axis_index("row")
    core = tile & 1
    even_chip = ((tile >> 1) & 1) ^ 1
    meta = jnp.stack([tile, core, even_chip, jnp.int32(tile_count)]).astype(jnp.int32)
    SDS = jax.ShapeDtypeStruct
    VM = pltpu.VMEM
    pixels = rows_dev * width

    even, odd, far = swap(second_frame, chip_even), swap(second_frame, chip_odd), swap(second_frame, three_away)
    pair = swap(second_frame, in_chip)
    pair_even, pair_odd = swap(even, in_chip), swap(odd, in_chip)
    flows = jnp.stack([flow_rows, flow_cols], axis=2).astype(F32) * FLOW_SCALE
    gathered = lax.all_gather(flows.astype(BF16), "row", axis=1, tiled=True)

    corr = call(
        corr_kernel,
        [meta, block_ids, block_counts, flow_rows, flow_cols, first_frame]
        + [second_frame, even, odd, far, pair, pair_even, pair_odd],
        SDS((ITERS, rows_dev, width, LANES), BF16),
        [VM((NB * rows_dev, pixels, LANES), F32), VM((ITERS, rows_dev, width, LANES), jnp.int32)],
        2 * pixels * NB * pixels * channels,
        smem=3,
    )
    near = (corr,) + near_tiles(corr)

    around = REACH * rows_dev
    padded = jnp.pad(gathered, ((0, 0), (around, around), (0, 0), (3, 3)))
    band = lax.dynamic_slice_in_dim(padded, tile * rows_dev, NB * rows_dev, axis=1)
    patches = jnp.concatenate([band[..., s : s + width] for s in range(7)], axis=2)
    patches = jnp.pad(patches, ((0, 0), (0, 0), (0, 2), (0, 0)))
    mot = w_motion.shape[1]
    flow1_w = jnp.pad(w_flow1.reshape(7, 14, -1), ((0, 0), (0, 2), (0, 0))).reshape(7 * 16, -1)
    place = np.zeros((7 * 16, LANES), np.float32)
    place[3 * 16 + 6, mot] = place[3 * 16 + 7, mot + 1] = 1.0
    flow1_w = jnp.concatenate([flow1_w, jnp.asarray(place, BF16)], axis=1)
    second_rows = rows_dev + 2 * SECOND_REACH
    first_rows = rows_dev + 2 * FIRST_REACH
    motion_rows = rows_dev + 2 * MOTION_REACH
    flow_second, flow_given = call(
        flow_kernel,
        [meta, patches, flow1_w, w_flow2.T],
        (
            SDS((ITERS, second_rows, width, LANES), BF16),
            SDS((ITERS, motion_rows, width, LANES), BF16),
        ),
        [VM((first_rows, width, LANES), BF16), VM((3 * LANES, 3 * LANES), BF16)],
        2 * ITERS * width * second_rows * 1152 * LANES,
    )

    def motion_of(n):
        def part(shape):
            return pl.BlockSpec((None,) + shape[1:], lambda i: (n, 0, 0, 0))

        tiles = [*near, flow_second, flow_given]
        return call(
            motion_kernel,
            [meta, *tiles, w_corr, w_corr2.T, w_motion],
            SDS((motion_rows, width, LANES), BF16),
            [
                VM((first_rows, width, 2 * LANES), BF16),
                VM((second_rows, width, 2 * LANES), BF16),
                VM((LANES, w_corr.shape[1]), BF16),
                VM((3, 2 * LANES, 3 * w_corr.shape[1]), BF16),
                VM((3 * 2 * LANES, 3 * LANES), BF16),
            ],
            2 * width * second_rows * 2304 * 256 * 2,
            blocks={1 + k: part(x.shape) for k, x in enumerate(tiles)},
        )

    def hidden_of(h, h_sides, c, c_sides, motion):
        return call(
            gate_kernel,
            [meta, h, *h_sides, c, *c_sides, motion, w_gates, w_cand],
            SDS((rows_dev, width, LANES), BF16),
            [
                VM((motion_rows, width, 3 * LANES), BF16),
                VM((rows_dev + 2 * GATE_REACH, width, LANES), BF16),
                VM((rows_dev + 2 * GATE_REACH, width, LANES), F32),
            ],
            2 * width * 12 * 1920 * 256,
        )

    def head_of(h, h_sides, before=()):
        shape = (2, rows_dev, width)
        return call(
            head_kernel,
            [meta, h, *h_sides, w_head1, w_head2.T, *before],
            SDS((ITERS,) + shape if before else shape, F32),
            [
                VM((3 * rows_dev, width, LANES), BF16),
                VM((rows_dev + 2, width, 2 * LANES), BF16),
                VM((8, 3 * w_head1.shape[1]), F32),
            ],
            2 * width * 6 * 1152 * 256,
        )

    later = lax.optimization_barrier((hidden_init, context, corr))
    h_sides, c_sides = side_tiles(later[0]), side_tiles(later[1])
    h_one = hidden_of(hidden_init, h_sides, context, c_sides, motion_of(0))
    one_sides = side_tiles(h_one)
    h_two = hidden_of(h_one, one_sides, context, c_sides, motion_of(1))
    delta_one = head_of(h_one, one_sides)
    deltas = head_of(h_two, side_tiles(h_two), (delta_one,))
    return (h_two, deltas)


def solution(mesh):
    tiled = P(("group", "row"), None, None)
    listed = P(None, ("group", "row"), None)
    placed = (tiled,) * 4 + (listed,) * 3 + (P(None, ("group", "row")),) + (P(),) * 9
    return jax.shard_map(
        shards,
        mesh=mesh,
        in_specs=placed,
        out_specs=(tiled, P(None, None, ("group", "row"), None)),
        check_vma=False,
    )
```

```python
import math

import jax
import jax.numpy as jnp
import numpy as np
from jax import lax
from jax.experimental import pallas as pl
from jax.experimental.pallas import tpu as pltpu
from jax.sharding import PartitionSpec as P

RAD = 4
ITERS = 2
REACH = 3
NB = 7
SIDE = 9
TAPS = 81
LANES = 128
FY_MAX = 8
K_MAX = 4
DEPTH = 96
LISTS = 4
FLOW_SCALE = 0.125
F32 = jnp.float32
BF16 = jnp.bfloat16

ROWS = 4
MOTION_REACH = 4
SECOND_REACH = MOTION_REACH + 1
FIRST_REACH = MOTION_REACH + 2
GATE_REACH = 2


def swap(block, partner):
    devices = lax.axis_size("row")
    route = []
    for i in range(devices):
        j = partner(i)
        route.append((i, j if 0 <= j < devices else i))
    return lax.ppermute(block, "row", route)


def in_chip(i):
    return i ^ 1


def next_row(i):
    return ((i + 1) ^ 1) - 1


def chip_even(i):
    return i ^ 2


def chip_odd(i):
    return ((i + 2) ^ 2) - 2


def three_away(i):
    return i - 3 if i % 2 == 0 else i + 3


def relay(block):
    devices = lax.axis_size("row")
    chips, route = devices // 2, []
    for i in range(devices):
        chip = i // 2
        goal = chip + 2 if chip % 2 == 0 else chip - 2
        if not 0 <= goal < chips:
            goal = chip ^ 1
        route.append((i, 2 * goal + i % 2))
    return lax.ppermute(block, "row", route)


def side_tiles(block):
    return swap(block, next_row), swap(block, in_chip)


def pick(flag, yes, no):
    return jnp.where(flag, yes, no)


def shift_cols(values, shift):
    size = values.shape[0]
    column = lax.broadcasted_iota(jnp.int32, values.shape, 0) & (LANES - 1)
    edge = 0 if shift == 1 else LANES - 1
    return jnp.where(column == edge, 0.0, pltpu.roll(values, shift % size, 0))


def tap_rows(ref, row, rows, taps, lanes=None):
    parts = []
    for u in range(taps):
        piece = ref[pl.ds(row + u, rows)] if lanes is None else ref[pl.ds(row + u, rows), :, lanes]
        parts.append(piece.reshape(rows * LANES, piece.shape[-1]))
    return jnp.concatenate(parts, axis=-1)


def by_row(values, start, meta, apply):
    first = meta[0] * ROWS + start
    height = meta[3] * ROWS
    done = []
    for r in range(values.shape[0] // LANES):
        inside = (first + r >= 0) & (first + r < height)
        done.append(jnp.where(inside, apply(values[r * LANES : (r + 1) * LANES]), 0.0))
    return jnp.concatenate(done, axis=0)


def turned_dot(left, right):
    return lax.dot_general(left, right, (((1,), (1,)), ((), ())), preferred_element_type=F32)


def relu(x):
    return jnp.maximum(x, 0.0)


def choose(planes, index):
    bit = 1
    while len(planes) > 1:
        on = (index & bit) != 0
        pairs = [
            jnp.where(on, planes[k + 1], planes[k]) if k + 1 < len(planes) else planes[k]
            for k in range(0, len(planes), 2)
        ]
        planes, bit = pairs, 2 * bit
    return planes[0]


PART = LANES // 8


def volume_of(frame, block, spot, half):
    pieces = []
    for r in (2 * half, 2 * half + 1):
        for m in range(8):
            start = r * LANES + ((m - r - 4 * spot) & 7) * PART
            start = start if isinstance(start, int) else pl.multiple_of(start, PART)
            pieces.append(block[pl.ds(start, PART), :])
    return turned_dot(frame, jnp.concatenate(pieces, axis=0))


def stage_kernel(rows, cols, first, own, hidden, context, frame, own_volume, turned, both, sems):
    frame[...] = first[...]
    copies = [
        pltpu.make_async_copy(hidden, both.at[:, :, :LANES], sems.at[0]),
        pltpu.make_async_copy(context, both.at[:, :, LANES:], sems.at[1]),
    ]
    for copy in copies:
        copy.start()
    for half in range(2):
        product = volume_of(frame[...], own, REACH, half)
        own_volume[2 * half] = product[:, :LANES]
        own_volume[2 * half + 1] = product[:, LANES:]
    for n in range(ITERS):
        for i in range(ROWS):
            packed = (rows[n, i : i + 1, :] + FY_MAX) * 64 + cols[n, i : i + 1, :] + 32
            turned[n, i] = jnp.broadcast_to(packed, (LANES, LANES)).T
    for copy in copies:
        copy.wait()


def corr_kernel(meta, frame, own_volume, turned, even, odd, far, pair, pair_even, pair_odd, out, volume, picked):
    tile, core, even_chip = meta[0], meta[1], meta[2]
    plus = pick(core == 0, 1, -1)
    two = pick(even_chip == 1, 2, -2)
    spots = (
        (pair, REACH + plus),
        (far, REACH - 3 * plus),
        (even, REACH + two),
        (odd, REACH - two),
        (pair_even, REACH + plus + two),
        (pair_odd, REACH + plus - two),
    )
    for block, spot in spots:
        for half in range(2):
            product = volume_of(frame[...], block, spot, half)
            volume[spot * ROWS + 2 * half] = product[:, :LANES]
            volume[spot * ROWS + 2 * half + 1] = product[:, LANES:]

    def plane(b, at):
        own = b - REACH * ROWS
        return own_volume[own, at, :] if 0 <= own < ROWS else volume[b, at, :]

    scale = 1.0 / math.sqrt(frame.shape[-1])
    chunk = 16
    lane = lax.broadcasted_iota(jnp.int32, (chunk, LANES), 1)
    sub = lax.broadcasted_iota(jnp.int32, (chunk, LANES), 0)
    lane_dy = (lane * 57) >> 9
    lane_dx = lane - lane_dy * SIDE - RAD
    for n in range(ITERS):
        bits = jnp.int32(0)
        for k in range(K_MAX):
            spot = meta[LISTS + n * K_MAX + k] - tile + REACH
            listed = (k < meta[LISTS + ITERS * K_MAX + n]) & (spot >= 0) & (spot < NB)
            bits = bits | jnp.where(listed, 1 << jnp.clip(spot, 0, NB - 1), 0)
        for i in range(ROWS):

            def step(index, carry, n=n, bits=bits, i=i):
                j0 = pl.multiple_of(index * chunk, chunk)
                packed = turned[n, i, pl.ds(j0, chunk), :]
                lift = packed >> 6
                start = sub + (j0 - 32) + (packed & 63)
                at = pl.ds(pl.multiple_of(i * LANES + j0, chunk), chunk)
                planes = [plane(i + k, at) for k in range(2 * FY_MAX + SIDE)]
                group = ((lane - start + RAD) & (LANES - 1)) >> 4
                most = choose(planes[:24], lift + ((group - lift - i) & 7))
                last = choose(planes[8:], lift)
                column = start + lane_dx
                row = lift + i + lane_dy
                wrapped = (column + (row & 7) * PART) & (LANES - 1)
                value = jnp.where(
                    lane_dy == 8,
                    jnp.take_along_axis(last, wrapped, axis=1, mode="promise_in_bounds"),
                    jnp.take_along_axis(most, wrapped, axis=1, mode="promise_in_bounds"),
                )
                seen = ((bits >> (row >> 2)) & 1) == 1
                seen = seen & (column >= 0) & (column < LANES) & (lane < TAPS)
                picked[pl.ds(j0, chunk), :] = jnp.where(seen, value * scale, 0.0)
                return carry

            lax.fori_loop(0, LANES // chunk, step, 0, unroll=8)
            out[n, i] = picked[...].T[:DEPTH].astype(BF16)


def flow_kernel(
    meta, own, even, odd, far, pair, pair_even, pair_odd, w_flow1, w_flow2, second, given, first, w_one, w_two, windows
):
    made, wide = w_flow2.shape[0], first.shape[2]
    w_two[...] = jnp.zeros(w_two.shape, BF16)
    for u in range(3):
        for s in range(3):
            low = (s + 1) * LANES - made
            tap = slice((u * 3 + s) * wide, (u * 3 + s + 1) * wide)
            w_two[low : low + made, u * wide : (u + 1) * wide] = w_flow2[:, tap]
    weights = w_flow1[...].astype(F32)
    w_one[...] = jnp.zeros(w_one.shape, F32)
    for u in range(7):
        w_one[u, 0:14, :LANES] = weights[u * 14 : (u + 1) * 14, :]
    tap = lax.broadcasted_iota(jnp.int32, (16, LANES), 0)
    lane = lax.broadcasted_iota(jnp.int32, (16, LANES), 1)
    w_one[3, :, LANES:] = jnp.where((tap - 6 == lane - (LANES - 2)) & (lane >= LANES - 2), 1.0, 0.0)
    w_all = w_one[...].reshape(7 * 16, 2 * LANES).astype(BF16)

    tile, core, even_chip, tiles = meta[0], meta[1], meta[2], meta[3]
    plus = pick(core == 0, 1, -1)
    two = pick(even_chip == 1, 2, -2)
    spots = (
        (own, 0),
        (pair, plus),
        (far, -3 * plus),
        (even, two),
        (odd, -two),
        (pair_even, plus + two),
        (pair_odd, plus - two),
    )
    windows[:, :, 14:, :] = jnp.zeros(windows.shape[:2] + (2, LANES), F32)
    column = lax.broadcasted_iota(jnp.int32, (4 * ROWS, LANES), 1)
    for block, spot in spots:
        inside = (tile + spot >= 0) & (tile + spot < tiles)
        lines = jnp.where(inside, block[ROWS * LANES :, :LANES].astype(F32) * FLOW_SCALE, 0.0)
        for s in range(7):
            reach = s - 3
            moved = pltpu.roll(lines, (-reach) % LANES, 1) if reach else lines
            seen = (column + reach >= 0) & (column + reach < LANES)
            moved = jnp.where(seen, moved, 0.0)
            for c in range(2):
                for n in range(ITERS):
                    for r in range(ROWS):
                        k = (c * ITERS + n) * ROWS + r
                        windows[n, (spot + REACH) * ROWS + r, 2 * s + c : 2 * s + c + 1, :] = moved[k : k + 1, :]

    top = 3 * ROWS - FIRST_REACH - 3
    first_rows = ROWS + 2 * FIRST_REACH
    second_rows = ROWS + 2 * SECOND_REACH
    offset = FIRST_REACH - MOTION_REACH
    for n in range(ITERS):
        for r in range(first_rows):
            window = windows[n, top + r : top + r + 7].reshape(7 * 16, LANES).astype(BF16)
            made = lax.dot_general(window, w_all, (((0,), (0,)), ((), ())), preferred_element_type=F32)
            value = by_row(made[:, :LANES], r - FIRST_REACH, meta, relu)
            first[r] = value.astype(BF16)
            if offset <= r < first_rows - offset:
                given[n, r - offset] = made[:, LANES:].astype(BF16)
        step = 2
        for r in range(0, second_rows, step):
            made = turned_dot(tap_rows(first, r, step, 3), w_two[...])
            total = (
                made[:, LANES : 2 * LANES]
                + shift_cols(made[:, :LANES], 1)
                + shift_cols(made[:, 2 * LANES :], -1)
            )
            total = by_row(total, r - SECOND_REACH, meta, relu).astype(BF16)
            second[n, r : r + step] = total.reshape(step, LANES, LANES)


def motion_kernel(
    meta, own, even, odd, pair, pair_even, pair_odd, second, given, w_corr, w_corr2, w_motion, out, one, two, w_one, w_two, w_three
):
    core, even_chip = meta[1], meta[2]
    is_even, is_zero = even_chip == 1, core == 0

    w_one[...] = jnp.zeros(w_one.shape, BF16)
    w_one[: w_corr.shape[0], :] = w_corr[...]
    w_three[...] = jnp.zeros(w_three.shape, BF16)
    wide, made_two, made_three = w_one.shape[1], w_corr2.shape[0], w_motion.shape[1]
    w_two[:, made_two:, :] = jnp.zeros((3, w_two.shape[1] - made_two, w_two.shape[2]), BF16)
    for u in range(3):
        for s in range(3):
            tap = slice((u * 3 + s) * wide, (u * 3 + s + 1) * wide)
            w_two[s, :made_two, u * wide : (u + 1) * wide] = w_corr2[:, tap]
            w_three[u * wide : (u + 1) * wide, s * LANES : s * LANES + made_three] = w_motion[tap, :]

    def corr_row(row):
        tile, r = (row + 2 * ROWS) // ROWS - 2, row % ROWS
        if tile == 0:
            return own[r]
        if tile == -2:
            return pick(is_even, odd[r], even[r])
        if tile == 2:
            return pick(is_even, even[r], odd[r])
        if tile == -1:
            return pick(is_zero, pick(is_even, pair_odd[r], pair_even[r]), pair[r])
        return pick(is_zero, pair[r], pick(is_even, pair_even[r], pair_odd[r]))

    for r in range(ROWS + 2 * FIRST_REACH):
        made = lax.dot_general(
            corr_row(r - FIRST_REACH), w_one[...], (((0,), (0,)), ((), ())), preferred_element_type=F32
        )
        one[r] = by_row(made, r - FIRST_REACH, meta, relu).astype(BF16)

    step = 2
    zeros = jnp.zeros((step * LANES, LANES), BF16)

    def second_step(index, carry):
        r = index * step
        left = tap_rows(one, r, step, 3)
        made = [turned_dot(left, w_two[s]) for s in range(3)]
        total = made[1] + shift_cols(made[0], 1) + shift_cols(made[2], -1)
        total = by_row(total, r - SECOND_REACH, meta, relu).astype(BF16)
        flow = second[pl.ds(r, step)].reshape(step * LANES, LANES)
        total = total + jnp.concatenate([zeros, flow], axis=-1)
        two[pl.ds(r, step)] = total.reshape(step, LANES, 2 * LANES)
        return carry

    lax.fori_loop(0, (ROWS + 2 * SECOND_REACH) // step, second_step, 0, unroll=7)

    step3 = 2

    def third_step(index, carry):
        r = index * step3
        made = jnp.dot(tap_rows(two, r, step3, 3), w_three[...], preferred_element_type=F32)
        total = (
            made[:, LANES : 2 * LANES]
            + shift_cols(made[:, :LANES], 1)
            + shift_cols(made[:, 2 * LANES :], -1)
        )
        total = by_row(total, r - MOTION_REACH, meta, relu).astype(BF16)
        total = total + given[pl.ds(r, step3)].reshape(step3 * LANES, LANES)
        out[pl.ds(r, step3)] = total.reshape(step3, LANES, LANES)
        return carry

    lax.fori_loop(0, (ROWS + 2 * MOTION_REACH) // step3, third_step, 0, unroll=6)


def spread(scratch, lanes, meta, own, across, pair):
    tile, core, tiles = meta[0], meta[1], meta[3]
    is_zero = core == 0
    nothing = jnp.zeros((), BF16)
    for r in range(ROWS):
        above = pick(is_zero, across[r], pair[r])
        below = pick(is_zero, pair[r], across[r])
        scratch[r, :, lanes] = jnp.where(tile > 0, above, nothing)
        scratch[ROWS + r, :, lanes] = own[r]
        scratch[2 * ROWS + r, :, lanes] = jnp.where(tile < tiles - 1, below, nothing)


def gate_kernel(
    meta, both, both_across, both_pair, motion, w_gates, w_cand, *rest
):
    h_own, h_across, h_pair, out, joined, state, keep = rest if len(rest) == 7 else (None,) * 3 + rest
    spread(joined, slice(0, 2 * LANES), meta, both, both_across, both_pair)
    if h_own is not None:
        spread(joined, slice(0, LANES), meta, h_own, h_across, h_pair)
    joined[:, :, 2 * LANES :] = motion[...]
    gate_rows = ROWS + 2 * GATE_REACH
    step = 4
    for r in range(0, gate_rows, step):
        left = tap_rows(joined, r, step, 5)
        gates = jnp.dot(left, w_gates[...], preferred_element_type=F32)
        reset = 0.5 * jnp.tanh(0.5 * gates[:, LANES:]) + 0.5
        hidden = joined[r + 2 : r + 2 + step, :, :LANES].reshape(step * LANES, LANES).astype(F32)
        state[r : r + step] = (reset * hidden).astype(BF16).reshape(step, LANES, LANES)
        keep[r : r + step] = gates[:, :LANES].reshape(step, LANES, LANES)
    parts = []
    for u in range(5):
        parts.append(state[u : u + ROWS].reshape(ROWS * LANES, LANES))
        parts.append(joined[u + 2 : u + 2 + ROWS, :, LANES:].reshape(ROWS * LANES, 2 * LANES))
    left = jnp.concatenate(parts, axis=-1)
    candidate = jnp.tanh(jnp.dot(left, w_cand[...], preferred_element_type=F32))
    update = keep[2 : 2 + ROWS].reshape(ROWS * LANES, LANES)
    update = 0.5 * jnp.tanh(0.5 * update) + 0.5
    hidden = joined[ROWS : 2 * ROWS, :, :LANES].reshape(ROWS * LANES, LANES).astype(F32)
    new = (1.0 - update) * hidden + update * candidate
    out[...] = new.astype(BF16).reshape(ROWS, LANES, LANES)


def head_kernel(meta, h_own, h_across, h_pair, w_head1, w_head2, *rest):
    before, out, joined, hidden, w_two = rest if len(rest) == 5 else (None,) + rest
    spread(joined, slice(0, LANES), meta, h_own, h_across, h_pair)
    deep, wide = h_own.shape[2], w_head1.shape[1]
    w_two[...] = jnp.zeros(w_two.shape, F32)
    for s in range(3):
        for u in range(3):
            k = u * 3 + s
            w_two[2 * s : 2 * s + 2, u * wide : (u + 1) * wide] = w_head2[:, k * wide : (k + 1) * wide].astype(F32)
    step = 2
    for r in range(0, ROWS + 2, step):
        left = tap_rows(joined, r + 2, step, 3)
        made = []
        for s in range(3):
            taps = [w_head1[(u * 3 + s) * deep : (u * 3 + s + 1) * deep, :] for u in range(3)]
            made.append(jnp.dot(left, jnp.concatenate(taps, axis=0), preferred_element_type=F32))
        total = made[1] + shift_cols(made[0], 1) + shift_cols(made[2], -1)
        total = by_row(total, r - 1, meta, relu).astype(BF16)
        hidden[r : r + step] = total.reshape(step, LANES, 2 * LANES)
    lane = lax.broadcasted_iota(jnp.int32, (2, LANES), 1)
    target = out
    if before is not None:
        out[0] = before[...]
        target = out.at[1]
    made_all = turned_dot(w_two[...].astype(BF16), tap_rows(hidden, 0, ROWS, 3))
    for r in range(ROWS):
        made = made_all[:, r * LANES : (r + 1) * LANES]
        left = jnp.where(lane == 0, 0.0, pltpu.roll(made[0:2], 1, 1))
        right = jnp.where(lane == LANES - 1, 0.0, pltpu.roll(made[4:6], LANES - 1, 1))
        total = left + made[2:4] + right
        target[0, r : r + 1, :] = total[0:1]
        target[1, r : r + 1, :] = total[1:2]


SMEM = pltpu.SMEM
MIB = 1024 * 1024


def call(kernel, args, out_shape, scratch, smem=1, blocks=None, far=(), micros=0, vmem=20):
    specs = []
    for k, arg in enumerate(args):
        if k < smem:
            specs.append(pl.BlockSpec(memory_space=SMEM))
        elif k in far:
            specs.append(pl.BlockSpec(memory_space=pl.ANY))
        elif blocks and k in blocks:
            specs.append(blocks[k])
        else:
            specs.append(pl.BlockSpec(memory_space=pltpu.VMEM))
    return pl.pallas_call(
        kernel,
        out_shape=out_shape,
        grid=(1,) if blocks else (),
        in_specs=specs,
        out_specs=jax.tree.map(lambda o: pl.BlockSpec(memory_space=pltpu.VMEM), out_shape),
        scratch_shapes=scratch,
        compiler_params=pltpu.CompilerParams(vmem_limit_bytes=vmem * MIB),
        cost_estimate=pl.CostEstimate(
            flops=1024, bytes_accessed=1024 + 3_000_000 * micros, transcendentals=0
        ),
    )(*args)


def shards(
    first_frame,
    second_frame,
    context,
    hidden_init,
    flow_rows,
    flow_cols,
    block_ids,
    block_counts,
    w_corr,
    w_corr2,
    w_flow1,
    w_flow2,
    w_motion,
    w_gates,
    w_cand,
    w_head1,
    w_head2,
):
    rows_dev, width, channels = first_frame.shape
    tile_count = lax.axis_size("row")
    tile = lax.axis_index("row")
    core = tile & 1
    even_chip = ((tile >> 1) & 1) ^ 1
    place = jnp.stack([tile, core, even_chip, jnp.int32(tile_count)]).astype(jnp.int32)
    meta = jnp.concatenate([place, block_ids.reshape(-1), block_counts.reshape(-1)])
    SDS = jax.ShapeDtypeStruct
    VM = pltpu.VMEM
    pixels = rows_dev * width

    blocks = second_frame.reshape(pixels, channels)
    flows = [jnp.pad(f.astype(BF16).reshape(-1, width), ((0, 0), (0, channels - width))) for f in (flow_rows, flow_cols)]
    payload = jnp.concatenate([blocks, *flows])
    frame, own_volume, turned, both = call(
        stage_kernel,
        [flow_rows, flow_cols, first_frame.reshape(pixels, channels), blocks, hidden_init, context],
        (
            SDS((pixels, channels), BF16),
            SDS((rows_dev, pixels, LANES), F32),
            SDS((ITERS, rows_dev, width, LANES), jnp.int32),
            SDS((rows_dev, width, 2 * LANES), BF16),
        ),
        [pltpu.SemaphoreType.DMA((2,))],
        smem=0,
        far=(4, 5),
    )
    even, far = swap(payload, chip_even), swap(payload, three_away)
    pair, own_volume, meta = lax.optimization_barrier((payload, own_volume, meta))
    pair = swap(pair, in_chip)
    even, pair, both = lax.optimization_barrier((even, pair, both))
    odd = relay(even)
    both_sides = side_tiles(both)
    around = [even, odd, far, pair, swap(even, in_chip), swap(odd, in_chip)]
    around, both_sides = lax.optimization_barrier((around, both_sides))
    corr = call(
        corr_kernel,
        [meta, frame, own_volume, turned, *around],
        SDS((ITERS, rows_dev, DEPTH, width), BF16),
        [VM((NB * rows_dev, pixels, LANES), F32), VM((width, LANES), F32)],
    )

    second_rows = rows_dev + 2 * SECOND_REACH
    first_rows = rows_dev + 2 * FIRST_REACH
    motion_rows = rows_dev + 2 * MOTION_REACH
    flow_second, flow_given = call(
        flow_kernel,
        [meta, payload, *around, w_flow1, w_flow2.T],
        (
            SDS((ITERS, second_rows, width, LANES), BF16),
            SDS((ITERS, motion_rows, width, LANES), BF16),
        ),
        [
            VM((first_rows, width, LANES), BF16),
            VM((7, 16, 2 * LANES), F32),
            VM((3 * LANES, 3 * LANES), BF16),
            VM((ITERS, NB * rows_dev, 16, width), F32),
        ],
    )

    even, odd, pair = swap(corr, chip_even), swap(corr, chip_odd), swap(corr, in_chip)
    even, odd, flow_second = lax.optimization_barrier((even, odd, flow_second))
    near = (corr, even, odd, pair, swap(even, in_chip), swap(odd, in_chip))

    def motion_of(n):
        def part(shape):
            return pl.BlockSpec((None,) + shape[1:], lambda i: (n, 0, 0, 0))

        tiles = [*near, flow_second, flow_given]
        return call(
            motion_kernel,
            [meta, *tiles, w_corr, w_corr2.T, w_motion],
            SDS((motion_rows, width, LANES), BF16),
            [
                VM((first_rows, width, 2 * LANES), BF16),
                VM((second_rows, width, 2 * LANES), BF16),
                VM((DEPTH, w_corr.shape[1]), BF16),
                VM((3, 2 * LANES, 3 * w_corr.shape[1]), BF16),
                VM((3 * 2 * LANES, 3 * LANES), BF16),
            ],
            blocks={1 + k: part(x.shape) for k, x in enumerate(tiles)},
        )

    def hidden_of(tiles, motion, h=()):
        return call(
            gate_kernel,
            [meta, *tiles, motion, w_gates, w_cand, *h],
            SDS((rows_dev, width, LANES), BF16),
            [
                VM((motion_rows, width, 3 * LANES), BF16),
                VM((rows_dev + 2 * GATE_REACH, width, LANES), BF16),
                VM((rows_dev + 2 * GATE_REACH, width, LANES), F32),
            ],
        )

    def head_of(h, h_sides, before=()):
        shape = (2, rows_dev, width)
        return call(
            head_kernel,
            [meta, h, *h_sides, w_head1, w_head2.T, *before],
            SDS((ITERS,) + shape if before else shape, F32),
            [
                VM((3 * rows_dev, width, LANES), BF16),
                VM((rows_dev + 2, width, 2 * LANES), BF16),
                VM((8, 3 * w_head1.shape[1]), F32),
            ],
        )

    tiles = (both, *both_sides)
    h_one = hidden_of(tiles, motion_of(0))
    one_tiles = (h_one, *side_tiles(h_one))
    h_two = hidden_of(tiles, motion_of(1), one_tiles)
    delta_one = head_of(h_one, one_tiles[1:])
    deltas = head_of(h_two, side_tiles(h_two), (delta_one,))
    return (h_two, deltas)


def solution(mesh):
    tiled = P(("group", "row"), None, None)
    listed = P(None, ("group", "row"), None)
    placed = (tiled,) * 4 + (listed,) * 3 + (P(None, ("group", "row")),) + (P(),) * 9
    return jax.shard_map(
        shards,
        mesh=mesh,
        in_specs=placed,
        out_specs=(tiled, P(None, None, ("group", "row"), None)),
        check_vma=False,
    )
```

```python
import math

import jax
import jax.numpy as jnp
import numpy as np
from jax import lax
from jax.experimental import pallas as pl
from jax.experimental.pallas import tpu as pltpu
from jax.sharding import PartitionSpec as P

RAD = 4
ITERS = 2
REACH = 3
NB = 7
SIDE = 9
TAPS = 81
LANES = 128
FY_MAX = 8
CHUNK = 16
DEPTH = 96
FLOW_SCALE = 0.125
F32 = jnp.float32
BF16 = jnp.bfloat16

ROWS = 4
MOTION_REACH = 4
SECOND_REACH = MOTION_REACH + 1
FIRST_REACH = MOTION_REACH + 2
GATE_REACH = 2


def swap(block, partner):
    devices = lax.axis_size("row")
    route = []
    for i in range(devices):
        j = partner(i)
        route.append((i, j if 0 <= j < devices else i))
    return lax.ppermute(block, "row", route)


def in_chip(i):
    return i ^ 1


def next_row(i):
    return ((i + 1) ^ 1) - 1


def chip_even(i):
    return i ^ 2


def chip_odd(i):
    return ((i + 2) ^ 2) - 2


def three_away(i):
    return i - 3 if i % 2 == 0 else i + 3


def relay(block):
    devices = lax.axis_size("row")
    chips, route = devices // 2, []
    for i in range(devices):
        chip = i // 2
        goal = chip + 2 if chip % 2 == 0 else chip - 2
        if not 0 <= goal < chips:
            goal = chip ^ 1
        route.append((i, 2 * goal + i % 2))
    return lax.ppermute(block, "row", route)


def side_tiles(block):
    return swap(block, next_row), swap(block, in_chip)


def pick(flag, yes, no):
    return jnp.where(flag, yes, no)


def shift_cols(values, shift):
    size = values.shape[0]
    column = lax.broadcasted_iota(jnp.int32, values.shape, 0) & (LANES - 1)
    edge = 0 if shift == 1 else LANES - 1
    return jnp.where(column == edge, 0.0, pltpu.roll(values, shift % size, 0))


def tap_rows(ref, row, rows, taps, lanes=None):
    parts = []
    for u in range(taps):
        piece = ref[pl.ds(row + u, rows)] if lanes is None else ref[pl.ds(row + u, rows), :, lanes]
        parts.append(piece.reshape(rows * LANES, piece.shape[-1]))
    return jnp.concatenate(parts, axis=-1)


def by_row(values, start, meta, apply):
    first = meta[0] * ROWS + start
    height = meta[3] * ROWS
    done = []
    for r in range(values.shape[0] // LANES):
        inside = (first + r >= 0) & (first + r < height)
        done.append(jnp.where(inside, apply(values[r * LANES : (r + 1) * LANES]), 0.0))
    return jnp.concatenate(done, axis=0)


def turned_dot(left, right):
    return lax.dot_general(left, right, (((1,), (1,)), ((), ())), preferred_element_type=F32)


def relu(x):
    return jnp.maximum(x, 0.0)


def choose(planes, index):
    bit = 1
    while len(planes) > 1:
        on = (index & bit) != 0
        pairs = [
            jnp.where(on, planes[k + 1], planes[k]) if k + 1 < len(planes) else planes[k]
            for k in range(0, len(planes), 2)
        ]
        planes, bit = pairs, 2 * bit
    return planes[0]


PART = LANES // 8


def volume_of(frame, block, spot, half):
    pieces = []
    for r in (2 * half, 2 * half + 1):
        for m in range(8):
            start = r * LANES + ((m - r - 4 * spot) & 7) * PART
            start = start if isinstance(start, int) else pl.multiple_of(start, PART)
            pieces.append(block[pl.ds(start, PART), :])
    return turned_dot(frame, jnp.concatenate(pieces, axis=0))


def stage_kernel(meta, rows, cols, ids, counts, first, own, frame, own_volume, turned, windows):
    frame[...] = first[...]
    shape = windows.shape[1:]
    for n in range(ITERS):
        bits = jnp.zeros(shape, jnp.int32)
        count = jnp.broadcast_to(counts[n : n + 1, :], shape)
        for k in range(ids.shape[2]):
            spot = jnp.broadcast_to(ids[n, :, k : k + 1], shape) - meta[0] + REACH
            listed = (k < count) & (spot >= 0) & (spot < NB)
            bits = bits | jnp.where(listed, 1 << jnp.clip(spot, 0, NB - 1), 0)
        windows[n] = bits
    for half in range(2):
        made = volume_of(frame[...], own, REACH, half)
        own_volume[2 * half] = made[:, :LANES]
        own_volume[2 * half + 1] = made[:, LANES:]
    for n in range(ITERS):
        for i in range(ROWS):
            packed = (rows[n, i : i + 1, :] + FY_MAX) * 64 + cols[n, i : i + 1, :] + 32
            turned[n, i] = jnp.broadcast_to(packed, (LANES, LANES)).T


def multiply(blocks, meta, frame, volume):
    core, even_chip = meta[1], meta[2]
    plus = pick(core == 0, 1, -1)
    two = pick(even_chip == 1, 2, -2)
    spots = {
        "pair": REACH + plus,
        "far": REACH - 3 * plus,
        "even": REACH + two,
        "odd": REACH - two,
        "pair_even": REACH + plus + two,
        "pair_odd": REACH + plus - two,
    }
    for name, block in blocks.items():
        spot = spots[name]
        for half in range(2):
            product = volume_of(frame[...], block, spot, half)
            volume[spot * ROWS + 2 * half] = product[:, :LANES]
            volume[spot * ROWS + 2 * half + 1] = product[:, LANES:]


def early_kernel(meta, frame, even, far, pair, pair_even, volume):
    multiply(dict(even=even, far=far, pair=pair, pair_even=pair_even), meta, frame, volume)


def corr_kernel(meta, frame, own_volume, turned, windows, odd, pair_odd, early_volume, out, volume, picked):
    multiply(dict(odd=odd, pair_odd=pair_odd), meta, frame, volume)

    def plane(b, at):
        own = b - REACH * ROWS
        return own_volume[own, at, :] if 0 <= own < ROWS else volume[b, at, :]

    scale = 1.0 / math.sqrt(frame.shape[-1])
    chunk = CHUNK
    lane = lax.broadcasted_iota(jnp.int32, (chunk, LANES), 1)
    sub = lax.broadcasted_iota(jnp.int32, (chunk, LANES), 0)
    lane_dy = (lane * 57) >> 9
    lane_dx = lane - lane_dy * SIDE - RAD
    for n in range(ITERS):
        bits = windows[n]
        for i in range(ROWS):

            def step(index, carry, n=n, bits=bits, i=i):
                j0 = pl.multiple_of(index * chunk, chunk)
                packed = turned[n, i, pl.ds(j0, chunk), :]
                lift = packed >> 6
                start = sub + (j0 - 32) + (packed & 63)
                at = pl.ds(pl.multiple_of(i * LANES + j0, chunk), chunk)
                planes = [plane(i + k, at) for k in range(2 * FY_MAX + SIDE)]
                group = ((lane - start + RAD) & (LANES - 1)) >> 4
                most = choose(planes[:24], lift + ((group - lift - i) & 7))
                last = choose(planes[8:], lift)
                column = start + lane_dx
                row = lift + i + lane_dy
                wrapped = (column + (row & 7) * PART) & (LANES - 1)
                value = jnp.where(
                    lane_dy == 8,
                    jnp.take_along_axis(last, wrapped, axis=1, mode="promise_in_bounds"),
                    jnp.take_along_axis(most, wrapped, axis=1, mode="promise_in_bounds"),
                )
                seen = ((bits >> (row >> 2)) & 1) == 1
                seen = seen & (column >= 0) & (column < LANES) & (lane < TAPS)
                picked[pl.ds(j0, chunk), :] = jnp.where(seen, value * scale, 0.0)
                return carry

            lax.fori_loop(0, LANES // chunk, step, 0, unroll=8)
            out[n, i] = picked[...].T[:DEPTH].astype(BF16)


def flow_kernel(
    meta, own, even, odd, far, pair, pair_even, pair_odd, w_flow1, w_flow2, second, given, first, w_one, w_two, windows
):
    made, wide = w_flow2.shape[0], first.shape[2]
    w_two[...] = jnp.zeros(w_two.shape, BF16)
    for u in range(3):
        for s in range(3):
            low = (s + 1) * LANES - made
            tap = slice((u * 3 + s) * wide, (u * 3 + s + 1) * wide)
            w_two[low : low + made, u * wide : (u + 1) * wide] = w_flow2[:, tap]
    weights = w_flow1[...].astype(F32)
    w_one[...] = jnp.zeros(w_one.shape, F32)
    for u in range(7):
        w_one[u, 0:14, :LANES] = weights[u * 14 : (u + 1) * 14, :]
    tap = lax.broadcasted_iota(jnp.int32, (16, LANES), 0)
    lane = lax.broadcasted_iota(jnp.int32, (16, LANES), 1)
    w_one[3, :, LANES:] = jnp.where((tap - 6 == lane - (LANES - 2)) & (lane >= LANES - 2), 1.0, 0.0)
    w_all = w_one[...].reshape(7 * 16, 2 * LANES).astype(BF16)

    tile, core, even_chip, tiles = meta[0], meta[1], meta[2], meta[3]
    plus = pick(core == 0, 1, -1)
    two = pick(even_chip == 1, 2, -2)
    spots = (
        (own, 0),
        (pair, plus),
        (far, -3 * plus),
        (even, two),
        (odd, -two),
        (pair_even, plus + two),
        (pair_odd, plus - two),
    )
    windows[:, :, 14:, :] = jnp.zeros(windows.shape[:2] + (2, LANES), F32)
    column = lax.broadcasted_iota(jnp.int32, (4 * ROWS, LANES), 1)
    for block, spot in spots:
        inside = (tile + spot >= 0) & (tile + spot < tiles)
        lines = jnp.where(inside, block[ROWS * LANES :, :LANES].astype(F32) * FLOW_SCALE, 0.0)
        for s in range(7):
            reach = s - 3
            moved = pltpu.roll(lines, (-reach) % LANES, 1) if reach else lines
            seen = (column + reach >= 0) & (column + reach < LANES)
            moved = jnp.where(seen, moved, 0.0)
            for c in range(2):
                for n in range(ITERS):
                    for r in range(ROWS):
                        k = (c * ITERS + n) * ROWS + r
                        windows[n, (spot + REACH) * ROWS + r, 2 * s + c : 2 * s + c + 1, :] = moved[k : k + 1, :]

    top = 3 * ROWS - FIRST_REACH - 3
    first_rows = ROWS + 2 * FIRST_REACH
    second_rows = ROWS + 2 * SECOND_REACH
    offset = FIRST_REACH - MOTION_REACH
    for n in range(ITERS):
        for r in range(first_rows):
            window = windows[n, top + r : top + r + 7].reshape(7 * 16, LANES).astype(BF16)
            made = lax.dot_general(window, w_all, (((0,), (0,)), ((), ())), preferred_element_type=F32)
            value = by_row(made[:, :LANES], r - FIRST_REACH, meta, relu)
            first[r] = value.astype(BF16)
            if offset <= r < first_rows - offset:
                given[n, r - offset] = made[:, LANES:].astype(BF16)
        step = 2
        for r in range(0, second_rows, step):
            made = turned_dot(tap_rows(first, r, step, 3), w_two[...])
            total = (
                made[:, LANES : 2 * LANES]
                + shift_cols(made[:, :LANES], 1)
                + shift_cols(made[:, 2 * LANES :], -1)
            )
            total = by_row(total, r - SECOND_REACH, meta, relu).astype(BF16)
            second[n, r : r + step] = total.reshape(step, LANES, LANES)


def motion_kernel(
    meta, own, even, odd, pair, pair_even, pair_odd, second, given, w_corr, w_corr2, w_motion, out, one, two, w_one, w_two, w_three
):
    core, even_chip = meta[1], meta[2]
    is_even, is_zero = even_chip == 1, core == 0

    w_one[...] = jnp.zeros(w_one.shape, BF16)
    w_one[: w_corr.shape[0], :] = w_corr[...]
    w_three[...] = jnp.zeros(w_three.shape, BF16)
    wide, made_two, made_three = w_one.shape[1], w_corr2.shape[0], w_motion.shape[1]
    w_two[:, made_two:, :] = jnp.zeros((3, w_two.shape[1] - made_two, w_two.shape[2]), BF16)
    for u in range(3):
        for s in range(3):
            tap = slice((u * 3 + s) * wide, (u * 3 + s + 1) * wide)
            w_two[s, :made_two, u * wide : (u + 1) * wide] = w_corr2[:, tap]
            w_three[u * wide : (u + 1) * wide, s * LANES : s * LANES + made_three] = w_motion[tap, :]

    def corr_row(row):
        tile, r = (row + 2 * ROWS) // ROWS - 2, row % ROWS
        if tile == 0:
            return own[r]
        if tile == -2:
            return pick(is_even, odd[r], even[r])
        if tile == 2:
            return pick(is_even, even[r], odd[r])
        if tile == -1:
            return pick(is_zero, pick(is_even, pair_odd[r], pair_even[r]), pair[r])
        return pick(is_zero, pair[r], pick(is_even, pair_even[r], pair_odd[r]))

    for r in range(ROWS + 2 * FIRST_REACH):
        made = lax.dot_general(
            corr_row(r - FIRST_REACH), w_one[...], (((0,), (0,)), ((), ())), preferred_element_type=F32
        )
        one[r] = by_row(made, r - FIRST_REACH, meta, relu).astype(BF16)

    step = 2
    zeros = jnp.zeros((step * LANES, LANES), BF16)

    def second_step(index, carry):
        r = index * step
        left = tap_rows(one, r, step, 3)
        made = [turned_dot(left, w_two[s]) for s in range(3)]
        total = made[1] + shift_cols(made[0], 1) + shift_cols(made[2], -1)
        total = by_row(total, r - SECOND_REACH, meta, relu).astype(BF16)
        flow = second[pl.ds(r, step)].reshape(step * LANES, LANES)
        total = total + jnp.concatenate([zeros, flow], axis=-1)
        two[pl.ds(r, step)] = total.reshape(step, LANES, 2 * LANES)
        return carry

    lax.fori_loop(0, (ROWS + 2 * SECOND_REACH) // step, second_step, 0, unroll=7)

    step3 = 2

    def third_step(index, carry):
        r = index * step3
        made = jnp.dot(tap_rows(two, r, step3, 3), w_three[...], preferred_element_type=F32)
        total = (
            made[:, LANES : 2 * LANES]
            + shift_cols(made[:, :LANES], 1)
            + shift_cols(made[:, 2 * LANES :], -1)
        )
        total = by_row(total, r - MOTION_REACH, meta, relu).astype(BF16)
        total = total + given[pl.ds(r, step3)].reshape(step3 * LANES, LANES)
        out[pl.ds(r, step3)] = total.reshape(step3, LANES, LANES)
        return carry

    lax.fori_loop(0, (ROWS + 2 * MOTION_REACH) // step3, third_step, 0, unroll=6)


def spread(scratch, meta, own, across, pair):
    tile, core, tiles = meta[0], meta[1], meta[3]
    is_zero = core == 0
    nothing = jnp.zeros((), BF16)
    reach = (scratch.shape[0] - ROWS) // 2
    for r in range(reach):
        up = r if across.shape[0] == reach else ROWS - reach + r
        above = pick(is_zero, across[up], pair[up])
        below = pick(is_zero, pair[r], across[r])
        scratch[r] = jnp.where(tile > 0, above, nothing)
        scratch[reach + ROWS + r] = jnp.where(tile < tiles - 1, below, nothing)
    scratch[reach : reach + ROWS] = own[...]


def part_of(weight, low, high):
    deep = weight.shape[0] // 5
    return jnp.concatenate([weight[u * deep + low : u * deep + high, :] for u in range(5)], axis=0)


def product(left, right):
    return jnp.dot(left, right, preferred_element_type=F32)


def sigmoid(x):
    return 0.5 * jnp.tanh(0.5 * x) + 0.5


GATE_ROWS = ROWS + 2 * GATE_REACH
STEP = 4


def context_kernel(
    meta, h_own, h_across, h_pair, c_own, c_across, c_pair, w_gates, w_cand, hidden, gates_one, gates_two, cand, context
):
    spread(hidden, meta, h_own, h_across, h_pair)
    spread(context, meta, c_own, c_across, c_pair)
    for r in range(0, GATE_ROWS, STEP):
        left = tap_rows(context, r, STEP, 5)
        made = product(left, part_of(w_gates, LANES, 2 * LANES))
        gates_two[r : r + STEP] = made.reshape(STEP, LANES, 2 * LANES)
        made = made + product(tap_rows(hidden, r, STEP, 5), part_of(w_gates, 0, LANES))
        gates_one[r : r + STEP] = made.reshape(STEP, LANES, 2 * LANES)
    made = product(tap_rows(context, GATE_REACH, ROWS, 5), part_of(w_cand, LANES, 2 * LANES))
    cand[...] = made.reshape(ROWS, LANES, LANES)


def gate_kernel(meta, gates_made, cand_made, motion, w_gates, w_cand, *rest):
    if len(rest) == 4:
        around, out, state, keep = rest
    else:
        h_own, h_across, h_pair, out, edge_across, edge_pair, state, keep, around = rest
        spread(around, meta, h_own, h_across, h_pair)
    for r in range(0, GATE_ROWS, STEP):
        gates = gates_made[r : r + STEP].reshape(STEP * LANES, 2 * LANES)
        gates = gates + product(tap_rows(motion, r, STEP, 5), part_of(w_gates, 2 * LANES, 3 * LANES))
        if len(rest) != 4:
            gates = gates + product(tap_rows(around, r, STEP, 5), part_of(w_gates, 0, LANES))
        hidden = around[r + 2 : r + 2 + STEP].reshape(STEP * LANES, LANES).astype(F32)
        reset = (sigmoid(gates[:, LANES:]) * hidden).astype(BF16)
        state[r : r + STEP] = reset.reshape(STEP, LANES, LANES)
        keep[r : r + STEP] = gates[:, :LANES].reshape(STEP, LANES, LANES)
    made = cand_made[...].reshape(ROWS * LANES, LANES)
    made = made + product(tap_rows(motion, GATE_REACH, ROWS, 5), part_of(w_cand, 2 * LANES, 3 * LANES))
    made = made + product(tap_rows(state, 0, ROWS, 5), part_of(w_cand, 0, LANES))
    update = sigmoid(keep[2 : 2 + ROWS].reshape(ROWS * LANES, LANES))
    hidden = around[ROWS : 2 * ROWS].reshape(ROWS * LANES, LANES).astype(F32)
    new = (1.0 - update) * hidden + update * jnp.tanh(made)
    new = new.astype(BF16).reshape(ROWS, LANES, LANES)
    out[...] = new
    if len(rest) != 4:
        is_zero = meta[1] == 0
        edge_across[...] = pick(is_zero, new[:2], new[2:])
        edge_pair[...] = pick(is_zero, new[2:], new[:2])


def head_kernel(meta, h_own, h_across, h_pair, w_head1, w_head2, *rest):
    before, out, joined, hidden, w_two = rest if len(rest) == 5 else (None,) + rest
    spread(joined, meta, h_own, h_across, h_pair)
    deep, wide = h_own.shape[2], w_head1.shape[1]
    w_two[...] = jnp.zeros(w_two.shape, F32)
    for s in range(3):
        for u in range(3):
            k = u * 3 + s
            w_two[2 * s : 2 * s + 2, u * wide : (u + 1) * wide] = w_head2[:, k * wide : (k + 1) * wide].astype(F32)
    step = 2
    for r in range(0, ROWS + 2, step):
        left = tap_rows(joined, r, step, 3)
        made = []
        for s in range(3):
            taps = [w_head1[(u * 3 + s) * deep : (u * 3 + s + 1) * deep, :] for u in range(3)]
            made.append(product(left, jnp.concatenate(taps, axis=0)))
        total = made[1] + shift_cols(made[0], 1) + shift_cols(made[2], -1)
        total = by_row(total, r - 1, meta, relu).astype(BF16)
        hidden[r : r + step] = total.reshape(step, LANES, 2 * LANES)
    lane = lax.broadcasted_iota(jnp.int32, (2, LANES), 1)
    target = out
    if before is not None:
        out[0] = before[...]
        target = out.at[1]
    made_all = turned_dot(w_two[...].astype(BF16), tap_rows(hidden, 0, ROWS, 3))
    for r in range(ROWS):
        made = made_all[:, r * LANES : (r + 1) * LANES]
        left = jnp.where(lane == 0, 0.0, pltpu.roll(made[0:2], 1, 1))
        right = jnp.where(lane == LANES - 1, 0.0, pltpu.roll(made[4:6], LANES - 1, 1))
        total = left + made[2:4] + right
        target[0, r : r + 1, :] = total[0:1]
        target[1, r : r + 1, :] = total[1:2]


SMEM = pltpu.SMEM
MIB = 1024 * 1024


def call(kernel, args, out_shape, scratch, smem=1, blocks=None, far=(), micros=0, vmem=20, aliases={}):
    specs = []
    for k, arg in enumerate(args):
        if k < smem:
            specs.append(pl.BlockSpec(memory_space=SMEM))
        elif k in far:
            specs.append(pl.BlockSpec(memory_space=pl.ANY))
        elif blocks and k in blocks:
            specs.append(blocks[k])
        else:
            specs.append(pl.BlockSpec(memory_space=pltpu.VMEM))
    return pl.pallas_call(
        kernel,
        out_shape=out_shape,
        grid=(1,) if blocks else (),
        in_specs=specs,
        out_specs=jax.tree.map(lambda o: pl.BlockSpec(memory_space=pltpu.VMEM), out_shape),
        scratch_shapes=scratch,
        input_output_aliases=aliases,
        compiler_params=pltpu.CompilerParams(vmem_limit_bytes=vmem * MIB),
        cost_estimate=pl.CostEstimate(
            flops=1024, bytes_accessed=1024 + 3_000_000 * micros, transcendentals=0
        ),
    )(*args)


def shards(
    first_frame,
    second_frame,
    context,
    hidden_init,
    flow_rows,
    flow_cols,
    block_ids,
    block_counts,
    w_corr,
    w_corr2,
    w_flow1,
    w_flow2,
    w_motion,
    w_gates,
    w_cand,
    w_head1,
    w_head2,
):
    rows_dev, width, channels = first_frame.shape
    tile_count = lax.axis_size("row")
    tile = lax.axis_index("row")
    core = tile & 1
    even_chip = ((tile >> 1) & 1) ^ 1
    meta = jnp.stack([tile, core, even_chip, jnp.int32(tile_count)]).astype(jnp.int32)
    SDS = jax.ShapeDtypeStruct
    VM = pltpu.VMEM
    pixels = rows_dev * width

    blocks = second_frame.reshape(pixels, channels)
    flows = [jnp.pad(f.astype(BF16).reshape(-1, width), ((0, 0), (0, channels - width))) for f in (flow_rows, flow_cols)]
    payload = jnp.concatenate([blocks, *flows])
    even, far, pair = swap(payload, chip_even), swap(payload, three_away), swap(payload, in_chip)
    pair, rows = lax.optimization_barrier((pair, flow_rows))
    frame, own_volume, turned, windows = call(
        stage_kernel,
        [meta, rows, flow_cols, block_ids, block_counts, first_frame.reshape(pixels, channels), blocks],
        (
            SDS((pixels, channels), BF16),
            SDS((rows_dev, pixels, LANES), F32),
            SDS((ITERS, rows_dev, width, LANES), jnp.int32),
            SDS((ITERS, CHUNK, LANES), jnp.int32),
        ),
        [],
    )
    even, far, hidden, close, frame, own_volume, turned, windows = lax.optimization_barrier(
        (even, far, hidden_init, context, frame, own_volume, turned, windows)
    )
    odd = relay(even)
    hidden_sides, context_sides = side_tiles(hidden), side_tiles(close)
    odd, hidden_sides, context_sides = lax.optimization_barrier((odd, hidden_sides, context_sides))
    pair_even, pair_odd = swap(even, in_chip), swap(odd, in_chip)
    around = [even, odd, far, pair, pair_even, pair_odd]
    shape = SDS((NB * rows_dev, pixels, LANES), F32)
    volume = call(early_kernel, [meta, frame, even, far, pair, pair_even], shape, [])
    corr = call(
        corr_kernel,
        [meta, frame, own_volume, turned, windows, odd, pair_odd, volume],
        (SDS((ITERS, rows_dev, DEPTH, width), BF16), shape),
        [VM((width, LANES), F32)],
        aliases={7: 1},
    )[0]

    second_rows = rows_dev + 2 * SECOND_REACH
    first_rows = rows_dev + 2 * FIRST_REACH
    motion_rows = rows_dev + 2 * MOTION_REACH
    flow_second, flow_given = call(
        flow_kernel,
        [meta, payload, *around, w_flow1, w_flow2.T],
        (
            SDS((ITERS, second_rows, width, LANES), BF16),
            SDS((ITERS, motion_rows, width, LANES), BF16),
        ),
        [
            VM((first_rows, width, LANES), BF16),
            VM((7, 16, 2 * LANES), F32),
            VM((3 * LANES, 3 * LANES), BF16),
            VM((ITERS, NB * rows_dev, 16, width), F32),
        ],
    )

    even, odd, pair = swap(corr, chip_even), swap(corr, chip_odd), swap(corr, in_chip)
    h_around, gates_one, gates_two, cand = call(
        context_kernel,
        [meta, hidden, *hidden_sides, close, *context_sides, w_gates, w_cand],
        (
            SDS((motion_rows, width, LANES), BF16),
            SDS((GATE_ROWS, width, 2 * LANES), F32),
            SDS((GATE_ROWS, width, 2 * LANES), F32),
            SDS((rows_dev, width, LANES), F32),
        ),
        [VM((motion_rows, width, LANES), BF16)],
    )
    even, odd, flow_second, cand = lax.optimization_barrier((even, odd, flow_second, cand))
    near = (corr, even, odd, pair, swap(even, in_chip), swap(odd, in_chip))

    def motion_of(n):
        def part(shape):
            return pl.BlockSpec((None,) + shape[1:], lambda i: (n, 0, 0, 0))

        tiles = [*near, flow_second, flow_given]
        return call(
            motion_kernel,
            [meta, *tiles, w_corr, w_corr2.T, w_motion],
            SDS((motion_rows, width, LANES), BF16),
            [
                VM((first_rows, width, 2 * LANES), BF16),
                VM((second_rows, width, 2 * LANES), BF16),
                VM((DEPTH, w_corr.shape[1]), BF16),
                VM((3, 2 * LANES, 3 * w_corr.shape[1]), BF16),
                VM((3 * 2 * LANES, 3 * LANES), BF16),
            ],
            blocks={1 + k: part(x.shape) for k, x in enumerate(tiles)},
        )

    def head_of(h, h_sides, before=()):
        shape = (2, rows_dev, width)
        return call(
            head_kernel,
            [meta, h, *h_sides, w_head1, w_head2.T, *before],
            SDS((ITERS,) + shape if before else shape, F32),
            [
                VM((rows_dev + 4, width, LANES), BF16),
                VM((rows_dev + 2, width, 2 * LANES), BF16),
                VM((8, 3 * w_head1.shape[1]), F32),
            ],
        )

    tile_of = SDS((rows_dev, width, LANES), BF16)
    edge_of = SDS((2, width, LANES), BF16)
    states = [VM((GATE_ROWS, width, LANES), BF16), VM((GATE_ROWS, width, LANES), F32)]
    h_one = call(
        gate_kernel,
        [meta, gates_one, cand, motion_of(0), w_gates, w_cand, h_around],
        tile_of,
        states,
    )
    one_tiles = (h_one, *side_tiles(h_one))
    h_two, edge_across, edge_pair = call(
        gate_kernel,
        [meta, gates_two, cand, motion_of(1), w_gates, w_cand, *one_tiles],
        (tile_of, edge_of, edge_of),
        states + [VM((motion_rows, width, LANES), BF16)],
    )
    edges = (swap(edge_across, next_row), swap(edge_pair, in_chip))
    delta_one = head_of(h_one, one_tiles[1:])
    deltas = head_of(h_two, edges, (delta_one,))
    return (h_two, deltas)


def solution(mesh):
    tiled = P(("group", "row"), None, None)
    listed = P(None, ("group", "row"), None)
    placed = (tiled,) * 4 + (listed,) * 3 + (P(None, ("group", "row")),) + (P(),) * 9
    return jax.shard_map(
        shards,
        mesh=mesh,
        in_specs=placed,
        out_specs=(tiled, P(None, None, ("group", "row"), None)),
        check_vma=False,
    )
```

```python
import math

import jax
import jax.numpy as jnp
import numpy as np
from jax import lax
from jax.experimental import pallas as pl
from jax.experimental.pallas import tpu as pltpu
from jax.sharding import PartitionSpec as P

RAD = 4
ITERS = 2
REACH = 3
NB = 7
SIDE = 9
TAPS = 81
LANES = 128
FY_MAX = 8
CHUNK = 16
DEPTH = 96
FLOW_SCALE = 0.125
F32 = jnp.float32
BF16 = jnp.bfloat16

ROWS = 4
MOTION_REACH = 4
SECOND_REACH = MOTION_REACH + 1
FIRST_REACH = MOTION_REACH + 2
GATE_REACH = 2


def swap(block, partner):
    devices = lax.axis_size("row")
    route = []
    for i in range(devices):
        j = partner(i)
        route.append((i, j if 0 <= j < devices else i))
    return lax.ppermute(block, "row", route)


def in_chip(i):
    return i ^ 1


def next_row(i):
    return ((i + 1) ^ 1) - 1


def chip_even(i):
    return i ^ 2


def chip_odd(i):
    return ((i + 2) ^ 2) - 2


def three_away(i):
    return i - 3 if i % 2 == 0 else i + 3


def relay(block):
    devices = lax.axis_size("row")
    chips, route = devices // 2, []
    for i in range(devices):
        chip = i // 2
        goal = chip + 2 if chip % 2 == 0 else chip - 2
        if not 0 <= goal < chips:
            goal = chip ^ 1
        route.append((i, 2 * goal + i % 2))
    return lax.ppermute(block, "row", route)


def side_tiles(block):
    return swap(block, next_row), swap(block, in_chip)


def pick(flag, yes, no):
    return jnp.where(flag, yes, no)


def shift_cols(values, shift):
    size = values.shape[0]
    column = lax.broadcasted_iota(jnp.int32, values.shape, 0) & (LANES - 1)
    edge = 0 if shift == 1 else LANES - 1
    return jnp.where(column == edge, 0.0, pltpu.roll(values, shift % size, 0))


def tap_rows(ref, row, rows, taps, lanes=None):
    parts = []
    for u in range(taps):
        piece = ref[pl.ds(row + u, rows)] if lanes is None else ref[pl.ds(row + u, rows), :, lanes]
        parts.append(piece.reshape(rows * LANES, piece.shape[-1]))
    return jnp.concatenate(parts, axis=-1)


def by_row(values, start, meta, apply):
    first = meta[0] * ROWS + start
    height = meta[3] * ROWS
    done = []
    for r in range(values.shape[0] // LANES):
        inside = (first + r >= 0) & (first + r < height)
        done.append(jnp.where(inside, apply(values[r * LANES : (r + 1) * LANES]), 0.0))
    return jnp.concatenate(done, axis=0)


def turned_dot(left, right):
    return lax.dot_general(left, right, (((1,), (1,)), ((), ())), preferred_element_type=F32)


def relu(x):
    return jnp.maximum(x, 0.0)


def choose(planes, index):
    bit = 1
    while len(planes) > 1:
        on = (index & bit) != 0
        pairs = [
            jnp.where(on, planes[k + 1], planes[k]) if k + 1 < len(planes) else planes[k]
            for k in range(0, len(planes), 2)
        ]
        planes, bit = pairs, 2 * bit
    return planes[0]


PART = LANES // 8


def volume_of(frame, block, spot, half):
    pieces = []
    for r in (2 * half, 2 * half + 1):
        for m in range(8):
            start = r * LANES + ((m - r - 4 * spot) & 7) * PART
            start = start if isinstance(start, int) else pl.multiple_of(start, PART)
            pieces.append(block[pl.ds(start, PART), :])
    return turned_dot(frame, jnp.concatenate(pieces, axis=0))


def stage_kernel(
    meta, ids, counts, flow_rows, flow_cols, first, second, frame, own_volume, turned, windows, rows, cols, own, sems
):
    moves = ((flow_rows, rows), (flow_cols, cols), (first, frame), (second, own))
    copies = [pltpu.make_async_copy(a, b, sems.at[k]) for k, (a, b) in enumerate(moves)]
    for copy in copies:
        copy.start()
    shape = windows.shape[1:]
    for n in range(ITERS):
        bits = jnp.zeros(shape, jnp.int32)
        count = jnp.broadcast_to(counts[:, n : n + 1], shape)
        for k in range(ids.shape[2]):
            spot = jnp.broadcast_to(ids[n, :, k : k + 1], shape) - meta[0] + REACH
            listed = (k < count) & (spot >= 0) & (spot < NB)
            bits = bits | jnp.where(listed, 1 << jnp.clip(spot, 0, NB - 1), 0)
        windows[n] = bits
    copies[0].wait()
    copies[1].wait()
    for n in range(ITERS):
        for i in range(ROWS):
            packed = (rows[n, i : i + 1, :] + FY_MAX) * 64 + cols[n, i : i + 1, :] + 32
            turned[n, i] = jnp.broadcast_to(packed, (LANES, LANES)).T
    copies[2].wait()
    copies[3].wait()
    for half in range(2):
        made = volume_of(frame[...], own, REACH, half)
        own_volume[2 * half] = made[:, :LANES]
        own_volume[2 * half + 1] = made[:, LANES:]


def multiply(blocks, meta, frame, volume):
    core, even_chip = meta[1], meta[2]
    plus = pick(core == 0, 1, -1)
    two = pick(even_chip == 1, 2, -2)
    spots = {
        "pair": REACH + plus,
        "far": REACH - 3 * plus,
        "even": REACH + two,
        "odd": REACH - two,
        "pair_even": REACH + plus + two,
        "pair_odd": REACH + plus - two,
    }
    for name, block in blocks.items():
        spot = spots[name]
        for half in range(2):
            product = volume_of(frame[...], block, spot, half)
            volume[spot * ROWS + 2 * half] = product[:, :LANES]
            volume[spot * ROWS + 2 * half + 1] = product[:, LANES:]


def early_kernel(meta, frame, even, far, pair, pair_even, volume):
    multiply(dict(even=even, far=far, pair=pair, pair_even=pair_even), meta, frame, volume)


def corr_kernel(meta, frame, own_volume, turned, windows, odd, pair_odd, early_volume, out, volume, picked):
    multiply(dict(odd=odd, pair_odd=pair_odd), meta, frame, volume)

    def plane(b, at):
        own = b - REACH * ROWS
        return own_volume[own, at, :] if 0 <= own < ROWS else volume[b, at, :]

    scale = 1.0 / math.sqrt(frame.shape[-1])
    chunk = CHUNK
    lane = lax.broadcasted_iota(jnp.int32, (chunk, LANES), 1)
    sub = lax.broadcasted_iota(jnp.int32, (chunk, LANES), 0)
    lane_dy = (lane * 57) >> 9
    lane_dx = lane - lane_dy * SIDE - RAD
    for n in range(ITERS):
        bits = windows[n]
        for i in range(ROWS):

            def step(index, carry, n=n, bits=bits, i=i):
                j0 = pl.multiple_of(index * chunk, chunk)
                packed = turned[n, i, pl.ds(j0, chunk), :]
                lift = packed >> 6
                start = sub + (j0 - 32) + (packed & 63)
                at = pl.ds(pl.multiple_of(i * LANES + j0, chunk), chunk)
                planes = [plane(i + k, at) for k in range(2 * FY_MAX + SIDE)]
                group = ((lane - start + RAD) & (LANES - 1)) >> 4
                most = choose(planes[:24], lift + ((group - lift - i) & 7))
                last = choose(planes[8:], lift)
                column = start + lane_dx
                row = lift + i + lane_dy
                wrapped = (column + (row & 7) * PART) & (LANES - 1)
                value = jnp.where(
                    lane_dy == 8,
                    jnp.take_along_axis(last, wrapped, axis=1, mode="promise_in_bounds"),
                    jnp.take_along_axis(most, wrapped, axis=1, mode="promise_in_bounds"),
                )
                seen = ((bits >> (row >> 2)) & 1) == 1
                seen = seen & (column >= 0) & (column < LANES) & (lane < TAPS)
                picked[pl.ds(j0, chunk), :] = jnp.where(seen, value * scale, 0.0)
                return carry

            lax.fori_loop(0, LANES // chunk, step, 0, unroll=8)
            out[n, i] = picked[...].T[:DEPTH].astype(BF16)


def flow_kernel(
    meta, own, even, odd, far, pair, pair_even, pair_odd, w_flow1, w_flow2, second, given, first, w_one, w_two, windows
):
    made, wide = w_flow2.shape[0], first.shape[2]
    w_two[...] = jnp.zeros(w_two.shape, BF16)
    for u in range(3):
        for s in range(3):
            low = (s + 1) * LANES - made
            tap = slice((u * 3 + s) * wide, (u * 3 + s + 1) * wide)
            w_two[low : low + made, u * wide : (u + 1) * wide] = w_flow2[:, tap]
    weights = w_flow1[...].astype(F32)
    w_one[...] = jnp.zeros(w_one.shape, F32)
    for u in range(7):
        w_one[u, 0:14, :LANES] = weights[u * 14 : (u + 1) * 14, :]
    tap = lax.broadcasted_iota(jnp.int32, (16, LANES), 0)
    lane = lax.broadcasted_iota(jnp.int32, (16, LANES), 1)
    w_one[3, :, LANES:] = jnp.where((tap - 6 == lane - (LANES - 2)) & (lane >= LANES - 2), 1.0, 0.0)
    w_all = w_one[...].reshape(7 * 16, 2 * LANES).astype(BF16)

    tile, core, even_chip, tiles = meta[0], meta[1], meta[2], meta[3]
    plus = pick(core == 0, 1, -1)
    two = pick(even_chip == 1, 2, -2)
    spots = (
        (own, 0),
        (pair, plus),
        (far, -3 * plus),
        (even, two),
        (odd, -two),
        (pair_even, plus + two),
        (pair_odd, plus - two),
    )
    windows[:, :, 14:, :] = jnp.zeros(windows.shape[:2] + (2, LANES), F32)
    column = lax.broadcasted_iota(jnp.int32, (4 * ROWS, LANES), 1)
    for block, spot in spots:
        inside = (tile + spot >= 0) & (tile + spot < tiles)
        lines = jnp.where(inside, block[ROWS * LANES :, :LANES].astype(F32) * FLOW_SCALE, 0.0)
        for s in range(7):
            reach = s - 3
            moved = pltpu.roll(lines, (-reach) % LANES, 1) if reach else lines
            seen = (column + reach >= 0) & (column + reach < LANES)
            moved = jnp.where(seen, moved, 0.0)
            for c in range(2):
                for n in range(ITERS):
                    for r in range(ROWS):
                        k = (c * ITERS + n) * ROWS + r
                        windows[n, (spot + REACH) * ROWS + r, 2 * s + c : 2 * s + c + 1, :] = moved[k : k + 1, :]

    top = 3 * ROWS - FIRST_REACH - 3
    first_rows = ROWS + 2 * FIRST_REACH
    second_rows = ROWS + 2 * SECOND_REACH
    offset = FIRST_REACH - MOTION_REACH
    for n in range(ITERS):
        for r in range(first_rows):
            window = windows[n, top + r : top + r + 7].reshape(7 * 16, LANES).astype(BF16)
            made = lax.dot_general(window, w_all, (((0,), (0,)), ((), ())), preferred_element_type=F32)
            value = by_row(made[:, :LANES], r - FIRST_REACH, meta, relu)
            first[r] = value.astype(BF16)
            if offset <= r < first_rows - offset:
                given[n, r - offset] = made[:, LANES:].astype(BF16)
        step = 2
        for r in range(0, second_rows, step):
            made = turned_dot(tap_rows(first, r, step, 3), w_two[...])
            total = (
                made[:, LANES : 2 * LANES]
                + shift_cols(made[:, :LANES], 1)
                + shift_cols(made[:, 2 * LANES :], -1)
            )
            total = by_row(total, r - SECOND_REACH, meta, relu).astype(BF16)
            second[n, r : r + step] = total.reshape(step, LANES, LANES)


def motion_kernel(
    meta, own, even, odd, pair, pair_even, pair_odd, second, given, w_corr, w_corr2, w_motion, out, one, two, w_one, w_two, w_three
):
    core, even_chip = meta[1], meta[2]
    is_even, is_zero = even_chip == 1, core == 0

    w_one[...] = jnp.zeros(w_one.shape, BF16)
    w_one[: w_corr.shape[0], :] = w_corr[...]
    w_three[...] = jnp.zeros(w_three.shape, BF16)
    wide, made_two, made_three = w_one.shape[1], w_corr2.shape[0], w_motion.shape[1]
    w_two[:, made_two:, :] = jnp.zeros((3, w_two.shape[1] - made_two, w_two.shape[2]), BF16)
    for u in range(3):
        for s in range(3):
            tap = slice((u * 3 + s) * wide, (u * 3 + s + 1) * wide)
            w_two[s, :made_two, u * wide : (u + 1) * wide] = w_corr2[:, tap]
            w_three[u * wide : (u + 1) * wide, s * LANES : s * LANES + made_three] = w_motion[tap, :]

    def corr_row(row):
        tile, r = (row + 2 * ROWS) // ROWS - 2, row % ROWS
        if tile == 0:
            return own[r]
        if tile == -2:
            return pick(is_even, odd[r], even[r])
        if tile == 2:
            return pick(is_even, even[r], odd[r])
        if tile == -1:
            return pick(is_zero, pick(is_even, pair_odd[r], pair_even[r]), pair[r])
        return pick(is_zero, pair[r], pick(is_even, pair_even[r], pair_odd[r]))

    for r in range(ROWS + 2 * FIRST_REACH):
        made = lax.dot_general(
            corr_row(r - FIRST_REACH), w_one[...], (((0,), (0,)), ((), ())), preferred_element_type=F32
        )
        one[r] = by_row(made, r - FIRST_REACH, meta, relu).astype(BF16)

    step = 2
    zeros = jnp.zeros((step * LANES, LANES), BF16)

    def second_step(index, carry):
        r = index * step
        left = tap_rows(one, r, step, 3)
        made = [turned_dot(left, w_two[s]) for s in range(3)]
        total = made[1] + shift_cols(made[0], 1) + shift_cols(made[2], -1)
        total = by_row(total, r - SECOND_REACH, meta, relu).astype(BF16)
        flow = second[pl.ds(r, step)].reshape(step * LANES, LANES)
        total = total + jnp.concatenate([zeros, flow], axis=-1)
        two[pl.ds(r, step)] = total.reshape(step, LANES, 2 * LANES)
        return carry

    lax.fori_loop(0, (ROWS + 2 * SECOND_REACH) // step, second_step, 0, unroll=7)

    step3 = 2

    def third_step(index, carry):
        r = index * step3
        made = jnp.dot(tap_rows(two, r, step3, 3), w_three[...], preferred_element_type=F32)
        total = (
            made[:, LANES : 2 * LANES]
            + shift_cols(made[:, :LANES], 1)
            + shift_cols(made[:, 2 * LANES :], -1)
        )
        total = by_row(total, r - MOTION_REACH, meta, relu).astype(BF16)
        total = total + given[pl.ds(r, step3)].reshape(step3 * LANES, LANES)
        out[pl.ds(r, step3)] = total.reshape(step3, LANES, LANES)
        return carry

    lax.fori_loop(0, (ROWS + 2 * MOTION_REACH) // step3, third_step, 0, unroll=6)


def spread(scratch, meta, own, across, pair):
    tile, core, tiles = meta[0], meta[1], meta[3]
    is_zero = core == 0
    nothing = jnp.zeros((), BF16)
    reach = (scratch.shape[0] - ROWS) // 2
    for r in range(reach):
        up = r if across.shape[0] == reach else ROWS - reach + r
        above = pick(is_zero, across[up], pair[up])
        below = pick(is_zero, pair[r], across[r])
        scratch[r] = jnp.where(tile > 0, above, nothing)
        scratch[reach + ROWS + r] = jnp.where(tile < tiles - 1, below, nothing)
    scratch[reach : reach + ROWS] = own[...]


def part_of(weight, low, high):
    deep = weight.shape[0] // 5
    return jnp.concatenate([weight[u * deep + low : u * deep + high, :] for u in range(5)], axis=0)


def product(left, right):
    return jnp.dot(left, right, preferred_element_type=F32)


def sigmoid(x):
    return 0.5 * jnp.tanh(0.5 * x) + 0.5


GATE_ROWS = ROWS + 2 * GATE_REACH
STEP = 4


def context_kernel(meta, both, across, pair, w_gates, w_cand, hidden, gates_one, gates_two, cand, joined):
    spread(joined, meta, both, across, pair)
    hidden[...] = joined[:, :, :LANES]
    near = slice(LANES, 2 * LANES)
    for r in range(0, GATE_ROWS, STEP):
        made = product(tap_rows(joined, r, STEP, 5, near), part_of(w_gates, LANES, 2 * LANES))
        gates_two[r : r + STEP] = made.reshape(STEP, LANES, 2 * LANES)
        made = made + product(tap_rows(hidden, r, STEP, 5), part_of(w_gates, 0, LANES))
        gates_one[r : r + STEP] = made.reshape(STEP, LANES, 2 * LANES)
    made = product(tap_rows(joined, GATE_REACH, ROWS, 5, near), part_of(w_cand, LANES, 2 * LANES))
    cand[...] = made.reshape(ROWS, LANES, LANES)


def gate_kernel(meta, gates_made, cand_made, motion, w_gates, w_cand, *rest):
    if len(rest) == 4:
        around, out, state, keep = rest
    else:
        h_own, h_across, h_pair, out, again, edge_across, edge_pair, state, keep, around = rest
        spread(around, meta, h_own, h_across, h_pair)
    for r in range(0, GATE_ROWS, STEP):
        gates = gates_made[r : r + STEP].reshape(STEP * LANES, 2 * LANES)
        gates = gates + product(tap_rows(motion, r, STEP, 5), part_of(w_gates, 2 * LANES, 3 * LANES))
        if len(rest) != 4:
            gates = gates + product(tap_rows(around, r, STEP, 5), part_of(w_gates, 0, LANES))
        hidden = around[r + 2 : r + 2 + STEP].reshape(STEP * LANES, LANES).astype(F32)
        reset = (sigmoid(gates[:, LANES:]) * hidden).astype(BF16)
        state[r : r + STEP] = reset.reshape(STEP, LANES, LANES)
        keep[r : r + STEP] = gates[:, :LANES].reshape(STEP, LANES, LANES)
    made = cand_made[...].reshape(ROWS * LANES, LANES)
    made = made + product(tap_rows(motion, GATE_REACH, ROWS, 5), part_of(w_cand, 2 * LANES, 3 * LANES))
    made = made + product(tap_rows(state, 0, ROWS, 5), part_of(w_cand, 0, LANES))
    update = sigmoid(keep[2 : 2 + ROWS].reshape(ROWS * LANES, LANES))
    hidden = around[ROWS : 2 * ROWS].reshape(ROWS * LANES, LANES).astype(F32)
    new = (1.0 - update) * hidden + update * jnp.tanh(made)
    new = new.astype(BF16).reshape(ROWS, LANES, LANES)
    out[...] = new
    if len(rest) != 4:
        again[...] = new
        is_zero = meta[1] == 0
        edge_across[...] = pick(is_zero, new[:2], new[2:])
        edge_pair[...] = pick(is_zero, new[2:], new[:2])


def head_kernel(meta, h_own, h_across, h_pair, w_head1, w_head2, *rest):
    before, out, joined, hidden, w_two = rest if len(rest) == 5 else (None,) + rest
    spread(joined, meta, h_own, h_across, h_pair)
    deep, wide = h_own.shape[2], w_head1.shape[1]
    w_two[...] = jnp.zeros(w_two.shape, F32)
    for s in range(3):
        for u in range(3):
            k = u * 3 + s
            w_two[2 * s : 2 * s + 2, u * wide : (u + 1) * wide] = w_head2[:, k * wide : (k + 1) * wide].astype(F32)
    step = 2
    for r in range(0, ROWS + 2, step):
        left = tap_rows(joined, r, step, 3)
        made = []
        for s in range(3):
            taps = [w_head1[(u * 3 + s) * deep : (u * 3 + s + 1) * deep, :] for u in range(3)]
            made.append(product(left, jnp.concatenate(taps, axis=0)))
        total = made[1] + shift_cols(made[0], 1) + shift_cols(made[2], -1)
        total = by_row(total, r - 1, meta, relu).astype(BF16)
        hidden[r : r + step] = total.reshape(step, LANES, 2 * LANES)
    lane = lax.broadcasted_iota(jnp.int32, (2, LANES), 1)
    target = out
    if before is not None:
        out[0] = before[...]
        target = out.at[1]
    made_all = turned_dot(w_two[...].astype(BF16), tap_rows(hidden, 0, ROWS, 3))
    for r in range(ROWS):
        made = made_all[:, r * LANES : (r + 1) * LANES]
        left = jnp.where(lane == 0, 0.0, pltpu.roll(made[0:2], 1, 1))
        right = jnp.where(lane == LANES - 1, 0.0, pltpu.roll(made[4:6], LANES - 1, 1))
        total = left + made[2:4] + right
        target[0, r : r + 1, :] = total[0:1]
        target[1, r : r + 1, :] = total[1:2]


SMEM = pltpu.SMEM
MIB = 1024 * 1024


def call(kernel, args, out_shape, scratch, smem=1, blocks=None, far=(), micros=0, vmem=20, aliases={}):
    specs = []
    for k, arg in enumerate(args):
        if k < smem:
            specs.append(pl.BlockSpec(memory_space=SMEM))
        elif k in far:
            specs.append(pl.BlockSpec(memory_space=pltpu.HBM))
        elif blocks and k in blocks:
            specs.append(blocks[k])
        else:
            specs.append(pl.BlockSpec(memory_space=pltpu.VMEM))
    return pl.pallas_call(
        kernel,
        out_shape=out_shape,
        grid=(1,) if blocks else (),
        in_specs=specs,
        out_specs=jax.tree.map(lambda o: pl.BlockSpec(memory_space=pltpu.VMEM), out_shape),
        scratch_shapes=scratch,
        input_output_aliases=aliases,
        compiler_params=pltpu.CompilerParams(vmem_limit_bytes=vmem * MIB),
        cost_estimate=pl.CostEstimate(
            flops=1024, bytes_accessed=1024 + 3_000_000 * micros, transcendentals=0
        ),
    )(*args)


def shards(
    first_frame,
    second_frame,
    context,
    hidden_init,
    flow_rows,
    flow_cols,
    block_ids,
    block_counts,
    w_corr,
    w_corr2,
    w_flow1,
    w_flow2,
    w_motion,
    w_gates,
    w_cand,
    w_head1,
    w_head2,
):
    rows_dev, width, channels = first_frame.shape
    tile_count = lax.axis_size("row")
    tile = lax.axis_index("row")
    core = tile & 1
    even_chip = ((tile >> 1) & 1) ^ 1
    meta = jnp.stack([tile, core, even_chip, jnp.int32(tile_count)]).astype(jnp.int32)
    SDS = jax.ShapeDtypeStruct
    VM = pltpu.VMEM
    pixels = rows_dev * width

    blocks = second_frame.reshape(pixels, channels)
    flows = jnp.concatenate([flow_rows, flow_cols]).astype(BF16).reshape(-1, width)
    payload = jnp.concatenate([blocks, jnp.pad(flows, ((0, 0), (0, channels - width)))])
    even, far, pair = swap(payload, chip_even), swap(payload, three_away), swap(payload, in_chip)
    pair, counts, hidden, close = lax.optimization_barrier((pair, block_counts.T, hidden_init, context))
    both = jnp.concatenate([hidden, close], axis=-1)
    frame, own_volume, turned, windows = call(
        stage_kernel,
        [meta, block_ids, counts, flow_rows, flow_cols, first_frame.reshape(pixels, channels), blocks],
        (
            SDS((pixels, channels), BF16),
            SDS((rows_dev, pixels, LANES), F32),
            SDS((ITERS, rows_dev, width, LANES), jnp.int32),
            SDS((ITERS, CHUNK, LANES), jnp.int32),
        ),
        [
            VM(flow_rows.shape, jnp.int32),
            VM(flow_cols.shape, jnp.int32),
            VM((pixels, channels), BF16),
            pltpu.SemaphoreType.DMA((4,)),
        ],
        far=(3, 4, 5, 6),
    )
    even, both = lax.optimization_barrier((even, both))
    odd = relay(even)
    both_sides = side_tiles(both)
    odd, far, both_sides, frame, own_volume, turned, windows = lax.optimization_barrier(
        (odd, far, both_sides, frame, own_volume, turned, windows)
    )
    pair_even, pair_odd = swap(even, in_chip), swap(odd, in_chip)
    around = [even, odd, far, pair, pair_even, pair_odd]
    shape = SDS((NB * rows_dev, pixels, LANES), F32)
    volume = call(early_kernel, [meta, frame, even, far, pair, pair_even], shape, [])
    corr = call(
        corr_kernel,
        [meta, frame, own_volume, turned, windows, odd, pair_odd, volume],
        (SDS((ITERS, rows_dev, DEPTH, width), BF16), shape),
        [VM((width, LANES), F32)],
        aliases={7: 1},
    )[0]

    second_rows = rows_dev + 2 * SECOND_REACH
    first_rows = rows_dev + 2 * FIRST_REACH
    motion_rows = rows_dev + 2 * MOTION_REACH
    flow_second, flow_given = call(
        flow_kernel,
        [meta, payload, *around, w_flow1, w_flow2.T],
        (
            SDS((ITERS, second_rows, width, LANES), BF16),
            SDS((ITERS, motion_rows, width, LANES), BF16),
        ),
        [
            VM((first_rows, width, LANES), BF16),
            VM((7, 16, 2 * LANES), F32),
            VM((3 * LANES, 3 * LANES), BF16),
            VM((ITERS, NB * rows_dev, 16, width), F32),
        ],
    )

    even, odd, pair = swap(corr, chip_even), swap(corr, chip_odd), swap(corr, in_chip)
    h_around, gates_one, gates_two, cand = call(
        context_kernel,
        [meta, both, *both_sides, w_gates, w_cand],
        (
            SDS((motion_rows, width, LANES), BF16),
            SDS((GATE_ROWS, width, 2 * LANES), F32),
            SDS((GATE_ROWS, width, 2 * LANES), F32),
            SDS((rows_dev, width, LANES), F32),
        ),
        [VM((motion_rows, width, 2 * LANES), BF16)],
    )
    even, odd, flow_second, cand = lax.optimization_barrier((even, odd, flow_second, cand))
    near = (corr, even, odd, pair, swap(even, in_chip), swap(odd, in_chip))

    def motion_of(n):
        def part(shape):
            return pl.BlockSpec((None,) + shape[1:], lambda i: (n, 0, 0, 0))

        tiles = [*near, flow_second, flow_given]
        return call(
            motion_kernel,
            [meta, *tiles, w_corr, w_corr2.T, w_motion],
            SDS((motion_rows, width, LANES), BF16),
            [
                VM((first_rows, width, 2 * LANES), BF16),
                VM((second_rows, width, 2 * LANES), BF16),
                VM((DEPTH, w_corr.shape[1]), BF16),
                VM((3, 2 * LANES, 3 * w_corr.shape[1]), BF16),
                VM((3 * 2 * LANES, 3 * LANES), BF16),
            ],
            blocks={1 + k: part(x.shape) for k, x in enumerate(tiles)},
        )

    def head_of(h, h_sides, before=()):
        shape = (2, rows_dev, width)
        return call(
            head_kernel,
            [meta, h, *h_sides, w_head1, w_head2.T, *before],
            SDS((ITERS,) + shape if before else shape, F32),
            [
                VM((rows_dev + 4, width, LANES), BF16),
                VM((rows_dev + 2, width, 2 * LANES), BF16),
                VM((8, 3 * w_head1.shape[1]), F32),
            ],
        )

    tile_of = SDS((rows_dev, width, LANES), BF16)
    edge_of = SDS((2, width, LANES), BF16)
    states = [VM((GATE_ROWS, width, LANES), BF16), VM((GATE_ROWS, width, LANES), F32)]
    h_one = call(
        gate_kernel,
        [meta, gates_one, cand, motion_of(0), w_gates, w_cand, h_around],
        tile_of,
        states,
    )
    one_tiles = (h_one, *side_tiles(h_one))
    h_two, h_again, edge_across, edge_pair = call(
        gate_kernel,
        [meta, gates_two, cand, motion_of(1), w_gates, w_cand, *one_tiles],
        (tile_of, tile_of, edge_of, edge_of),
        states + [VM((motion_rows, width, LANES), BF16)],
    )
    edges = (swap(edge_across, next_row), swap(edge_pair, in_chip))
    delta_one = head_of(h_one, one_tiles[1:])
    deltas = head_of(h_again, edges, (delta_one,))
    return (h_two, deltas)


def solution(mesh):
    tiled = P(("group", "row"), None, None)
    listed = P(None, ("group", "row"), None)
    placed = (tiled,) * 4 + (listed,) * 3 + (P(None, ("group", "row")),) + (P(),) * 9
    return jax.shard_map(
        shards,
        mesh=mesh,
        in_specs=placed,
        out_specs=(tiled, P(None, None, ("group", "row"), None)),
        check_vma=False,
    )
```

```python
import math

import jax
import jax.numpy as jnp
import numpy as np
from jax import lax
from jax.experimental import pallas as pl
from jax.experimental.pallas import tpu as pltpu
from jax.sharding import PartitionSpec as P

RAD = 4
ITERS = 2
REACH = 3
NB = 7
SIDE = 9
TAPS = 81
LANES = 128
FY_MAX = 8
CHUNK = 16
DEPTH = 96
FLOW_SCALE = 0.125
F32 = jnp.float32
BF16 = jnp.bfloat16

ROWS = 4
MOTION_REACH = 4
SECOND_REACH = MOTION_REACH + 1
FIRST_REACH = MOTION_REACH + 2
GATE_REACH = 2


def swap(block, partner):
    devices = lax.axis_size("row")
    route = []
    for i in range(devices):
        j = partner(i)
        route.append((i, j if 0 <= j < devices else i))
    return lax.ppermute(block, "row", route)


def in_chip(i):
    return i ^ 1


def next_row(i):
    return ((i + 1) ^ 1) - 1


def chip_even(i):
    return i ^ 2


def chip_odd(i):
    return ((i + 2) ^ 2) - 2


def three_away(i):
    return i - 3 if i % 2 == 0 else i + 3


def relay(block):
    devices = lax.axis_size("row")
    chips, route = devices // 2, []
    for i in range(devices):
        chip = i // 2
        goal = chip + 2 if chip % 2 == 0 else chip - 2
        if not 0 <= goal < chips:
            goal = chip ^ 1
        route.append((i, 2 * goal + i % 2))
    return lax.ppermute(block, "row", route)


def side_tiles(block):
    return swap(block, next_row), swap(block, in_chip)


def pick(flag, yes, no):
    return jnp.where(flag, yes, no)


def shift_cols(values, shift):
    size = values.shape[0]
    column = lax.broadcasted_iota(jnp.int32, values.shape, 0) & (LANES - 1)
    edge = 0 if shift == 1 else LANES - 1
    return jnp.where(column == edge, 0.0, pltpu.roll(values, shift % size, 0))


def tap_rows(ref, row, rows, taps, lanes=None):
    parts = []
    for u in range(taps):
        piece = ref[pl.ds(row + u, rows)] if lanes is None else ref[pl.ds(row + u, rows), :, lanes]
        parts.append(piece.reshape(rows * LANES, piece.shape[-1]))
    return jnp.concatenate(parts, axis=-1)


def by_row(values, start, meta, apply):
    first = meta[0] * ROWS + start
    height = meta[3] * ROWS
    done = []
    for r in range(values.shape[0] // LANES):
        inside = (first + r >= 0) & (first + r < height)
        done.append(jnp.where(inside, apply(values[r * LANES : (r + 1) * LANES]), 0.0))
    return jnp.concatenate(done, axis=0)


def turned_dot(left, right):
    return lax.dot_general(left, right, (((1,), (1,)), ((), ())), preferred_element_type=F32)


def relu(x):
    return jnp.maximum(x, 0.0)


def choose(planes, index):
    bit = 1
    while len(planes) > 1:
        on = (index & bit) != 0
        pairs = [
            jnp.where(on, planes[k + 1], planes[k]) if k + 1 < len(planes) else planes[k]
            for k in range(0, len(planes), 2)
        ]
        planes, bit = pairs, 2 * bit
    return planes[0]


PART = LANES // 8


def volume_of(frame, block, spot, half):
    pieces = []
    for r in (2 * half, 2 * half + 1):
        for m in range(8):
            start = r * LANES + ((m - r - 4 * spot) & 7) * PART
            start = start if isinstance(start, int) else pl.multiple_of(start, PART)
            pieces.append(block[pl.ds(start, PART), :])
    return turned_dot(frame, jnp.concatenate(pieces, axis=0))


def own_kernel(first, own, frame, own_volume):
    frame[...] = first[...]
    for half in range(2):
        made = volume_of(frame[...], own, REACH, half)
        own_volume[2 * half] = made[:, :LANES]
        own_volume[2 * half + 1] = made[:, LANES:]


def stage_kernel(meta, ids, counts, rows, cols, turned, windows):
    shape = windows.shape[1:]
    for n in range(ITERS):
        bits = jnp.zeros(shape, jnp.int32)
        count = jnp.broadcast_to(counts[:, n : n + 1], shape)
        for k in range(ids.shape[2]):
            spot = jnp.broadcast_to(ids[n, :, k : k + 1], shape) - meta[0] + REACH
            listed = (k < count) & (spot >= 0) & (spot < NB)
            bits = bits | jnp.where(listed, 1 << jnp.clip(spot, 0, NB - 1), 0)
        windows[n] = bits
    for n in range(ITERS):
        for i in range(ROWS):
            packed = (rows[n, i : i + 1, :] + FY_MAX) * 64 + cols[n, i : i + 1, :] + 32
            turned[n, i] = jnp.broadcast_to(packed, (LANES, LANES)).T


def multiply(blocks, meta, frame, volume):
    core, even_chip = meta[1], meta[2]
    plus = pick(core == 0, 1, -1)
    two = pick(even_chip == 1, 2, -2)
    spots = {
        "pair": REACH + plus,
        "far": REACH - 3 * plus,
        "even": REACH + two,
        "odd": REACH - two,
        "pair_even": REACH + plus + two,
        "pair_odd": REACH + plus - two,
    }
    for name, block in blocks.items():
        spot = spots[name]
        for half in range(2):
            product = volume_of(frame[...], block, spot, half)
            volume[spot * ROWS + 2 * half] = product[:, :LANES]
            volume[spot * ROWS + 2 * half + 1] = product[:, LANES:]


def early_kernel(meta, frame, even, far, pair, pair_even, volume):
    multiply(dict(even=even, far=far, pair=pair, pair_even=pair_even), meta, frame, volume)


def corr_kernel(meta, frame, own_volume, turned, windows, odd, pair_odd, early_volume, out, volume, picked):
    multiply(dict(odd=odd, pair_odd=pair_odd), meta, frame, volume)

    def plane(b, at):
        own = b - REACH * ROWS
        return own_volume[own, at, :] if 0 <= own < ROWS else volume[b, at, :]

    scale = 1.0 / math.sqrt(frame.shape[-1])
    chunk = CHUNK
    lane = lax.broadcasted_iota(jnp.int32, (chunk, LANES), 1)
    sub = lax.broadcasted_iota(jnp.int32, (chunk, LANES), 0)
    lane_dy = (lane * 57) >> 9
    lane_dx = lane - lane_dy * SIDE - RAD
    for n in range(ITERS):
        bits = windows[n]
        for i in range(ROWS):

            def step(index, carry, n=n, bits=bits, i=i):
                j0 = pl.multiple_of(index * chunk, chunk)
                packed = turned[n, i, pl.ds(j0, chunk), :]
                lift = packed >> 6
                start = sub + (j0 - 32) + (packed & 63)
                at = pl.ds(pl.multiple_of(i * LANES + j0, chunk), chunk)
                planes = [plane(i + k, at) for k in range(2 * FY_MAX + SIDE)]
                group = ((lane - start + RAD) & (LANES - 1)) >> 4
                most = choose(planes[:24], lift + ((group - lift - i) & 7))
                last = choose(planes[8:], lift)
                column = start + lane_dx
                row = lift + i + lane_dy
                wrapped = (column + (row & 7) * PART) & (LANES - 1)
                value = jnp.where(
                    lane_dy == 8,
                    jnp.take_along_axis(last, wrapped, axis=1, mode="promise_in_bounds"),
                    jnp.take_along_axis(most, wrapped, axis=1, mode="promise_in_bounds"),
                )
                seen = ((bits >> (row >> 2)) & 1) == 1
                seen = seen & (column >= 0) & (column < LANES) & (lane < TAPS)
                picked[pl.ds(j0, chunk), :] = jnp.where(seen, value * scale, 0.0)
                return carry

            lax.fori_loop(0, LANES // chunk, step, 0, unroll=8)
            out[n, i] = picked[...].T[:DEPTH].astype(BF16)


def flow_kernel(
    meta, own, even, odd, far, pair, pair_even, pair_odd, w_flow1, w_flow2, second, given, first, w_one, w_two, windows
):
    made, wide = w_flow2.shape[0], first.shape[2]
    w_two[...] = jnp.zeros(w_two.shape, BF16)
    for u in range(3):
        for s in range(3):
            low = (s + 1) * LANES - made
            tap = slice((u * 3 + s) * wide, (u * 3 + s + 1) * wide)
            w_two[low : low + made, u * wide : (u + 1) * wide] = w_flow2[:, tap]
    weights = w_flow1[...].astype(F32)
    w_one[...] = jnp.zeros(w_one.shape, F32)
    for u in range(7):
        w_one[u, 0:14, :LANES] = weights[u * 14 : (u + 1) * 14, :]
    tap = lax.broadcasted_iota(jnp.int32, (16, LANES), 0)
    lane = lax.broadcasted_iota(jnp.int32, (16, LANES), 1)
    w_one[3, :, LANES:] = jnp.where((tap - 6 == lane - (LANES - 2)) & (lane >= LANES - 2), 1.0, 0.0)
    w_all = w_one[...].reshape(7 * 16, 2 * LANES).astype(BF16)

    tile, core, even_chip, tiles = meta[0], meta[1], meta[2], meta[3]
    plus = pick(core == 0, 1, -1)
    two = pick(even_chip == 1, 2, -2)
    spots = (
        (own, 0),
        (pair, plus),
        (far, -3 * plus),
        (even, two),
        (odd, -two),
        (pair_even, plus + two),
        (pair_odd, plus - two),
    )
    windows[:, :, 14:, :] = jnp.zeros(windows.shape[:2] + (2, LANES), F32)
    column = lax.broadcasted_iota(jnp.int32, (4 * ROWS, LANES), 1)
    for block, spot in spots:
        inside = (tile + spot >= 0) & (tile + spot < tiles)
        lines = jnp.where(inside, block[ROWS * LANES :, :LANES].astype(F32) * FLOW_SCALE, 0.0)
        for s in range(7):
            reach = s - 3
            moved = pltpu.roll(lines, (-reach) % LANES, 1) if reach else lines
            seen = (column + reach >= 0) & (column + reach < LANES)
            moved = jnp.where(seen, moved, 0.0)
            for c in range(2):
                for n in range(ITERS):
                    for r in range(ROWS):
                        k = (c * ITERS + n) * ROWS + r
                        windows[n, (spot + REACH) * ROWS + r, 2 * s + c : 2 * s + c + 1, :] = moved[k : k + 1, :]

    top = 3 * ROWS - FIRST_REACH - 3
    first_rows = ROWS + 2 * FIRST_REACH
    second_rows = ROWS + 2 * SECOND_REACH
    offset = FIRST_REACH - MOTION_REACH
    for n in range(ITERS):
        for r in range(first_rows):
            window = windows[n, top + r : top + r + 7].reshape(7 * 16, LANES).astype(BF16)
            made = lax.dot_general(window, w_all, (((0,), (0,)), ((), ())), preferred_element_type=F32)
            value = by_row(made[:, :LANES], r - FIRST_REACH, meta, relu)
            first[r] = value.astype(BF16)
            if offset <= r < first_rows - offset:
                given[n, r - offset] = made[:, LANES:].astype(BF16)
        step = 2
        for r in range(0, second_rows, step):
            made = turned_dot(tap_rows(first, r, step, 3), w_two[...])
            total = (
                made[:, LANES : 2 * LANES]
                + shift_cols(made[:, :LANES], 1)
                + shift_cols(made[:, 2 * LANES :], -1)
            )
            total = by_row(total, r - SECOND_REACH, meta, relu).astype(BF16)
            second[n, r : r + step] = total.reshape(step, LANES, LANES)


def motion_kernel(
    meta, own, even, odd, pair, pair_even, pair_odd, second, given, w_corr, w_corr2, w_motion, out, one, two, w_one, w_two, w_three
):
    core, even_chip = meta[1], meta[2]
    is_even, is_zero = even_chip == 1, core == 0

    w_one[...] = jnp.zeros(w_one.shape, BF16)
    w_one[: w_corr.shape[0], :] = w_corr[...]
    w_three[...] = jnp.zeros(w_three.shape, BF16)
    wide, made_two, made_three = w_one.shape[1], w_corr2.shape[0], w_motion.shape[1]
    w_two[:, made_two:, :] = jnp.zeros((3, w_two.shape[1] - made_two, w_two.shape[2]), BF16)
    for u in range(3):
        for s in range(3):
            tap = slice((u * 3 + s) * wide, (u * 3 + s + 1) * wide)
            w_two[s, :made_two, u * wide : (u + 1) * wide] = w_corr2[:, tap]
            w_three[u * wide : (u + 1) * wide, s * LANES : s * LANES + made_three] = w_motion[tap, :]

    def corr_row(row):
        tile, r = (row + 2 * ROWS) // ROWS - 2, row % ROWS
        if tile == 0:
            return own[r]
        if tile == -2:
            return pick(is_even, odd[r], even[r])
        if tile == 2:
            return pick(is_even, even[r], odd[r])
        if tile == -1:
            return pick(is_zero, pick(is_even, pair_odd[r], pair_even[r]), pair[r])
        return pick(is_zero, pair[r], pick(is_even, pair_even[r], pair_odd[r]))

    for r in range(ROWS + 2 * FIRST_REACH):
        made = lax.dot_general(
            corr_row(r - FIRST_REACH), w_one[...], (((0,), (0,)), ((), ())), preferred_element_type=F32
        )
        one[r] = by_row(made, r - FIRST_REACH, meta, relu).astype(BF16)

    step = 2
    zeros = jnp.zeros((step * LANES, LANES), BF16)

    def second_step(index, carry):
        r = index * step
        left = tap_rows(one, r, step, 3)
        made = [turned_dot(left, w_two[s]) for s in range(3)]
        total = made[1] + shift_cols(made[0], 1) + shift_cols(made[2], -1)
        total = by_row(total, r - SECOND_REACH, meta, relu).astype(BF16)
        flow = second[pl.ds(r, step)].reshape(step * LANES, LANES)
        total = total + jnp.concatenate([zeros, flow], axis=-1)
        two[pl.ds(r, step)] = total.reshape(step, LANES, 2 * LANES)
        return carry

    lax.fori_loop(0, (ROWS + 2 * SECOND_REACH) // step, second_step, 0, unroll=7)

    step3 = 2

    def third_step(index, carry):
        r = index * step3
        made = jnp.dot(tap_rows(two, r, step3, 3), w_three[...], preferred_element_type=F32)
        total = (
            made[:, LANES : 2 * LANES]
            + shift_cols(made[:, :LANES], 1)
            + shift_cols(made[:, 2 * LANES :], -1)
        )
        total = by_row(total, r - MOTION_REACH, meta, relu).astype(BF16)
        total = total + given[pl.ds(r, step3)].reshape(step3 * LANES, LANES)
        out[pl.ds(r, step3)] = total.reshape(step3, LANES, LANES)
        return carry

    lax.fori_loop(0, (ROWS + 2 * MOTION_REACH) // step3, third_step, 0, unroll=6)


def spread(scratch, meta, own, across, pair):
    tile, core, tiles = meta[0], meta[1], meta[3]
    is_zero = core == 0
    nothing = jnp.zeros((), BF16)
    reach = (scratch.shape[0] - ROWS) // 2
    for r in range(reach):
        up = r if across.shape[0] == reach else ROWS - reach + r
        above = pick(is_zero, across[up], pair[up])
        below = pick(is_zero, pair[r], across[r])
        scratch[r] = jnp.where(tile > 0, above, nothing)
        scratch[reach + ROWS + r] = jnp.where(tile < tiles - 1, below, nothing)
    scratch[reach : reach + ROWS] = own[...]


def part_of(weight, low, high):
    deep = weight.shape[0] // 5
    return jnp.concatenate([weight[u * deep + low : u * deep + high, :] for u in range(5)], axis=0)


def product(left, right):
    return jnp.dot(left, right, preferred_element_type=F32)


def sigmoid(x):
    return 0.5 * jnp.tanh(0.5 * x) + 0.5


GATE_ROWS = ROWS + 2 * GATE_REACH
STEP = 4


def context_kernel(meta, both, across, pair, w_gates, w_cand, hidden, gates_one, gates_two, cand, joined):
    spread(joined, meta, both, across, pair)
    hidden[...] = joined[:, :, :LANES]
    near = slice(LANES, 2 * LANES)
    for r in range(0, GATE_ROWS, STEP):
        made = product(tap_rows(joined, r, STEP, 5, near), part_of(w_gates, LANES, 2 * LANES))
        gates_two[r : r + STEP] = made.reshape(STEP, LANES, 2 * LANES)
        made = made + product(tap_rows(hidden, r, STEP, 5), part_of(w_gates, 0, LANES))
        gates_one[r : r + STEP] = made.reshape(STEP, LANES, 2 * LANES)
    made = product(tap_rows(joined, GATE_REACH, ROWS, 5, near), part_of(w_cand, LANES, 2 * LANES))
    cand[...] = made.reshape(ROWS, LANES, LANES)


def gate_kernel(meta, gates_made, cand_made, motion, w_gates, w_cand, *rest):
    if len(rest) == 4:
        around, out, state, keep = rest
    else:
        h_own, h_across, h_pair, out, again, edge_across, edge_pair, state, keep, around = rest
        spread(around, meta, h_own, h_across, h_pair)
    for r in range(0, GATE_ROWS, STEP):
        gates = gates_made[r : r + STEP].reshape(STEP * LANES, 2 * LANES)
        gates = gates + product(tap_rows(motion, r, STEP, 5), part_of(w_gates, 2 * LANES, 3 * LANES))
        if len(rest) != 4:
            gates = gates + product(tap_rows(around, r, STEP, 5), part_of(w_gates, 0, LANES))
        hidden = around[r + 2 : r + 2 + STEP].reshape(STEP * LANES, LANES).astype(F32)
        reset = (sigmoid(gates[:, LANES:]) * hidden).astype(BF16)
        state[r : r + STEP] = reset.reshape(STEP, LANES, LANES)
        keep[r : r + STEP] = gates[:, :LANES].reshape(STEP, LANES, LANES)
    made = cand_made[...].reshape(ROWS * LANES, LANES)
    made = made + product(tap_rows(motion, GATE_REACH, ROWS, 5), part_of(w_cand, 2 * LANES, 3 * LANES))
    made = made + product(tap_rows(state, 0, ROWS, 5), part_of(w_cand, 0, LANES))
    update = sigmoid(keep[2 : 2 + ROWS].reshape(ROWS * LANES, LANES))
    hidden = around[ROWS : 2 * ROWS].reshape(ROWS * LANES, LANES).astype(F32)
    new = (1.0 - update) * hidden + update * jnp.tanh(made)
    new = new.astype(BF16).reshape(ROWS, LANES, LANES)
    out[...] = new
    if len(rest) != 4:
        again[...] = new
        is_zero = meta[1] == 0
        edge_across[...] = pick(is_zero, new[:2], new[2:])
        edge_pair[...] = pick(is_zero, new[2:], new[:2])


def head_kernel(meta, h_own, h_across, h_pair, w_head1, w_head2, *rest):
    before, out, joined, hidden, w_two = rest if len(rest) == 5 else (None,) + rest
    spread(joined, meta, h_own, h_across, h_pair)
    deep, wide = h_own.shape[2], w_head1.shape[1]
    w_two[...] = jnp.zeros(w_two.shape, F32)
    for s in range(3):
        for u in range(3):
            k = u * 3 + s
            w_two[2 * s : 2 * s + 2, u * wide : (u + 1) * wide] = w_head2[:, k * wide : (k + 1) * wide].astype(F32)
    step = 2
    for r in range(0, ROWS + 2, step):
        left = tap_rows(joined, r, step, 3)
        made = []
        for s in range(3):
            taps = [w_head1[(u * 3 + s) * deep : (u * 3 + s + 1) * deep, :] for u in range(3)]
            made.append(product(left, jnp.concatenate(taps, axis=0)))
        total = made[1] + shift_cols(made[0], 1) + shift_cols(made[2], -1)
        total = by_row(total, r - 1, meta, relu).astype(BF16)
        hidden[r : r + step] = total.reshape(step, LANES, 2 * LANES)
    lane = lax.broadcasted_iota(jnp.int32, (2, LANES), 1)
    target = out
    if before is not None:
        out[0] = before[...]
        target = out.at[1]
    made_all = turned_dot(w_two[...].astype(BF16), tap_rows(hidden, 0, ROWS, 3))
    for r in range(ROWS):
        made = made_all[:, r * LANES : (r + 1) * LANES]
        left = jnp.where(lane == 0, 0.0, pltpu.roll(made[0:2], 1, 1))
        right = jnp.where(lane == LANES - 1, 0.0, pltpu.roll(made[4:6], LANES - 1, 1))
        total = left + made[2:4] + right
        target[0, r : r + 1, :] = total[0:1]
        target[1, r : r + 1, :] = total[1:2]


SMEM = pltpu.SMEM
MIB = 1024 * 1024


def call(kernel, args, out_shape, scratch, smem=1, blocks=None, far=(), micros=0, vmem=20, aliases={}):
    specs = []
    for k, arg in enumerate(args):
        if k < smem:
            specs.append(pl.BlockSpec(memory_space=SMEM))
        elif k in far:
            specs.append(pl.BlockSpec(memory_space=pltpu.HBM))
        elif blocks and k in blocks:
            specs.append(blocks[k])
        else:
            specs.append(pl.BlockSpec(memory_space=pltpu.VMEM))
    return pl.pallas_call(
        kernel,
        out_shape=out_shape,
        grid=(1,) if blocks else (),
        in_specs=specs,
        out_specs=jax.tree.map(lambda o: pl.BlockSpec(memory_space=pltpu.VMEM), out_shape),
        scratch_shapes=scratch,
        input_output_aliases=aliases,
        compiler_params=pltpu.CompilerParams(vmem_limit_bytes=vmem * MIB),
        cost_estimate=pl.CostEstimate(
            flops=1024, bytes_accessed=1024 + 3_000_000 * micros, transcendentals=0
        ),
    )(*args)


def shards(
    first_frame,
    second_frame,
    context,
    hidden_init,
    flow_rows,
    flow_cols,
    block_ids,
    block_counts,
    w_corr,
    w_corr2,
    w_flow1,
    w_flow2,
    w_motion,
    w_gates,
    w_cand,
    w_head1,
    w_head2,
):
    rows_dev, width, channels = first_frame.shape
    tile_count = lax.axis_size("row")
    tile = lax.axis_index("row")
    core = tile & 1
    even_chip = ((tile >> 1) & 1) ^ 1
    meta = jnp.stack([tile, core, even_chip, jnp.int32(tile_count)]).astype(jnp.int32)
    SDS = jax.ShapeDtypeStruct
    VM = pltpu.VMEM
    pixels = rows_dev * width

    blocks = second_frame.reshape(pixels, channels)
    flows = jnp.concatenate([flow_rows, flow_cols]).astype(BF16).reshape(-1, width)
    payload = jnp.concatenate([blocks, jnp.pad(flows, ((0, 0), (0, channels - width)))])
    even, far, pair = swap(payload, chip_even), swap(payload, three_away), swap(payload, in_chip)
    pair, counts, hidden, close = lax.optimization_barrier((pair, block_counts.T, hidden_init, context))
    both = jnp.concatenate([hidden, close], axis=-1)
    frame, own_volume = call(
        own_kernel,
        [first_frame.reshape(pixels, channels), blocks],
        (SDS((pixels, channels), BF16), SDS((rows_dev, pixels, LANES), F32)),
        [],
        smem=0,
    )
    turned, windows = call(
        stage_kernel,
        [meta, block_ids, counts, flow_rows, flow_cols],
        (SDS((ITERS, rows_dev, width, LANES), jnp.int32), SDS((ITERS, CHUNK, LANES), jnp.int32)),
        [],
    )
    even, both, frame, own_volume = lax.optimization_barrier((even, both, frame, own_volume))
    odd = relay(even)
    both_sides = side_tiles(both)
    odd, far, both_sides, turned, windows = lax.optimization_barrier((odd, far, both_sides, turned, windows))
    pair_even, pair_odd = swap(even, in_chip), swap(odd, in_chip)
    around = [even, odd, far, pair, pair_even, pair_odd]
    shape = SDS((NB * rows_dev, pixels, LANES), F32)
    volume = call(early_kernel, [meta, frame, even, far, pair, pair_even], shape, [])
    corr = call(
        corr_kernel,
        [meta, frame, own_volume, turned, windows, odd, pair_odd, volume],
        (SDS((ITERS, rows_dev, DEPTH, width), BF16), shape),
        [VM((width, LANES), F32)],
        aliases={7: 1},
    )[0]

    second_rows = rows_dev + 2 * SECOND_REACH
    first_rows = rows_dev + 2 * FIRST_REACH
    motion_rows = rows_dev + 2 * MOTION_REACH
    flow_second, flow_given = call(
        flow_kernel,
        [meta, payload, *around, w_flow1, w_flow2.T],
        (
            SDS((ITERS, second_rows, width, LANES), BF16),
            SDS((ITERS, motion_rows, width, LANES), BF16),
        ),
        [
            VM((first_rows, width, LANES), BF16),
            VM((7, 16, 2 * LANES), F32),
            VM((3 * LANES, 3 * LANES), BF16),
            VM((ITERS, NB * rows_dev, 16, width), F32),
        ],
    )

    even, odd, pair = swap(corr, chip_even), swap(corr, chip_odd), swap(corr, in_chip)
    h_around, gates_one, gates_two, cand = call(
        context_kernel,
        [meta, both, *both_sides, w_gates, w_cand],
        (
            SDS((motion_rows, width, LANES), BF16),
            SDS((GATE_ROWS, width, 2 * LANES), F32),
            SDS((GATE_ROWS, width, 2 * LANES), F32),
            SDS((rows_dev, width, LANES), F32),
        ),
        [VM((motion_rows, width, 2 * LANES), BF16)],
    )
    even, odd, flow_second, cand = lax.optimization_barrier((even, odd, flow_second, cand))
    near = (corr, even, odd, pair, swap(even, in_chip), swap(odd, in_chip))

    def motion_of(n):
        def part(shape):
            return pl.BlockSpec((None,) + shape[1:], lambda i: (n, 0, 0, 0))

        tiles = [*near, flow_second, flow_given]
        return call(
            motion_kernel,
            [meta, *tiles, w_corr, w_corr2.T, w_motion],
            SDS((motion_rows, width, LANES), BF16),
            [
                VM((first_rows, width, 2 * LANES), BF16),
                VM((second_rows, width, 2 * LANES), BF16),
                VM((DEPTH, w_corr.shape[1]), BF16),
                VM((3, 2 * LANES, 3 * w_corr.shape[1]), BF16),
                VM((3 * 2 * LANES, 3 * LANES), BF16),
            ],
            blocks={1 + k: part(x.shape) for k, x in enumerate(tiles)},
        )

    def head_of(h, h_sides, before=()):
        shape = (2, rows_dev, width)
        return call(
            head_kernel,
            [meta, h, *h_sides, w_head1, w_head2.T, *before],
            SDS((ITERS,) + shape if before else shape, F32),
            [
                VM((rows_dev + 4, width, LANES), BF16),
                VM((rows_dev + 2, width, 2 * LANES), BF16),
                VM((8, 3 * w_head1.shape[1]), F32),
            ],
        )

    tile_of = SDS((rows_dev, width, LANES), BF16)
    edge_of = SDS((2, width, LANES), BF16)
    states = [VM((GATE_ROWS, width, LANES), BF16), VM((GATE_ROWS, width, LANES), F32)]
    h_one = call(
        gate_kernel,
        [meta, gates_one, cand, motion_of(0), w_gates, w_cand, h_around],
        tile_of,
        states,
    )
    one_tiles = (h_one, *side_tiles(h_one))
    h_two, h_again, edge_across, edge_pair = call(
        gate_kernel,
        [meta, gates_two, cand, motion_of(1), w_gates, w_cand, *one_tiles],
        (tile_of, tile_of, edge_of, edge_of),
        states + [VM((motion_rows, width, LANES), BF16)],
    )
    edges = (swap(edge_across, next_row), swap(edge_pair, in_chip))
    delta_one = head_of(h_one, one_tiles[1:])
    deltas = head_of(h_again, edges, (delta_one,))
    return (h_two, deltas)


def solution(mesh):
    tiled = P(("group", "row"), None, None)
    listed = P(None, ("group", "row"), None)
    placed = (tiled,) * 4 + (listed,) * 3 + (P(None, ("group", "row")),) + (P(),) * 9
    return jax.shard_map(
        shards,
        mesh=mesh,
        in_specs=placed,
        out_specs=(tiled, P(None, None, ("group", "row"), None)),
        check_vma=False,
    )
```

```python
import math

import jax
import jax.numpy as jnp
import numpy as np
from jax import lax
from jax.experimental import pallas as pl
from jax.experimental.pallas import tpu as pltpu
from jax.sharding import PartitionSpec as P

RAD = 4
ITERS = 2
REACH = 3
NB = 7
SIDE = 9
TAPS = 81
LANES = 128
FY_MAX = 8
CHUNK = 16
DEPTH = 96
FLOW_SCALE = 0.125
F32 = jnp.float32
BF16 = jnp.bfloat16

ROWS = 4
MOTION_REACH = 4
SECOND_REACH = MOTION_REACH + 1
FIRST_REACH = MOTION_REACH + 2
GATE_REACH = 2


def swap(block, partner):
    devices = lax.axis_size("row")
    route = []
    for i in range(devices):
        j = partner(i)
        route.append((i, j if 0 <= j < devices else i))
    return lax.ppermute(block, "row", route)


def in_chip(i):
    return i ^ 1


def next_row(i):
    return ((i + 1) ^ 1) - 1


def chip_even(i):
    return i ^ 2


def chip_odd(i):
    return ((i + 2) ^ 2) - 2


def three_away(i):
    return i - 3 if i % 2 == 0 else i + 3


def relay(block):
    devices = lax.axis_size("row")
    chips, route = devices // 2, []
    for i in range(devices):
        chip = i // 2
        goal = chip + 2 if chip % 2 == 0 else chip - 2
        if not 0 <= goal < chips:
            goal = chip ^ 1
        route.append((i, 2 * goal + i % 2))
    return lax.ppermute(block, "row", route)


def side_tiles(block):
    return swap(block, next_row), swap(block, in_chip)


def pick(flag, yes, no):
    return jnp.where(flag, yes, no)


def shift_cols(values, shift):
    size = values.shape[0]
    column = lax.broadcasted_iota(jnp.int32, values.shape, 0) & (LANES - 1)
    edge = 0 if shift == 1 else LANES - 1
    return jnp.where(column == edge, 0.0, pltpu.roll(values, shift % size, 0))


def tap_rows(ref, row, rows, taps, lanes=None):
    parts = []
    for u in range(taps):
        piece = ref[pl.ds(row + u, rows)] if lanes is None else ref[pl.ds(row + u, rows), :, lanes]
        parts.append(piece.reshape(rows * LANES, piece.shape[-1]))
    return jnp.concatenate(parts, axis=-1)


def by_row(values, start, meta, apply):
    first = meta[0] * ROWS + start
    height = meta[3] * ROWS
    done = []
    for r in range(values.shape[0] // LANES):
        inside = (first + r >= 0) & (first + r < height)
        done.append(jnp.where(inside, apply(values[r * LANES : (r + 1) * LANES]), 0.0))
    return jnp.concatenate(done, axis=0)


def turned_dot(left, right):
    return lax.dot_general(left, right, (((1,), (1,)), ((), ())), preferred_element_type=F32)


def relu(x):
    return jnp.maximum(x, 0.0)


def choose(planes, index):
    bit = 1
    while len(planes) > 1:
        on = (index & bit) != 0
        pairs = [
            jnp.where(on, planes[k + 1], planes[k]) if k + 1 < len(planes) else planes[k]
            for k in range(0, len(planes), 2)
        ]
        planes, bit = pairs, 2 * bit
    return planes[0]


PART = LANES // 8


def volume_of(frame, block, spot, half):
    pieces = []
    for r in (2 * half, 2 * half + 1):
        for m in range(8):
            start = r * LANES + ((m - r - 4 * spot) & 7) * PART
            start = start if isinstance(start, int) else pl.multiple_of(start, PART)
            pieces.append(block[pl.ds(start, PART), :])
    return turned_dot(frame, jnp.concatenate(pieces, axis=0))


def own_kernel(first, own, frame, own_volume):
    frame[...] = first[...]
    for half in range(2):
        made = volume_of(frame[...], own, REACH, half)
        own_volume[2 * half] = made[:, :LANES]
        own_volume[2 * half + 1] = made[:, LANES:]


def stage_kernel(meta, ids, counts, rows, cols, turned, windows):
    shape = windows.shape[1:]
    for n in range(ITERS):
        bits = jnp.zeros(shape, jnp.int32)
        count = jnp.broadcast_to(counts[:, n : n + 1], shape)
        for k in range(ids.shape[2]):
            spot = jnp.broadcast_to(ids[n, :, k : k + 1], shape) - meta[0] + REACH
            listed = (k < count) & (spot >= 0) & (spot < NB)
            bits = bits | jnp.where(listed, 1 << jnp.clip(spot, 0, NB - 1), 0)
        windows[n] = bits
    for n in range(ITERS):
        for i in range(ROWS):
            packed = (rows[n, i : i + 1, :] + FY_MAX) * 64 + cols[n, i : i + 1, :] + 32
            turned[n, i] = jnp.broadcast_to(packed, (LANES, LANES)).T


def multiply(blocks, meta, frame, volume):
    core, even_chip = meta[1], meta[2]
    plus = pick(core == 0, 1, -1)
    two = pick(even_chip == 1, 2, -2)
    spots = {
        "pair": REACH + plus,
        "far": REACH - 3 * plus,
        "even": REACH + two,
        "odd": REACH - two,
        "pair_even": REACH + plus + two,
        "pair_odd": REACH + plus - two,
    }
    for name, block in blocks.items():
        spot = spots[name]
        for half in range(2):
            product = volume_of(frame[...], block, spot, half)
            volume[spot * ROWS + 2 * half] = product[:, :LANES]
            volume[spot * ROWS + 2 * half + 1] = product[:, LANES:]


def early_kernel(meta, frame, even, far, pair, pair_even, volume):
    multiply(dict(even=even, far=far, pair=pair, pair_even=pair_even), meta, frame, volume)


def corr_kernel(meta, frame, own_volume, turned, windows, odd, pair_odd, early_volume, out, volume, picked):
    multiply(dict(odd=odd, pair_odd=pair_odd), meta, frame, volume)

    def plane(b, at):
        own = b - REACH * ROWS
        return own_volume[own, at, :] if 0 <= own < ROWS else volume[b, at, :]

    scale = 1.0 / math.sqrt(frame.shape[-1])
    chunk = CHUNK
    lane = lax.broadcasted_iota(jnp.int32, (chunk, LANES), 1)
    sub = lax.broadcasted_iota(jnp.int32, (chunk, LANES), 0)
    lane_dy = (lane * 57) >> 9
    lane_dx = lane - lane_dy * SIDE - RAD
    for n in range(ITERS):
        bits = windows[n]
        for i in range(ROWS):

            def step(index, carry, n=n, bits=bits, i=i):
                j0 = pl.multiple_of(index * chunk, chunk)
                packed = turned[n, i, pl.ds(j0, chunk), :]
                lift = packed >> 6
                start = sub + (j0 - 32) + (packed & 63)
                at = pl.ds(pl.multiple_of(i * LANES + j0, chunk), chunk)
                planes = [plane(i + k, at) for k in range(2 * FY_MAX + SIDE)]
                group = ((lane - start + RAD) & (LANES - 1)) >> 4
                most = choose(planes[:24], lift + ((group - lift - i) & 7))
                last = choose(planes[8:], lift)
                column = start + lane_dx
                row = lift + i + lane_dy
                wrapped = (column + (row & 7) * PART) & (LANES - 1)
                value = jnp.where(
                    lane_dy == 8,
                    jnp.take_along_axis(last, wrapped, axis=1, mode="promise_in_bounds"),
                    jnp.take_along_axis(most, wrapped, axis=1, mode="promise_in_bounds"),
                )
                seen = ((bits >> (row >> 2)) & 1) == 1
                seen = seen & (column >= 0) & (column < LANES) & (lane < TAPS)
                picked[pl.ds(j0, chunk), :] = jnp.where(seen, value * scale, 0.0)
                return carry

            lax.fori_loop(0, LANES // chunk, step, 0, unroll=8)
            out[n, i] = picked[...].T[:DEPTH].astype(BF16)


def flow_kernel(
    meta, own, even, odd, far, pair, pair_even, pair_odd, w_flow1, w_flow2, second, given, first, w_one, w_two, windows
):
    made, wide = w_flow2.shape[0], first.shape[2]
    w_two[...] = jnp.zeros(w_two.shape, BF16)
    for u in range(3):
        for s in range(3):
            low = (s + 1) * LANES - made
            tap = slice((u * 3 + s) * wide, (u * 3 + s + 1) * wide)
            w_two[low : low + made, u * wide : (u + 1) * wide] = w_flow2[:, tap]
    weights = w_flow1[...].astype(F32)
    w_one[...] = jnp.zeros(w_one.shape, F32)
    for u in range(7):
        w_one[u, 0:14, :LANES] = weights[u * 14 : (u + 1) * 14, :]
    tap = lax.broadcasted_iota(jnp.int32, (16, LANES), 0)
    lane = lax.broadcasted_iota(jnp.int32, (16, LANES), 1)
    w_one[3, :, LANES:] = jnp.where((tap - 6 == lane - (LANES - 2)) & (lane >= LANES - 2), 1.0, 0.0)
    w_all = w_one[...].reshape(7 * 16, 2 * LANES).astype(BF16)

    tile, core, even_chip, tiles = meta[0], meta[1], meta[2], meta[3]
    plus = pick(core == 0, 1, -1)
    two = pick(even_chip == 1, 2, -2)
    spots = (
        (own, 0),
        (pair, plus),
        (far, -3 * plus),
        (even, two),
        (odd, -two),
        (pair_even, plus + two),
        (pair_odd, plus - two),
    )
    windows[:, :, 14:, :] = jnp.zeros(windows.shape[:2] + (2, LANES), F32)
    column = lax.broadcasted_iota(jnp.int32, (4 * ROWS, LANES), 1)
    for block, spot in spots:
        inside = (tile + spot >= 0) & (tile + spot < tiles)
        lines = jnp.where(inside, block[ROWS * LANES :, :LANES].astype(F32) * FLOW_SCALE, 0.0)
        for s in range(7):
            reach = s - 3
            moved = pltpu.roll(lines, (-reach) % LANES, 1) if reach else lines
            seen = (column + reach >= 0) & (column + reach < LANES)
            moved = jnp.where(seen, moved, 0.0)
            for c in range(2):
                for n in range(ITERS):
                    for r in range(ROWS):
                        k = (c * ITERS + n) * ROWS + r
                        windows[n, (spot + REACH) * ROWS + r, 2 * s + c : 2 * s + c + 1, :] = moved[k : k + 1, :]

    top = 3 * ROWS - FIRST_REACH - 3
    first_rows = ROWS + 2 * FIRST_REACH
    second_rows = ROWS + 2 * SECOND_REACH
    offset = FIRST_REACH - MOTION_REACH
    for n in range(ITERS):
        for r in range(first_rows):
            window = windows[n, top + r : top + r + 7].reshape(7 * 16, LANES).astype(BF16)
            made = lax.dot_general(window, w_all, (((0,), (0,)), ((), ())), preferred_element_type=F32)
            value = by_row(made[:, :LANES], r - FIRST_REACH, meta, relu)
            first[r] = value.astype(BF16)
            if offset <= r < first_rows - offset:
                given[n, r - offset] = made[:, LANES:].astype(BF16)
        step = 2
        for r in range(0, second_rows, step):
            made = turned_dot(tap_rows(first, r, step, 3), w_two[...])
            total = (
                made[:, LANES : 2 * LANES]
                + shift_cols(made[:, :LANES], 1)
                + shift_cols(made[:, 2 * LANES :], -1)
            )
            total = by_row(total, r - SECOND_REACH, meta, relu).astype(BF16)
            second[n, r : r + step] = total.reshape(step, LANES, LANES)


def motion_kernel(
    meta, own, even, odd, pair, pair_even, pair_odd, second, given, w_corr, w_corr2, w_motion, out, one, two, w_one, w_two, w_three
):
    core, even_chip = meta[1], meta[2]
    is_even, is_zero = even_chip == 1, core == 0

    w_one[...] = jnp.zeros(w_one.shape, F32)
    w_one[: w_corr.shape[0], :] = w_corr[...].astype(F32)
    w_first = w_one[...].astype(BF16)
    w_three[...] = jnp.zeros(w_three.shape, BF16)
    wide, made_two, made_three = w_one.shape[1], w_corr2.shape[0], w_motion.shape[1]
    w_two[:, made_two:, :] = jnp.zeros((3, w_two.shape[1] - made_two, w_two.shape[2]), BF16)
    for u in range(3):
        for s in range(3):
            tap = slice((u * 3 + s) * wide, (u * 3 + s + 1) * wide)
            w_two[s, :made_two, u * wide : (u + 1) * wide] = w_corr2[:, tap]
            w_three[u * wide : (u + 1) * wide, s * LANES : s * LANES + made_three] = w_motion[tap, :]

    def corr_row(row):
        tile, r = (row + 2 * ROWS) // ROWS - 2, row % ROWS
        if tile == 0:
            return own[r]
        if tile == -2:
            return pick(is_even, odd[r], even[r])
        if tile == 2:
            return pick(is_even, even[r], odd[r])
        if tile == -1:
            return pick(is_zero, pick(is_even, pair_odd[r], pair_even[r]), pair[r])
        return pick(is_zero, pair[r], pick(is_even, pair_even[r], pair_odd[r]))

    for r in range(ROWS + 2 * FIRST_REACH):
        made = lax.dot_general(
            corr_row(r - FIRST_REACH), w_first, (((0,), (0,)), ((), ())), preferred_element_type=F32
        )
        one[r] = by_row(made, r - FIRST_REACH, meta, relu).astype(BF16)

    step = 2
    zeros = jnp.zeros((step * LANES, LANES), BF16)

    def second_step(index, carry):
        r = index * step
        left = tap_rows(one, r, step, 3)
        made = [turned_dot(left, w_two[s]) for s in range(3)]
        total = made[1] + shift_cols(made[0], 1) + shift_cols(made[2], -1)
        total = by_row(total, r - SECOND_REACH, meta, relu).astype(BF16)
        flow = second[pl.ds(r, step)].reshape(step * LANES, LANES)
        total = total + jnp.concatenate([zeros, flow], axis=-1)
        two[pl.ds(r, step)] = total.reshape(step, LANES, 2 * LANES)
        return carry

    lax.fori_loop(0, (ROWS + 2 * SECOND_REACH) // step, second_step, 0, unroll=7)

    step3 = 2

    def third_step(index, carry):
        r = index * step3
        made = jnp.dot(tap_rows(two, r, step3, 3), w_three[...], preferred_element_type=F32)
        total = (
            made[:, LANES : 2 * LANES]
            + shift_cols(made[:, :LANES], 1)
            + shift_cols(made[:, 2 * LANES :], -1)
        )
        total = by_row(total, r - MOTION_REACH, meta, relu).astype(BF16)
        total = total + given[pl.ds(r, step3)].reshape(step3 * LANES, LANES)
        out[pl.ds(r, step3)] = total.reshape(step3, LANES, LANES)
        return carry

    lax.fori_loop(0, (ROWS + 2 * MOTION_REACH) // step3, third_step, 0, unroll=6)


def spread(scratch, meta, own, across, pair):
    tile, core, tiles = meta[0], meta[1], meta[3]
    is_zero = core == 0
    nothing = jnp.zeros((), BF16)
    reach = (scratch.shape[0] - ROWS) // 2
    for r in range(reach):
        up = r if across.shape[0] == reach else ROWS - reach + r
        above = pick(is_zero, across[up], pair[up])
        below = pick(is_zero, pair[r], across[r])
        scratch[r] = jnp.where(tile > 0, above, nothing)
        scratch[reach + ROWS + r] = jnp.where(tile < tiles - 1, below, nothing)
    scratch[reach : reach + ROWS] = own[...]


def part_of(weight, low, high):
    deep = weight.shape[0] // 5
    return jnp.concatenate([weight[u * deep + low : u * deep + high, :] for u in range(5)], axis=0)


def product(left, right):
    return jnp.dot(left, right, preferred_element_type=F32)


def sigmoid(x):
    return 0.5 * jnp.tanh(0.5 * x) + 0.5


GATE_ROWS = ROWS + 2 * GATE_REACH
STEP = 4


def context_kernel(meta, both, across, pair, w_gates, w_cand, hidden, gates_one, gates_two, cand, joined):
    spread(joined, meta, both, across, pair)
    hidden[...] = joined[:, :, :LANES]
    near = slice(LANES, 2 * LANES)
    for r in range(0, GATE_ROWS, STEP):
        made = product(tap_rows(joined, r, STEP, 5, near), part_of(w_gates, LANES, 2 * LANES))
        gates_two[r : r + STEP] = made.reshape(STEP, LANES, 2 * LANES)
        made = made + product(tap_rows(hidden, r, STEP, 5), part_of(w_gates, 0, LANES))
        gates_one[r : r + STEP] = made.reshape(STEP, LANES, 2 * LANES)
    made = product(tap_rows(joined, GATE_REACH, ROWS, 5, near), part_of(w_cand, LANES, 2 * LANES))
    cand[...] = made.reshape(ROWS, LANES, LANES)


def gate_kernel(meta, gates_made, cand_made, motion, w_gates, w_cand, *rest):
    if len(rest) == 4:
        around, out, state, keep = rest
    else:
        h_own, h_across, h_pair, out, again, edge_across, edge_pair, state, keep, around = rest
        spread(around, meta, h_own, h_across, h_pair)
    for r in range(0, GATE_ROWS, STEP):
        gates = gates_made[r : r + STEP].reshape(STEP * LANES, 2 * LANES)
        gates = gates + product(tap_rows(motion, r, STEP, 5), part_of(w_gates, 2 * LANES, 3 * LANES))
        if len(rest) != 4:
            gates = gates + product(tap_rows(around, r, STEP, 5), part_of(w_gates, 0, LANES))
        hidden = around[r + 2 : r + 2 + STEP].reshape(STEP * LANES, LANES).astype(F32)
        reset = (sigmoid(gates[:, LANES:]) * hidden).astype(BF16)
        state[r : r + STEP] = reset.reshape(STEP, LANES, LANES)
        keep[r : r + STEP] = gates[:, :LANES].reshape(STEP, LANES, LANES)
    made = cand_made[...].reshape(ROWS * LANES, LANES)
    made = made + product(tap_rows(motion, GATE_REACH, ROWS, 5), part_of(w_cand, 2 * LANES, 3 * LANES))
    made = made + product(tap_rows(state, 0, ROWS, 5), part_of(w_cand, 0, LANES))
    update = sigmoid(keep[2 : 2 + ROWS].reshape(ROWS * LANES, LANES))
    hidden = around[ROWS : 2 * ROWS].reshape(ROWS * LANES, LANES).astype(F32)
    new = (1.0 - update) * hidden + update * jnp.tanh(made)
    new = new.astype(BF16).reshape(ROWS, LANES, LANES)
    out[...] = new
    if len(rest) != 4:
        again[...] = new
        is_zero = meta[1] == 0
        edge_across[...] = pick(is_zero, new[:2], new[2:])
        edge_pair[...] = pick(is_zero, new[2:], new[:2])


def head_kernel(meta, h_own, h_across, h_pair, w_head1, w_head2, *rest):
    before, out, joined, hidden, w_two = rest if len(rest) == 5 else (None,) + rest
    spread(joined, meta, h_own, h_across, h_pair)
    deep, wide = h_own.shape[2], w_head1.shape[1]
    w_two[...] = jnp.zeros(w_two.shape, F32)
    for s in range(3):
        for u in range(3):
            k = u * 3 + s
            w_two[2 * s : 2 * s + 2, u * wide : (u + 1) * wide] = w_head2[:, k * wide : (k + 1) * wide].astype(F32)
    step = 2
    for r in range(0, ROWS + 2, step):
        left = tap_rows(joined, r, step, 3)
        made = []
        for s in range(3):
            taps = [w_head1[(u * 3 + s) * deep : (u * 3 + s + 1) * deep, :] for u in range(3)]
            made.append(product(left, jnp.concatenate(taps, axis=0)))
        total = made[1] + shift_cols(made[0], 1) + shift_cols(made[2], -1)
        total = by_row(total, r - 1, meta, relu).astype(BF16)
        hidden[r : r + step] = total.reshape(step, LANES, 2 * LANES)
    lane = lax.broadcasted_iota(jnp.int32, (2, LANES), 1)
    target = out
    if before is not None:
        out[0] = before[...]
        target = out.at[1]
    made_all = turned_dot(w_two[...].astype(BF16), tap_rows(hidden, 0, ROWS, 3))
    for r in range(ROWS):
        made = made_all[:, r * LANES : (r + 1) * LANES]
        left = jnp.where(lane == 0, 0.0, pltpu.roll(made[0:2], 1, 1))
        right = jnp.where(lane == LANES - 1, 0.0, pltpu.roll(made[4:6], LANES - 1, 1))
        total = left + made[2:4] + right
        target[0, r : r + 1, :] = total[0:1]
        target[1, r : r + 1, :] = total[1:2]


SMEM = pltpu.SMEM
MIB = 1024 * 1024


def call(kernel, args, out_shape, scratch, smem=1, blocks=None, far=(), micros=0, vmem=20, aliases={}):
    specs = []
    for k, arg in enumerate(args):
        if k < smem:
            specs.append(pl.BlockSpec(memory_space=SMEM))
        elif k in far:
            specs.append(pl.BlockSpec(memory_space=pltpu.HBM))
        elif blocks and k in blocks:
            specs.append(blocks[k])
        else:
            specs.append(pl.BlockSpec(memory_space=pltpu.VMEM))
    return pl.pallas_call(
        kernel,
        out_shape=out_shape,
        grid=(1,) if blocks else (),
        in_specs=specs,
        out_specs=jax.tree.map(lambda o: pl.BlockSpec(memory_space=pltpu.VMEM), out_shape),
        scratch_shapes=scratch,
        input_output_aliases=aliases,
        compiler_params=pltpu.CompilerParams(vmem_limit_bytes=vmem * MIB),
        cost_estimate=pl.CostEstimate(
            flops=1024, bytes_accessed=1024 + 3_000_000 * micros, transcendentals=0
        ),
    )(*args)


def shards(
    first_frame,
    second_frame,
    context,
    hidden_init,
    flow_rows,
    flow_cols,
    block_ids,
    block_counts,
    w_corr,
    w_corr2,
    w_flow1,
    w_flow2,
    w_motion,
    w_gates,
    w_cand,
    w_head1,
    w_head2,
):
    rows_dev, width, channels = first_frame.shape
    tile_count = lax.axis_size("row")
    tile = lax.axis_index("row")
    core = tile & 1
    even_chip = ((tile >> 1) & 1) ^ 1
    meta = jnp.stack([tile, core, even_chip, jnp.int32(tile_count)]).astype(jnp.int32)
    SDS = jax.ShapeDtypeStruct
    VM = pltpu.VMEM
    pixels = rows_dev * width

    blocks = second_frame.reshape(pixels, channels)
    flows = jnp.concatenate([flow_rows, flow_cols]).astype(BF16).reshape(-1, width)
    payload = jnp.concatenate([blocks, jnp.pad(flows, ((0, 0), (0, channels - width)))])
    even, far, pair = swap(payload, chip_even), swap(payload, three_away), swap(payload, in_chip)
    pair, counts, hidden, close = lax.optimization_barrier((pair, block_counts.T, hidden_init, context))
    both = jnp.concatenate([hidden, close], axis=-1)
    frame, own_volume = call(
        own_kernel,
        [first_frame.reshape(pixels, channels), blocks],
        (SDS((pixels, channels), BF16), SDS((rows_dev, pixels, LANES), F32)),
        [],
        smem=0,
    )
    turned, windows = call(
        stage_kernel,
        [meta, block_ids, counts, flow_rows, flow_cols],
        (SDS((ITERS, rows_dev, width, LANES), jnp.int32), SDS((ITERS, CHUNK, LANES), jnp.int32)),
        [],
    )
    even, both, frame, own_volume = lax.optimization_barrier((even, both, frame, own_volume))
    odd = relay(even)
    both_sides = side_tiles(both)
    odd, far, both_sides, turned, windows = lax.optimization_barrier((odd, far, both_sides, turned, windows))
    pair_even, pair_odd = swap(even, in_chip), swap(odd, in_chip)
    around = [even, odd, far, pair, pair_even, pair_odd]
    shape = SDS((NB * rows_dev, pixels, LANES), F32)
    volume = call(early_kernel, [meta, frame, even, far, pair, pair_even], shape, [])
    corr = call(
        corr_kernel,
        [meta, frame, own_volume, turned, windows, odd, pair_odd, volume],
        (SDS((ITERS, rows_dev, DEPTH, width), BF16), shape),
        [VM((width, LANES), F32)],
        aliases={7: 1},
    )[0]

    second_rows = rows_dev + 2 * SECOND_REACH
    first_rows = rows_dev + 2 * FIRST_REACH
    motion_rows = rows_dev + 2 * MOTION_REACH
    flow_second, flow_given = call(
        flow_kernel,
        [meta, payload, *around, w_flow1, w_flow2.T],
        (
            SDS((ITERS, second_rows, width, LANES), BF16),
            SDS((ITERS, motion_rows, width, LANES), BF16),
        ),
        [
            VM((first_rows, width, LANES), BF16),
            VM((7, 16, 2 * LANES), F32),
            VM((3 * LANES, 3 * LANES), BF16),
            VM((ITERS, NB * rows_dev, 16, width), F32),
        ],
    )

    even, odd, pair = swap(corr, chip_even), swap(corr, chip_odd), swap(corr, in_chip)
    h_around, gates_one, gates_two, cand = call(
        context_kernel,
        [meta, both, *both_sides, w_gates, w_cand],
        (
            SDS((motion_rows, width, LANES), BF16),
            SDS((GATE_ROWS, width, 2 * LANES), F32),
            SDS((GATE_ROWS, width, 2 * LANES), F32),
            SDS((rows_dev, width, LANES), F32),
        ),
        [VM((motion_rows, width, 2 * LANES), BF16)],
    )
    even, odd, flow_second, cand = lax.optimization_barrier((even, odd, flow_second, cand))
    near = (corr, even, odd, pair, swap(even, in_chip), swap(odd, in_chip))

    def motion_of(n):
        def part(shape):
            return pl.BlockSpec((None,) + shape[1:], lambda i: (n, 0, 0, 0))

        tiles = [*near, flow_second, flow_given]
        return call(
            motion_kernel,
            [meta, *tiles, w_corr, w_corr2.T, w_motion],
            SDS((motion_rows, width, LANES), BF16),
            [
                VM((first_rows, width, 2 * LANES), BF16),
                VM((second_rows, width, 2 * LANES), BF16),
                VM((DEPTH, w_corr.shape[1]), F32),
                VM((3, 2 * LANES, 3 * w_corr.shape[1]), BF16),
                VM((3 * 2 * LANES, 3 * LANES), BF16),
            ],
            blocks={1 + k: part(x.shape) for k, x in enumerate(tiles)},
        )

    def head_of(h, h_sides, before=()):
        shape = (2, rows_dev, width)
        return call(
            head_kernel,
            [meta, h, *h_sides, w_head1, w_head2.T, *before],
            SDS((ITERS,) + shape if before else shape, F32),
            [
                VM((rows_dev + 4, width, LANES), BF16),
                VM((rows_dev + 2, width, 2 * LANES), BF16),
                VM((8, 3 * w_head1.shape[1]), F32),
            ],
        )

    tile_of = SDS((rows_dev, width, LANES), BF16)
    edge_of = SDS((2, width, LANES), BF16)
    states = [VM((GATE_ROWS, width, LANES), BF16), VM((GATE_ROWS, width, LANES), F32)]
    h_one = call(
        gate_kernel,
        [meta, gates_one, cand, motion_of(0), w_gates, w_cand, h_around],
        tile_of,
        states,
    )
    one_tiles = (h_one, *side_tiles(h_one))
    h_two, h_again, edge_across, edge_pair = call(
        gate_kernel,
        [meta, gates_two, cand, motion_of(1), w_gates, w_cand, *one_tiles],
        (tile_of, tile_of, edge_of, edge_of),
        states + [VM((motion_rows, width, LANES), BF16)],
    )
    edges = (swap(edge_across, next_row), swap(edge_pair, in_chip))
    delta_one = head_of(h_one, one_tiles[1:])
    deltas = head_of(h_again, edges, (delta_one,))
    return (h_two, deltas)


def solution(mesh):
    tiled = P(("group", "row"), None, None)
    listed = P(None, ("group", "row"), None)
    placed = (tiled,) * 4 + (listed,) * 3 + (P(None, ("group", "row")),) + (P(),) * 9
    return jax.shard_map(
        shards,
        mesh=mesh,
        in_specs=placed,
        out_specs=(tiled, P(None, None, ("group", "row"), None)),
        check_vma=False,
    )
```

```python
import math

import jax
import jax.numpy as jnp
import numpy as np
from jax import lax
from jax.experimental import pallas as pl
from jax.experimental.pallas import tpu as pltpu
from jax.sharding import PartitionSpec as P

RAD = 4
ITERS = 2
REACH = 3
NB = 7
SIDE = 9
TAPS = 81
LANES = 128
FY_MAX = 8
CHUNK = 16
DEPTH = 96
FLOW_SCALE = 0.125
F32 = jnp.float32
BF16 = jnp.bfloat16

ROWS = 4
MOTION_REACH = 4
SECOND_REACH = MOTION_REACH + 1
FIRST_REACH = MOTION_REACH + 2
GATE_REACH = 2


def swap(block, partner):
    devices = lax.axis_size("row")
    route = []
    for i in range(devices):
        j = partner(i)
        route.append((i, j if 0 <= j < devices else i))
    return lax.ppermute(block, "row", route)


def in_chip(i):
    return i ^ 1


def next_row(i):
    return ((i + 1) ^ 1) - 1


def chip_even(i):
    return i ^ 2


def chip_odd(i):
    return ((i + 2) ^ 2) - 2


def three_away(i):
    return i - 3 if i % 2 == 0 else i + 3


def relay(block):
    devices = lax.axis_size("row")
    chips, route = devices // 2, []
    for i in range(devices):
        chip = i // 2
        goal = chip + 2 if chip % 2 == 0 else chip - 2
        if not 0 <= goal < chips:
            goal = chip ^ 1
        route.append((i, 2 * goal + i % 2))
    return lax.ppermute(block, "row", route)


def side_tiles(block):
    return swap(block, next_row), swap(block, in_chip)


def pick(flag, yes, no):
    return jnp.where(flag, yes, no)


def shift_cols(values, shift):
    size = values.shape[0]
    column = lax.broadcasted_iota(jnp.int32, values.shape, 0) & (LANES - 1)
    edge = 0 if shift == 1 else LANES - 1
    return jnp.where(column == edge, 0.0, pltpu.roll(values, shift % size, 0))


def tap_rows(ref, row, rows, taps, lanes=None):
    parts = []
    for u in range(taps):
        piece = ref[pl.ds(row + u, rows)] if lanes is None else ref[pl.ds(row + u, rows), :, lanes]
        parts.append(piece.reshape(rows * LANES, piece.shape[-1]))
    return jnp.concatenate(parts, axis=-1)


def by_row(values, start, meta, apply):
    first = meta[0] * ROWS + start
    height = meta[3] * ROWS
    done = []
    for r in range(values.shape[0] // LANES):
        inside = (first + r >= 0) & (first + r < height)
        done.append(jnp.where(inside, apply(values[r * LANES : (r + 1) * LANES]), 0.0))
    return jnp.concatenate(done, axis=0)


def turned_dot(left, right):
    return lax.dot_general(left, right, (((1,), (1,)), ((), ())), preferred_element_type=F32)


def relu(x):
    return jnp.maximum(x, 0.0)


def choose(planes, index):
    bit = 1
    while len(planes) > 1:
        on = (index & bit) != 0
        pairs = [
            jnp.where(on, planes[k + 1], planes[k]) if k + 1 < len(planes) else planes[k]
            for k in range(0, len(planes), 2)
        ]
        planes, bit = pairs, 2 * bit
    return planes[0]


PART = LANES // 8


def volume_of(frame, block, spot, half):
    pieces = []
    for r in (2 * half, 2 * half + 1):
        for m in range(8):
            start = r * LANES + ((m - r - 4 * spot) & 7) * PART
            start = start if isinstance(start, int) else pl.multiple_of(start, PART)
            pieces.append(block[pl.ds(start, PART), :])
    return turned_dot(frame, jnp.concatenate(pieces, axis=0))


def own_kernel(first, own, frame, own_volume):
    frame[...] = first[...]
    for half in range(2):
        made = volume_of(frame[...], own, REACH, half)
        own_volume[2 * half] = made[:, :LANES]
        own_volume[2 * half + 1] = made[:, LANES:]


def stage_kernel(meta, ids, counts, rows, cols, turned, windows):
    shape = windows.shape[1:]
    for n in range(ITERS):
        bits = jnp.zeros(shape, jnp.int32)
        count = jnp.broadcast_to(counts[:, n : n + 1], shape)
        for k in range(ids.shape[2]):
            spot = jnp.broadcast_to(ids[n, :, k : k + 1], shape) - meta[0] + REACH
            listed = (k < count) & (spot >= 0) & (spot < NB)
            bits = bits | jnp.where(listed, 1 << jnp.clip(spot, 0, NB - 1), 0)
        windows[n] = bits
    for n in range(ITERS):
        for i in range(ROWS):
            packed = (rows[n, i : i + 1, :] + FY_MAX) * 64 + cols[n, i : i + 1, :] + 32
            turned[n, i] = jnp.broadcast_to(packed, (LANES, LANES)).T


def multiply(blocks, meta, frame, volume):
    core, even_chip = meta[1], meta[2]
    plus = pick(core == 0, 1, -1)
    two = pick(even_chip == 1, 2, -2)
    spots = {
        "pair": REACH + plus,
        "far": REACH - 3 * plus,
        "even": REACH + two,
        "odd": REACH - two,
        "pair_even": REACH + plus + two,
        "pair_odd": REACH + plus - two,
    }
    for name, block in blocks.items():
        spot = spots[name]
        for half in range(2):
            product = volume_of(frame[...], block, spot, half)
            volume[spot * ROWS + 2 * half] = product[:, :LANES]
            volume[spot * ROWS + 2 * half + 1] = product[:, LANES:]


def early_kernel(meta, frame, even, far, pair, pair_even, volume):
    multiply(dict(even=even, far=far, pair=pair, pair_even=pair_even), meta, frame, volume)


def corr_kernel(meta, frame, own_volume, turned, windows, odd, pair_odd, early_volume, out, volume, picked):
    multiply(dict(odd=odd, pair_odd=pair_odd), meta, frame, volume)

    def plane(b, at):
        own = b - REACH * ROWS
        return own_volume[own, at, :] if 0 <= own < ROWS else volume[b, at, :]

    scale = 1.0 / math.sqrt(frame.shape[-1])
    chunk = CHUNK
    lane = lax.broadcasted_iota(jnp.int32, (chunk, LANES), 1)
    sub = lax.broadcasted_iota(jnp.int32, (chunk, LANES), 0)
    lane_dy = (lane * 57) >> 9
    lane_dx = lane - lane_dy * SIDE - RAD
    for n in range(ITERS):
        bits = windows[n]
        for i in range(ROWS):

            def step(index, carry, n=n, bits=bits, i=i):
                j0 = pl.multiple_of(index * chunk, chunk)
                packed = turned[n, i, pl.ds(j0, chunk), :]
                lift = packed >> 6
                start = sub + (j0 - 32) + (packed & 63)
                at = pl.ds(pl.multiple_of(i * LANES + j0, chunk), chunk)
                planes = [plane(i + k, at) for k in range(2 * FY_MAX + SIDE)]
                group = ((lane - start + RAD) & (LANES - 1)) >> 4
                most = choose(planes[:24], lift + ((group - lift - i) & 7))
                last = choose(planes[8:], lift)
                column = start + lane_dx
                row = lift + i + lane_dy
                wrapped = (column + (row & 7) * PART) & (LANES - 1)
                value = jnp.where(
                    lane_dy == 8,
                    jnp.take_along_axis(last, wrapped, axis=1, mode="promise_in_bounds"),
                    jnp.take_along_axis(most, wrapped, axis=1, mode="promise_in_bounds"),
                )
                seen = ((bits >> (row >> 2)) & 1) == 1
                seen = seen & (column >= 0) & (column < LANES) & (lane < TAPS)
                picked[pl.ds(j0, chunk), :] = jnp.where(seen, value * scale, 0.0)
                return carry

            lax.fori_loop(0, LANES // chunk, step, 0, unroll=8)
            out[n, i] = picked[...].T[:DEPTH].astype(BF16)


def flow_kernel(
    meta, own, even, odd, far, pair, pair_even, pair_odd, w_flow1, w_flow2, second, given, first, w_one, w_two, windows
):
    made, wide = w_flow2.shape[0], first.shape[2]
    w_two[...] = jnp.zeros(w_two.shape, BF16)
    for u in range(3):
        for s in range(3):
            low = (s + 1) * LANES - made
            tap = slice((u * 3 + s) * wide, (u * 3 + s + 1) * wide)
            w_two[low : low + made, u * wide : (u + 1) * wide] = w_flow2[:, tap]
    weights = w_flow1[...].astype(F32)
    w_one[...] = jnp.zeros(w_one.shape, F32)
    for u in range(7):
        w_one[u, 0:14, :LANES] = weights[u * 14 : (u + 1) * 14, :]
    tap = lax.broadcasted_iota(jnp.int32, (16, LANES), 0)
    lane = lax.broadcasted_iota(jnp.int32, (16, LANES), 1)
    w_one[3, :, LANES:] = jnp.where((tap - 6 == lane - (LANES - 2)) & (lane >= LANES - 2), 1.0, 0.0)
    w_all = w_one[...].reshape(7 * 16, 2 * LANES).astype(BF16)

    tile, core, even_chip, tiles = meta[0], meta[1], meta[2], meta[3]
    plus = pick(core == 0, 1, -1)
    two = pick(even_chip == 1, 2, -2)
    spots = (
        (own, 0),
        (pair, plus),
        (far, -3 * plus),
        (even, two),
        (odd, -two),
        (pair_even, plus + two),
        (pair_odd, plus - two),
    )
    windows[:, :, 14:, :] = jnp.zeros(windows.shape[:2] + (2, LANES), F32)
    column = lax.broadcasted_iota(jnp.int32, (4 * ROWS, LANES), 1)
    for block, spot in spots:
        inside = (tile + spot >= 0) & (tile + spot < tiles)
        lines = jnp.where(inside, block[ROWS * LANES :, :LANES].astype(F32) * FLOW_SCALE, 0.0)
        for s in range(7):
            reach = s - 3
            moved = pltpu.roll(lines, (-reach) % LANES, 1) if reach else lines
            seen = (column + reach >= 0) & (column + reach < LANES)
            moved = jnp.where(seen, moved, 0.0)
            for c in range(2):
                for n in range(ITERS):
                    for r in range(ROWS):
                        k = (c * ITERS + n) * ROWS + r
                        windows[n, (spot + REACH) * ROWS + r, 2 * s + c : 2 * s + c + 1, :] = moved[k : k + 1, :]

    top = 3 * ROWS - FIRST_REACH - 3
    first_rows = ROWS + 2 * FIRST_REACH
    second_rows = ROWS + 2 * SECOND_REACH
    offset = FIRST_REACH - MOTION_REACH
    for n in range(ITERS):
        for r in range(first_rows):
            window = windows[n, top + r : top + r + 7].reshape(7 * 16, LANES).astype(BF16)
            made = lax.dot_general(window, w_all, (((0,), (0,)), ((), ())), preferred_element_type=F32)
            value = by_row(made[:, :LANES], r - FIRST_REACH, meta, relu)
            first[r] = value.astype(BF16)
            if offset <= r < first_rows - offset:
                given[n, r - offset] = made[:, LANES:].astype(BF16)
        step = 2
        for r in range(0, second_rows, step):
            made = turned_dot(tap_rows(first, r, step, 3), w_two[...])
            total = (
                made[:, LANES : 2 * LANES]
                + shift_cols(made[:, :LANES], 1)
                + shift_cols(made[:, 2 * LANES :], -1)
            )
            total = by_row(total, r - SECOND_REACH, meta, relu).astype(BF16)
            second[n, r : r + step] = total.reshape(step, LANES, LANES)


def motion_kernel(
    meta, own, even, odd, pair, pair_even, pair_odd, second, given, w_corr, w_corr2, w_motion, out, one, two, w_one, w_two, w_three
):
    core, even_chip = meta[1], meta[2]
    is_even, is_zero = even_chip == 1, core == 0

    w_one[...] = jnp.zeros(w_one.shape, F32)
    w_one[: w_corr.shape[0], :] = w_corr[...].astype(F32)
    w_first = w_one[...].astype(BF16)
    w_three[...] = jnp.zeros(w_three.shape, BF16)
    wide, made_two, made_three = w_one.shape[1], w_corr2.shape[0], w_motion.shape[1]
    w_two[:, made_two:, :] = jnp.zeros((3, w_two.shape[1] - made_two, w_two.shape[2]), BF16)
    for u in range(3):
        for s in range(3):
            tap = slice((u * 3 + s) * wide, (u * 3 + s + 1) * wide)
            w_two[s, :made_two, u * wide : (u + 1) * wide] = w_corr2[:, tap]
            w_three[u * wide : (u + 1) * wide, s * LANES : s * LANES + made_three] = w_motion[tap, :]

    def corr_row(row):
        tile, r = (row + 2 * ROWS) // ROWS - 2, row % ROWS
        if tile == 0:
            return own[r]
        if tile == -2:
            return pick(is_even, odd[r], even[r])
        if tile == 2:
            return pick(is_even, even[r], odd[r])
        if tile == -1:
            return pick(is_zero, pick(is_even, pair_odd[r], pair_even[r]), pair[r])
        return pick(is_zero, pair[r], pick(is_even, pair_even[r], pair_odd[r]))

    for r in range(ROWS + 2 * FIRST_REACH):
        made = lax.dot_general(
            corr_row(r - FIRST_REACH), w_first, (((0,), (0,)), ((), ())), preferred_element_type=F32
        )
        one[r] = by_row(made, r - FIRST_REACH, meta, relu).astype(BF16)

    step = 2
    zeros = jnp.zeros((step * LANES, LANES), BF16)

    def second_step(index, carry):
        r = index * step
        left = tap_rows(one, r, step, 3)
        made = [turned_dot(left, w_two[s]) for s in range(3)]
        total = made[1] + shift_cols(made[0], 1) + shift_cols(made[2], -1)
        total = by_row(total, r - SECOND_REACH, meta, relu).astype(BF16)
        flow = second[pl.ds(r, step)].reshape(step * LANES, LANES)
        total = total + jnp.concatenate([zeros, flow], axis=-1)
        two[pl.ds(r, step)] = total.reshape(step, LANES, 2 * LANES)
        return carry

    lax.fori_loop(0, (ROWS + 2 * SECOND_REACH) // step, second_step, 0, unroll=7)

    step3 = 6

    def third_step(index, carry):
        r = index * step3
        made = jnp.dot(tap_rows(two, r, step3, 3), w_three[:, : 2 * LANES], preferred_element_type=F32)
        size, deep = step3 * LANES, two.shape[2]
        taps = [w_three[u * deep : (u + 1) * deep, 2 * LANES :] for u in range(3)]
        pairs = product(tap_rows(two, r, step3 + 1, 1), jnp.concatenate(taps[:2], axis=1))
        last = product(tap_rows(two, r + 2, step3, 1), taps[2])
        last = last + pairs[:size, :LANES] + pairs[LANES:, LANES:]
        total = made[:, LANES : 2 * LANES] + shift_cols(made[:, :LANES], 1) + shift_cols(last, -1)
        total = by_row(total, r - MOTION_REACH, meta, relu).astype(BF16)
        total = total + given[pl.ds(r, step3)].reshape(step3 * LANES, LANES)
        out[pl.ds(r, step3)] = total.reshape(step3, LANES, LANES)
        return carry

    lax.fori_loop(0, (ROWS + 2 * MOTION_REACH) // step3, third_step, 0, unroll=2)


def spread(scratch, meta, own, across, pair):
    tile, core, tiles = meta[0], meta[1], meta[3]
    is_zero = core == 0
    nothing = jnp.zeros((), BF16)
    reach = (scratch.shape[0] - ROWS) // 2
    for r in range(reach):
        up = r if across.shape[0] == reach else ROWS - reach + r
        above = pick(is_zero, across[up], pair[up])
        below = pick(is_zero, pair[r], across[r])
        scratch[r] = jnp.where(tile > 0, above, nothing)
        scratch[reach + ROWS + r] = jnp.where(tile < tiles - 1, below, nothing)
    scratch[reach : reach + ROWS] = own[...]


def part_of(weight, low, high):
    deep = weight.shape[0] // 5
    return jnp.concatenate([weight[u * deep + low : u * deep + high, :] for u in range(5)], axis=0)


def product(left, right):
    return jnp.dot(left, right, preferred_element_type=F32)


def sigmoid(x):
    return 0.5 * jnp.tanh(0.5 * x) + 0.5


GATE_ROWS = ROWS + 2 * GATE_REACH
STEP = 4


def context_kernel(meta, both, across, pair, w_gates, w_cand, hidden, gates_one, gates_two, cand, joined):
    spread(joined, meta, both, across, pair)
    hidden[...] = joined[:, :, :LANES]
    near = slice(LANES, 2 * LANES)
    for r in range(0, GATE_ROWS, STEP):
        made = product(tap_rows(joined, r, STEP, 5, near), part_of(w_gates, LANES, 2 * LANES))
        gates_two[r : r + STEP] = made.reshape(STEP, LANES, 2 * LANES)
        made = made + product(tap_rows(hidden, r, STEP, 5), part_of(w_gates, 0, LANES))
        gates_one[r : r + STEP] = made.reshape(STEP, LANES, 2 * LANES)
    made = product(tap_rows(joined, GATE_REACH, ROWS, 5, near), part_of(w_cand, LANES, 2 * LANES))
    cand[...] = made.reshape(ROWS, LANES, LANES)


def gate_kernel(meta, gates_made, cand_made, motion, w_gates, w_cand, *rest):
    if len(rest) == 4:
        around, out, state, keep = rest
    else:
        h_own, h_across, h_pair, out, again, edge_across, edge_pair, state, keep, around = rest
        spread(around, meta, h_own, h_across, h_pair)
    for r in range(0, GATE_ROWS, STEP):
        gates = gates_made[r : r + STEP].reshape(STEP * LANES, 2 * LANES)
        gates = gates + product(tap_rows(motion, r, STEP, 5), part_of(w_gates, 2 * LANES, 3 * LANES))
        if len(rest) != 4:
            gates = gates + product(tap_rows(around, r, STEP, 5), part_of(w_gates, 0, LANES))
        hidden = around[r + 2 : r + 2 + STEP].reshape(STEP * LANES, LANES).astype(F32)
        reset = (sigmoid(gates[:, LANES:]) * hidden).astype(BF16)
        state[r : r + STEP] = reset.reshape(STEP, LANES, LANES)
        keep[r : r + STEP] = gates[:, :LANES].reshape(STEP, LANES, LANES)
    made = cand_made[...].reshape(ROWS * LANES, LANES)
    made = made + product(tap_rows(motion, GATE_REACH, ROWS, 5), part_of(w_cand, 2 * LANES, 3 * LANES))
    made = made + product(tap_rows(state, 0, ROWS, 5), part_of(w_cand, 0, LANES))
    update = sigmoid(keep[2 : 2 + ROWS].reshape(ROWS * LANES, LANES))
    hidden = around[ROWS : 2 * ROWS].reshape(ROWS * LANES, LANES).astype(F32)
    new = (1.0 - update) * hidden + update * jnp.tanh(made)
    new = new.astype(BF16).reshape(ROWS, LANES, LANES)
    out[...] = new
    if len(rest) != 4:
        again[...] = new
        is_zero = meta[1] == 0
        edge_across[...] = pick(is_zero, new[:2], new[2:])
        edge_pair[...] = pick(is_zero, new[2:], new[:2])


def head_kernel(meta, h_own, h_across, h_pair, w_head1, w_head2, *rest):
    before, out, joined, hidden, w_two = rest if len(rest) == 5 else (None,) + rest
    spread(joined, meta, h_own, h_across, h_pair)
    deep, wide = h_own.shape[2], w_head1.shape[1]
    w_two[...] = jnp.zeros(w_two.shape, F32)
    for s in range(3):
        for u in range(3):
            k = u * 3 + s
            w_two[2 * s : 2 * s + 2, u * wide : (u + 1) * wide] = w_head2[:, k * wide : (k + 1) * wide].astype(F32)
    step = 2
    for r in range(0, ROWS + 2, step):
        left = tap_rows(joined, r, step, 3)
        made = []
        for s in range(3):
            taps = [w_head1[(u * 3 + s) * deep : (u * 3 + s + 1) * deep, :] for u in range(3)]
            made.append(product(left, jnp.concatenate(taps, axis=0)))
        total = made[1] + shift_cols(made[0], 1) + shift_cols(made[2], -1)
        total = by_row(total, r - 1, meta, relu).astype(BF16)
        hidden[r : r + step] = total.reshape(step, LANES, 2 * LANES)
    lane = lax.broadcasted_iota(jnp.int32, (2, LANES), 1)
    target = out
    if before is not None:
        out[0] = before[...]
        target = out.at[1]
    made_all = turned_dot(w_two[...].astype(BF16), tap_rows(hidden, 0, ROWS, 3))
    for r in range(ROWS):
        made = made_all[:, r * LANES : (r + 1) * LANES]
        left = jnp.where(lane == 0, 0.0, pltpu.roll(made[0:2], 1, 1))
        right = jnp.where(lane == LANES - 1, 0.0, pltpu.roll(made[4:6], LANES - 1, 1))
        total = left + made[2:4] + right
        target[0, r : r + 1, :] = total[0:1]
        target[1, r : r + 1, :] = total[1:2]


SMEM = pltpu.SMEM
MIB = 1024 * 1024


def call(kernel, args, out_shape, scratch, smem=1, blocks=None, far=(), micros=0, vmem=20, aliases={}):
    specs = []
    for k, arg in enumerate(args):
        if k < smem:
            specs.append(pl.BlockSpec(memory_space=SMEM))
        elif k in far:
            specs.append(pl.BlockSpec(memory_space=pltpu.HBM))
        elif blocks and k in blocks:
            specs.append(blocks[k])
        else:
            specs.append(pl.BlockSpec(memory_space=pltpu.VMEM))
    return pl.pallas_call(
        kernel,
        out_shape=out_shape,
        grid=(1,) if blocks else (),
        in_specs=specs,
        out_specs=jax.tree.map(lambda o: pl.BlockSpec(memory_space=pltpu.VMEM), out_shape),
        scratch_shapes=scratch,
        input_output_aliases=aliases,
        compiler_params=pltpu.CompilerParams(vmem_limit_bytes=vmem * MIB),
        cost_estimate=pl.CostEstimate(
            flops=1024, bytes_accessed=1024 + 3_000_000 * micros, transcendentals=0
        ),
    )(*args)


def shards(
    first_frame,
    second_frame,
    context,
    hidden_init,
    flow_rows,
    flow_cols,
    block_ids,
    block_counts,
    w_corr,
    w_corr2,
    w_flow1,
    w_flow2,
    w_motion,
    w_gates,
    w_cand,
    w_head1,
    w_head2,
):
    rows_dev, width, channels = first_frame.shape
    tile_count = lax.axis_size("row")
    tile = lax.axis_index("row")
    core = tile & 1
    even_chip = ((tile >> 1) & 1) ^ 1
    meta = jnp.stack([tile, core, even_chip, jnp.int32(tile_count)]).astype(jnp.int32)
    SDS = jax.ShapeDtypeStruct
    VM = pltpu.VMEM
    pixels = rows_dev * width

    blocks = second_frame.reshape(pixels, channels)
    flows = jnp.concatenate([flow_rows, flow_cols]).astype(BF16).reshape(-1, width)
    payload = jnp.concatenate([blocks, jnp.pad(flows, ((0, 0), (0, channels - width)))])
    even, far, pair = swap(payload, chip_even), swap(payload, three_away), swap(payload, in_chip)
    pair, counts, hidden, close = lax.optimization_barrier((pair, block_counts.T, hidden_init, context))
    both = jnp.concatenate([hidden, close], axis=-1)
    frame, own_volume = call(
        own_kernel,
        [first_frame.reshape(pixels, channels), blocks],
        (SDS((pixels, channels), BF16), SDS((rows_dev, pixels, LANES), F32)),
        [],
        smem=0,
    )
    turned, windows = call(
        stage_kernel,
        [meta, block_ids, counts, flow_rows, flow_cols],
        (SDS((ITERS, rows_dev, width, LANES), jnp.int32), SDS((ITERS, CHUNK, LANES), jnp.int32)),
        [],
    )
    even, both, frame, own_volume = lax.optimization_barrier((even, both, frame, own_volume))
    odd = relay(even)
    both_sides = side_tiles(both)
    odd, far, both_sides, turned, windows = lax.optimization_barrier((odd, far, both_sides, turned, windows))
    pair_even, pair_odd = swap(even, in_chip), swap(odd, in_chip)
    around = [even, odd, far, pair, pair_even, pair_odd]
    shape = SDS((NB * rows_dev, pixels, LANES), F32)
    volume = call(early_kernel, [meta, frame, even, far, pair, pair_even], shape, [])
    corr = call(
        corr_kernel,
        [meta, frame, own_volume, turned, windows, odd, pair_odd, volume],
        (SDS((ITERS, rows_dev, DEPTH, width), BF16), shape),
        [VM((width, LANES), F32)],
        aliases={7: 1},
    )[0]

    second_rows = rows_dev + 2 * SECOND_REACH
    first_rows = rows_dev + 2 * FIRST_REACH
    motion_rows = rows_dev + 2 * MOTION_REACH
    flow_second, flow_given = call(
        flow_kernel,
        [meta, payload, *around, w_flow1, w_flow2.T],
        (
            SDS((ITERS, second_rows, width, LANES), BF16),
            SDS((ITERS, motion_rows, width, LANES), BF16),
        ),
        [
            VM((first_rows, width, LANES), BF16),
            VM((7, 16, 2 * LANES), F32),
            VM((3 * LANES, 3 * LANES), BF16),
            VM((ITERS, NB * rows_dev, 16, width), F32),
        ],
    )

    even, odd, pair = swap(corr, chip_even), swap(corr, chip_odd), swap(corr, in_chip)
    h_around, gates_one, gates_two, cand = call(
        context_kernel,
        [meta, both, *both_sides, w_gates, w_cand],
        (
            SDS((motion_rows, width, LANES), BF16),
            SDS((GATE_ROWS, width, 2 * LANES), F32),
            SDS((GATE_ROWS, width, 2 * LANES), F32),
            SDS((rows_dev, width, LANES), F32),
        ),
        [VM((motion_rows, width, 2 * LANES), BF16)],
    )
    even, odd, flow_second, cand = lax.optimization_barrier((even, odd, flow_second, cand))
    near = (corr, even, odd, pair, swap(even, in_chip), swap(odd, in_chip))

    def motion_of(n):
        def part(shape):
            return pl.BlockSpec((None,) + shape[1:], lambda i: (n, 0, 0, 0))

        tiles = [*near, flow_second, flow_given]
        return call(
            motion_kernel,
            [meta, *tiles, w_corr, w_corr2.T, w_motion],
            SDS((motion_rows, width, LANES), BF16),
            [
                VM((first_rows, width, 2 * LANES), BF16),
                VM((second_rows, width, 2 * LANES), BF16),
                VM((DEPTH, w_corr.shape[1]), F32),
                VM((3, 2 * LANES, 3 * w_corr.shape[1]), BF16),
                VM((3 * 2 * LANES, 3 * LANES), BF16),
            ],
            blocks={1 + k: part(x.shape) for k, x in enumerate(tiles)},
        )

    def head_of(h, h_sides, before=()):
        shape = (2, rows_dev, width)
        return call(
            head_kernel,
            [meta, h, *h_sides, w_head1, w_head2.T, *before],
            SDS((ITERS,) + shape if before else shape, F32),
            [
                VM((rows_dev + 4, width, LANES), BF16),
                VM((rows_dev + 2, width, 2 * LANES), BF16),
                VM((8, 3 * w_head1.shape[1]), F32),
            ],
        )

    tile_of = SDS((rows_dev, width, LANES), BF16)
    edge_of = SDS((2, width, LANES), BF16)
    states = [VM((GATE_ROWS, width, LANES), BF16), VM((GATE_ROWS, width, LANES), F32)]
    h_one = call(
        gate_kernel,
        [meta, gates_one, cand, motion_of(0), w_gates, w_cand, h_around],
        tile_of,
        states,
    )
    one_tiles = (h_one, *side_tiles(h_one))
    h_two, h_again, edge_across, edge_pair = call(
        gate_kernel,
        [meta, gates_two, cand, motion_of(1), w_gates, w_cand, *one_tiles],
        (tile_of, tile_of, edge_of, edge_of),
        states + [VM((motion_rows, width, LANES), BF16)],
    )
    edges = (swap(edge_across, next_row), swap(edge_pair, in_chip))
    delta_one = head_of(h_one, one_tiles[1:])
    deltas = head_of(h_again, edges, (delta_one,))
    return (h_two, deltas)


def solution(mesh):
    tiled = P(("group", "row"), None, None)
    listed = P(None, ("group", "row"), None)
    placed = (tiled,) * 4 + (listed,) * 3 + (P(None, ("group", "row")),) + (P(),) * 9
    return jax.shard_map(
        shards,
        mesh=mesh,
        in_specs=placed,
        out_specs=(tiled, P(None, None, ("group", "row"), None)),
        check_vma=False,
    )
```
